256 devices in a mesh: row: 16 (over y, x_lo, core), col: 16 (over x_hi, z).
Axes of the slice: x: 4 (x_hi: 2, x_lo: 2; x = x_hi * 2 + x_lo), y: 4, z: 8, core: 2. Of those that a mesh axis runs over, the one named last changes fastest.
Arguments:
- gradient: bfloat16 [5120, 5120], P('row', 'col'), may hold values from -6 to 6
- left_basis: bfloat16 [5120, 5120], P(None, 'row'), may hold values from -0.078125 to 0.078125
- right_basis: bfloat16 [5120, 5120], P(None, 'col'), may hold values from -0.078125 to 0.078125
- exp_avg: float32 [5120, 5120], P('row', 'col'), may hold values from -4 to 4
- exp_avg_sq: float32 [5120, 5120], P('row', 'col'), may hold values from 0.1 to 2
Outputs:
- new_avg: float32 [5120, 5120], P('row', 'col')
- new_sq: float32 [5120, 5120], P('row', 'col')
- update: bfloat16 [5120, 5120], P('row', 'col')
The draws below stay inside these ranges and needn't reach their ends.
All inputs are finite; a program needn't handle non-finite values.
Results may differ from the reference program's by a relative error of at most 0.029.
Values may be sent and summed in bfloat16 or wider, within the bound.
No kernel may reach another device: no remote copies, remote signals or barrier semaphores. Data moves between devices by JAX's collectives and lax.ppermute only.
A program may use at most 64 MiB of HBM per device.

```python
import math
import jax
import jax.numpy as jnp
from jax import lax

D = 5120
BLOCK = 5120
N_ROW = 16
N_COL = 16


def levels(key, dims, shards, least, largest):
    gain, own = 1.0, jax.random.fold_in(key, 6)
    for axis_at, blocks in shards:
        steps = jnp.exp(jax.random.uniform(jax.random.fold_in(own, axis_at), (blocks,), jnp.float32, least / len(shards), largest / len(shards)))
        gain = gain * jnp.repeat(steps, dims[axis_at] // blocks).reshape([-1 if axis == axis_at else 1 for axis in range(len(dims))])
    return gain


def normal_values(key, dims, spread, limit, pieces=(), dtype=jnp.bfloat16):
    factor_of = levels(key, dims, pieces, -0.22, 0.18) if pieces else 1.0
    values = jax.random.normal(key, dims, jnp.float32) * spread * factor_of
    return jnp.minimum(jnp.maximum(values, -limit), limit).astype(dtype)


def setup_inputs(seed: int = 0) -> dict:
    streams_of = jax.random.split(jax.random.key(seed), 6)
    gradient = normal_values(streams_of[0], (D, BLOCK), 1.0, 6.0, ((0, 16), (1, 16)))
    left_basis = normal_values(streams_of[1], (D, D), D ** -0.5, 0.078125, ((1, 16),))
    right_basis = normal_values(streams_of[2], (BLOCK, BLOCK), BLOCK ** -0.5, 0.078125, ((1, 16),))
    exp_avg = normal_values(streams_of[3], (D, BLOCK), 0.3, 4.0, ((0, 16), (1, 16)), jnp.float32)
    exp_avg_sq = jnp.clip(jnp.exp(math.log(2.0) - 2.9957323 * jax.random.uniform(streams_of[4], (D, BLOCK), jnp.float32) ** levels(streams_of[4], (D, BLOCK), ((0, 16), (1, 16)), -0.2, 0.2)), 0.1, 2.0)
    return dict(gradient=gradient, left_basis=left_basis, right_basis=right_basis, exp_avg=exp_avg, exp_avg_sq=exp_avg_sq)


first_fix = 0.9999734386
second_fix = 0.9940794709

def rounded_sum(lefts, rights, rows, cols):

    def step(total, pair):
        part = jnp.dot(pair[0], pair[1], preferred_element_type=jnp.float32).astype(jnp.bfloat16)
        part = lax.optimization_barrier(part)
        return (total + part.astype(jnp.float32), None)
    start = jnp.zeros((rows, cols), jnp.float32)
    total, unused = lax.scan(step, start, (lefts, rights))
    return total

def reference(gradient, left_basis, right_basis, exp_avg, exp_avg_sq):
    rot_left = jnp.dot(left_basis.T, gradient, preferred_element_type=jnp.float32).astype(jnp.bfloat16)
    rotated = jnp.dot(rot_left, right_basis, preferred_element_type=jnp.float32)
    new_avg = 0.9 * exp_avg + 0.1 * rotated
    new_sq = 0.95 * exp_avg_sq + 0.05 * rotated * rotated
    direction = (new_avg / first_fix / (jnp.sqrt(new_sq / second_fix) + 1e-08)).astype(jnp.bfloat16)
    col_width = BLOCK // N_COL
    dir_blocks = jnp.transpose(direction.reshape(D, N_COL, col_width), (1, 0, 2))
    basis_blocks = jnp.transpose(right_basis.reshape(BLOCK, N_COL, col_width), (1, 2, 0))
    back_right = rounded_sum(dir_blocks, basis_blocks, D, BLOCK).astype(jnp.bfloat16)
    row_width = D // N_ROW
    left_blocks = jnp.transpose(left_basis.reshape(D, N_ROW, row_width), (1, 0, 2))
    back_blocks = back_right.reshape(N_ROW, row_width, BLOCK)
    update = rounded_sum(left_blocks, back_blocks, D, BLOCK).astype(jnp.bfloat16)
    return (new_avg, new_sq, update)
```

```python
import jax
import jax.numpy as jnp
from jax import lax
from jax.experimental import pallas as pl
from jax.experimental.pallas import tpu as pltpu
from jax.sharding import PartitionSpec as P

first_fix = 0.9999734386
second_fix = 0.9940794709

AXES = ("row", "col")
SIZES = {"y": 4, "xl": 2, "k": 2, "xh": 2, "z": 8}
BF, F32 = jnp.bfloat16, jnp.float32
B, H, W = 320, 160, 640
YX = [(0, 0), (-1, 0), (1, 0), (0, 1), (-1, 1), (1, 1), (2, 0), (2, 1)]
ZS = [0, -1, 1, -2, 2, -3, 3, 4]
LANES = [(0, 256), (256, 384)]


def place(i):
    r, c = divmod(i, 16)
    return {"y": r // 4, "xl": r // 2 % 2, "k": r % 2, "xh": c // 8, "z": c % 8}


def move(x, **steps):
    pairs = []
    for i in range(256):
        d = place(i)
        for name, step in steps.items():
            d[name] = (d[name] + step) % SIZES[name]
        pairs.append((i, (d["y"] * 4 + d["xl"] * 2 + d["k"]) * 16 + d["xh"] * 8 + d["z"]))
    return lax.ppermute(x, AXES, pairs)


def vmem(n):
    return [pl.BlockSpec(memory_space=pltpu.VMEM)] * n


SMEM = pl.BlockSpec(memory_space=pltpu.SMEM)


def call(body, out, args, scratch=(), limit=40, flops=0):
    single = not isinstance(out, (list, tuple))
    outs = [out] if single else list(out)
    size = sum(a.size * a.dtype.itemsize for a in args) + sum(o.size * o.dtype.itemsize for o in outs)
    res = pl.pallas_call(
        body,
        out_shape=outs,
        in_specs=[SMEM] + vmem(len(args) - 1),
        out_specs=vmem(len(outs)),
        scratch_shapes=list(scratch),
        compiler_params=pltpu.CompilerParams(vmem_limit_bytes=limit << 20),
        cost_estimate=pl.CostEstimate(flops=flops, bytes_accessed=size, transcendentals=0),
    )(*args)
    return res[0] if single else res


def sds(shape, dtype=BF):
    return jax.ShapeDtypeStruct(shape, dtype)


def chip_at(at, dy, p):
    return lax.rem(at[0] + dy + 4, 4) * 2 + lax.rem(at[1] + p, 2)


def ring_at(at, d):
    return lax.rem(at[4] + d + 8, 8)


def to_half(at, own, other, n):
    def body(at, own, other, *rest):
        outs, (stack, turned) = rest[:n], rest[n:]
        k = at[2]
        stack[pl.ds(pl.multiple_of(B * k, 16), B), 0:B] = own[...]
        stack[pl.ds(pl.multiple_of(B * (1 - k), 16), B), 0:B] = other[...]
        turned[...] = jnp.transpose(stack[...])
        step = H // n
        for i in range(n):
            outs[i][...] = turned[pl.ds(pl.multiple_of(H * k + step * i, 16), step), :]

    dt = own.dtype
    return call(
        body, [sds((H // n, W), dt)] * n, (at, own, other), [pltpu.VMEM((W, 384), dt), pltpu.VMEM((384, W), dt)]
    )


def from_half(at, own, other):
    n = len(own)

    def body(at, *rest):
        mine, theirs, (out, stack, turned) = rest[:n], rest[n : 2 * n], rest[2 * n :]
        k = at[2]
        off = 0
        for a, b in zip(mine, theirs):
            w = a.shape[1]
            stack[pl.ds(pl.multiple_of(H * k, 16), H), off : off + w] = a[...]
            stack[pl.ds(pl.multiple_of(H * (1 - k), 16), H), off : off + w] = b[...]
            off += w
        turned[...] = jnp.transpose(stack[...])
        out[...] = turned[pl.ds(pl.multiple_of(B * k, 16), B), 0:B]

    dt = own[0].dtype
    return call(
        body, sds((B, B), dt), (at, *own, *other), [pltpu.VMEM((384, W), dt), pltpu.VMEM((W, 384), dt)]
    )


def right_parts(at, own, got, passed):
    def body(at, own, got, passed, t0, t1, flat, stack, turned, pick):
        k = at[2]
        stack[0:B, :] = own[...]
        wide = 4 * B
        stack[B:W, pl.ds(pl.multiple_of(wide * k, 128), wide)] = got[...]
        stack[B:W, pl.ds(pl.multiple_of(wide * (1 - k), 128), wide)] = passed[...]
        for t in range(20):
            turned[128 * t : 128 * t + 128, :] = jnp.transpose(stack[:, 128 * t : 128 * t + 128])
        for z in range(8):
            flat[H * z : H * z + H, :] = turned[pl.ds(pl.multiple_of(B * z + H * k, 16), H), :]
        for h, out in ((0, t0), (1, t1)):
            for z in range(8):
                pick[80 * z : 80 * z + 80, :] = flat[H * z + 80 * h : H * z + 80 * h + 80, :]
            out[...] = jnp.transpose(pick[...])

    return call(
        body,
        [sds((W, W)), sds((W, W)), sds((4 * B, W))],
        (at, own, got, passed),
        [pltpu.VMEM((W, 8 * B), BF), pltpu.VMEM((8 * B, W), BF), pltpu.VMEM((W, W), BF)],
    )


def gather_yx(x, up):
    got = {(0, 0): x}
    got[0, 1] = move(x, xl=1)
    got[-1, 0] = move(x, y=1)
    got[1, 0] = move(x, y=-1)
    got[2, 0] = move(got[-1, 0], y=1) if up else move(got[1, 0], y=-1)
    got[-1, 1] = move(got[0, 1], y=1)
    got[1, 1] = move(got[0, 1], y=-1)
    got[2, 1] = move(got[2, 0], xl=1)
    return [got[d] for d in YX]


def add(*xs):
    total = xs[0].astype(F32)
    for x in xs[1:]:
        total = total + x.astype(F32)
    return total.astype(BF)


def scatter_yx(parts, up):
    part = dict(zip(YX, parts))
    far = add(part[2, 0], move(part[2, 1], xl=1))
    side = add(part[0, 1], move(part[1, 1], y=1), move(part[-1, 1], y=-1))
    right, left = part[1, 0], part[-1, 0]
    if up:
        right = add(right, move(far, y=1))
    else:
        left = add(left, move(far, y=-1))
    return add(part[0, 0], move(right, y=1), move(left, y=-1), move(side, xl=1))


def gather_z(x, up):
    got = {0: x}
    plus = minus = x
    for s in range(1, 5 if up else 4):
        got[-s] = plus = move(plus, z=1)
    for s in range(1, 4 if up else 5):
        got[s] = minus = move(minus, z=-1)
    if up:
        got[4] = got.pop(-4)
    return [got[d] for d in ZS]


def scatter_z(parts, up):
    part = dict(zip(ZS, parts))
    part[-4] = part[4]
    ends = []
    for sign, far in ((1, 4 if up else 3), (-1, 3 if up else 4)):
        total = part[sign * far]
        for s in range(far - 1, 0, -1):
            total = add(part[sign * s], move(total, z=sign))
        ends.append(move(total, z=sign))
    return add(part[0], *ends)


def times_left(at, pieces, left):
    rows = pieces[0].shape[0]

    def body(at, *rest):
        blocks, left, out = rest[:8], rest[8], rest[9]
        total = jnp.zeros((rows, W), F32)
        for (dy, p), block in zip(YX, blocks):
            cols = pl.ds(pl.multiple_of(chip_at(at, dy, p) * W, 128), W)
            total += lax.dot_general(block[...], left[:, cols], (((1,), (1,)), ((), ())), preferred_element_type=F32)
        out[...] = total.astype(BF)

    return call(body, sds((rows, W)), (at, *pieces, left), flops=2 * rows * W * 8 * W)


def times_right(at, pieces, right, before):
    rows = pieces[0].shape[0]

    def body(at, *rest):
        blocks, right = rest[:8], rest[8]
        stack = rest[-1]
        for d, block in zip(ZS, blocks):
            stack[pl.ds(pl.multiple_of(ring_at(at, d) * rows, 16), rows), :] = block[...]
        part = jnp.dot(right[...], stack[...], preferred_element_type=F32)
        if before is None:
            rest[9][...] = part
            return
        total = rest[-2]
        total[...] = rest[9][...] + part
        keep, far, give, give_far = rest[10:14]
        k = at[2]
        mine, theirs = pl.multiple_of(H * k, 16), pl.multiple_of(H * (1 - k), 16)
        keep[...] = total[pl.ds(mine, H), :]
        far[...] = total[pl.ds(B + mine, H), :]
        give[...] = total[pl.ds(theirs, H), :].astype(BF)
        give_far[...] = total[pl.ds(B + theirs, H), :].astype(BF)

    stack = pltpu.VMEM((W, W), BF)
    flops = 2 * W * W * W
    if before is None:
        return call(body, sds((W, W), F32), (at, *pieces, right), [stack], flops=flops)
    outs = [sds((H, W), F32), sds((H, W), F32), sds((H, W)), sds((H, W))]
    return call(body, outs, (at, *pieces, right, before), [pltpu.VMEM((W, W), F32), stack], flops=flops)


def moments(at, keep, near, far, avg, sq):
    def body(at, keep, near, far, avg, sq, new_avg, new_sq, direction):
        rotated = keep[...] + near[...].astype(F32) + far[...].astype(F32)
        a = 0.9 * avg[...] + 0.1 * rotated
        s = 0.95 * sq[...] + 0.05 * rotated * rotated
        new_avg[...] = a
        new_sq[...] = s
        direction[...] = (a / first_fix / (jnp.sqrt(s / second_fix) + 1e-08)).astype(BF)

    return call(body, [sds((H, W), F32), sds((H, W), F32), sds((H, W))], (at, keep, near, far, avg, sq))


def left_back(at, direction, left, off, width):
    def body(at, direction, left, *outs):
        for (dy, p), out in zip(YX, outs):
            cols = pl.ds(pl.multiple_of(chip_at(at, dy, p) * W + off, 128), width)
            out[...] = jnp.dot(direction[...], left[:, cols], preferred_element_type=F32).astype(BF)

    return call(body, [sds((H, width))] * 8, (at, direction, left), flops=2 * H * W * 8 * width)


def right_back(at, own, near, far, far_near, right):
    width = own.shape[1]

    def body(at, own, near, far, far_near, right, *rest):
        outs, (stack, total) = rest[:8], rest[8:]
        k = at[2]
        mine, theirs = pl.multiple_of(H * k, 16), pl.multiple_of(H * (1 - k), 16)
        stack[pl.ds(mine, H), :] = own[...]
        stack[pl.ds(theirs, H), :] = near[...]
        stack[pl.ds(B + mine, H), :] = far[...]
        stack[pl.ds(B + theirs, H), :] = far_near[...]
        total[...] = jnp.dot(right[...], stack[...], preferred_element_type=F32).astype(BF)
        for d, out in zip(ZS, outs):
            out[...] = total[pl.ds(pl.multiple_of(ring_at(at, d) * H, 16), H), :]

    scratch = [pltpu.VMEM((W, width), BF), pltpu.VMEM((4 * B, width), BF)]
    return call(
        body, [sds((H, width))] * 8, (at, own, near, far, far_near, right), scratch, flops=2 * 4 * B * W * width
    )


def per_device(gradient, left_basis, right_basis, exp_avg, exp_avg_sq):
    row, col = lax.axis_index("row"), lax.axis_index("col")
    k, xh = row % 2, col // 8
    at = jnp.stack([row // 4, row // 2 % 2, k, xh, col % 8]).astype(jnp.int32)

    gradient_far = move(gradient, k=1)
    own_left = left_basis.T
    half = 4 * B
    own_right = right_basis.T
    sent = lax.dynamic_slice(own_right, (0, (1 - xh) * 2 * half + k * half), (B, half))
    got = move(sent, xh=1, xl=1)
    far_left = move(own_left, k=1)
    left = jnp.where(
        k == 0, jnp.concatenate([own_left, far_left], 0), jnp.concatenate([far_left, own_left], 0)
    )
    passed = move(got, k=1)
    kept = lax.dynamic_slice(own_right, (0, xh * 2 * half), (B, 2 * half))
    right0, right1, right = right_parts(at, kept, got, passed)
    (avg,) = to_half(at, exp_avg, move(exp_avg, k=1), 1)
    (sq,) = to_half(at, exp_avg_sq, move(exp_avg_sq, k=1), 1)

    first, second = to_half(at, gradient, gradient_far, 2)
    x0 = times_left(at, gather_yx(first, True), left)
    x1 = times_left(at, gather_yx(second, False), left)
    part = times_right(at, gather_z(x0, True), right0, None)
    keep, far, give, give_far = times_right(at, gather_z(x1, False), right1, part)
    far = add(far, move(give_far, k=1))
    a, s, direction = moments(at, keep, move(give, k=1), move(far, xh=1), avg, sq)
    new_avg = from_half(at, [a], [move(a, k=1)])
    new_sq = from_half(at, [s], [move(s, k=1)])

    ends = []
    for i, (off, width) in enumerate(LANES):
        parts = left_back(at, direction, left, off, width)
        own = scatter_yx(parts, i == 0)
        far = move(own, xh=1)
        parts = right_back(at, own, move(own, k=1), far, move(far, k=1), right)
        ends.append(scatter_z(parts, i == 0))
    update = from_half(at, ends, [move(e, k=1) for e in ends])
    return (new_avg, new_sq, update)


def solution(mesh):
    placed = (P("row", "col"), P(None, "row"), P(None, "col"), P("row", "col"), P("row", "col"))
    return jax.shard_map(
        per_device,
        mesh=mesh,
        in_specs=placed,
        out_specs=(P("row", "col"), P("row", "col"), P("row", "col")),
        check_vma=False,
    )
```

```python
import jax
import jax.numpy as jnp
import numpy as np
from jax import lax
from jax.experimental import pallas as pl
from jax.experimental.pallas import tpu as pltpu
from jax.sharding import PartitionSpec as P

first_fix = 0.9999734386
second_fix = 0.9940794709

AXES = ("row", "col")
SIZES = {"y": 4, "xl": 2, "k": 2, "xh": 2, "z": 8}
BF, F32 = jnp.bfloat16, jnp.float32
B, H, W = 320, 160, 640
YX = [(0, 0), (-1, 0), (1, 0), (0, 1), (-1, 1), (1, 1), (2, 0), (2, 1)]
ZS = [0, -1, 1, -2, 2, -3, 3, 4]
STEP = 80


def place(i):
    r, c = divmod(i, 16)
    return {"y": r // 4, "xl": r // 2 % 2, "k": r % 2, "xh": c // 8, "z": c % 8}


def move(x, **steps):
    pairs = []
    for i in range(256):
        d = place(i)
        for name, step in steps.items():
            d[name] = (d[name] + step) % SIZES[name]
        pairs.append((i, (d["y"] * 4 + d["xl"] * 2 + d["k"]) * 16 + d["xh"] * 8 + d["z"]))
    return lax.ppermute(x, AXES, pairs)


ANY = pl.BlockSpec(memory_space=pl.ANY)
VMEM = pl.BlockSpec(memory_space=pltpu.VMEM)
SMEM = pl.BlockSpec(memory_space=pltpu.SMEM)


def call(body, out, at, apart=(), vmem=(), scratch=(), limit=40, flops=0, out_spec=None):
    args = [at, *apart, *vmem]
    size = sum(a.size * a.dtype.itemsize for a in args) + sum(
        int(np.prod(o.shape)) * jnp.dtype(o.dtype).itemsize for o in out
    )
    return pl.pallas_call(
        body,
        out_shape=list(out),
        in_specs=[SMEM] + [ANY] * len(apart) + [VMEM] * len(vmem),
        out_specs=[out_spec or VMEM] * len(out),
        scratch_shapes=list(scratch),
        compiler_params=pltpu.CompilerParams(vmem_limit_bytes=limit << 20),
        cost_estimate=pl.CostEstimate(flops=flops, bytes_accessed=size, transcendentals=0),
    )(*args)


def sds(shape, dtype=BF):
    return jax.ShapeDtypeStruct(shape, dtype)


def far_sds(shape, dtype=BF):
    return pltpu.HBM(shape, dtype)


def in_hbm(x):
    return pltpu.with_memory_space_constraint(x, pltpu.HBM)


def after(x, *others):
    return lax.optimization_barrier((x, *others))[0]


def chip_at(at, dy, p):
    return lax.rem(at[0] + dy + 4, 4) * 2 + lax.rem(at[1] + p, 2)


def ring_at(at, d):
    return lax.rem(at[4] + d + 8, 8)


def copies(pairs, sems):
    started = []
    for n, (a, b) in enumerate(pairs):
        c = pltpu.make_async_copy(a, b, sems.at[n])
        c.start()
        started.append(c)
    for c in started:
        c.wait()


def rows(i, n):
    return pl.ds(pl.multiple_of(i, 16), n)


def to_half(at, own, other, parts, shape=sds):
    dt = own.dtype

    def body(at, own, other, *rest):
        outs, (stack, turned) = rest[: len(parts)], rest[len(parts) :]
        k = at[2]
        stack[rows(B * k, B), 0:B] = own[...]
        stack[rows(B * (1 - k), B), 0:B] = other[...]
        turned[...] = jnp.transpose(stack[...])
        for out, (lo, n) in zip(outs, parts):
            out[...] = turned[rows(H * k + lo, n), :]

    return call(
        body,
        [shape((n, W), dt) for _, n in parts],
        at,
        vmem=(own, other),
        scratch=[pltpu.VMEM((W, 384), dt), pltpu.VMEM((384, W), dt)],
        limit=16,
        out_spec=pl.BlockSpec() if shape is far_sds else None,
    )


def from_half(at, own, other):
    n = len(own)
    dt = own[0].dtype

    def body(at, *rest):
        mine, theirs, (out, stack, turned) = rest[:n], rest[n : 2 * n], rest[2 * n :]
        k = at[2]
        lo = 0
        for a, b in zip(mine, theirs):
            h = a.shape[0]
            stack[rows(H * k + lo, h), :] = a[...]
            stack[rows(H * (1 - k) + lo, h), :] = b[...]
            lo += h
        turned[...] = jnp.transpose(stack[...])
        out[...] = turned[rows(B * k, B), 0:B]

    return call(
        body,
        [sds((B, B), dt)],
        at,
        vmem=(*own, *other),
        scratch=[pltpu.VMEM((384, W), dt), pltpu.VMEM((W, 384), dt)],
        limit=16,
    )[0]


def both_left(at, own, other):
    def body(at, own, other, out, sems):
        k = at[2]
        copies([(own, out.at[rows(B * k, B), :]), (other, out.at[rows(B * (1 - k), B), :])], sems)

    return call(
        body, [sds((W, 16 * B))], at, apart=(own, other), scratch=[pltpu.SemaphoreType.DMA((2,))], limit=4, out_spec=ANY
    )[0]


def right_parts(at, own, got, passed):
    def body(at, own, got, passed, turned_out, flat, stack, turned):
        k = at[2]
        stack[0:B, :] = own[...]
        wide = 4 * B
        stack[B:W, pl.ds(pl.multiple_of(wide * k, 128), wide)] = got[...]
        stack[B:W, pl.ds(pl.multiple_of(wide * (1 - k), 128), wide)] = passed[...]
        for t in range(20):
            turned[128 * t : 128 * t + 128, :] = jnp.transpose(stack[:, 128 * t : 128 * t + 128])
        for z in range(8):
            flat[H * z : H * z + H, :] = turned[rows(B * z + H * k, H), :]
        for t in range(10):
            turned_out[:, 128 * t : 128 * t + 128] = jnp.transpose(flat[128 * t : 128 * t + 128, :])

    return call(
        body,
        [sds((W, 4 * B)), sds((4 * B, W))],
        at,
        vmem=(own, got, passed),
        scratch=[pltpu.VMEM((W, 8 * B), BF), pltpu.VMEM((8 * B, W), BF)],
        limit=24,
    )


def gather_yx(x, top, bottom):
    side = move(x, xl=1)
    behind, ahead = move(x, y=1), move(x, y=-1)
    far = [move(top, y=2), move(bottom, y=-2)]
    side_behind, side_ahead = move(side, y=1), move(side, y=-1)
    side_far = [move(f, xl=1) for f in far]
    x, behind, ahead, side = (in_hbm(a) for a in (x, behind, ahead, side))
    return [[x], [behind], [ahead], [side], [side_behind], [side_ahead], far, side_far]


def add(*xs):
    total = xs[0].astype(F32)
    for x in xs[1:]:
        total = total + x.astype(F32)
    return total.astype(BF)


def scatter_yx(part):
    far = add(part[2, 0], move(part[2, 1], xl=1))
    side = add(part[0, 1], move(part[1, 1], y=1), move(part[-1, 1], y=-1))
    near = [move(part[1, 0], y=1), move(part[-1, 0], y=-1)]
    far = jnp.concatenate([move(far[:STEP], y=2), move(far[STEP:], y=-2)], 0)
    return add(part[0, 0], *near, far, move(side, xl=1))


def gather_z(x, up):
    got = {0: x}
    plus = minus = x
    for s in range(1, 5):
        if s < 4 or up:
            got[-s] = plus = move(plus, z=1)
        if s < 4 or not up:
            got[s] = minus = move(minus, z=-1)
        plus, minus = lax.optimization_barrier((plus, minus))
    if up:
        got[4] = got.pop(-4)
    return [in_hbm(got[d]) if abs(d) < 3 else got[d] for d in ZS]


def scatter_z(part, up):
    part[-4] = part[4]
    ends = []
    for sign, far in ((1, 4 if up else 3), (-1, 3 if up else 4)):
        total = part[sign * far]
        for s in range(far - 1, 0, -1):
            total = add(part[sign * s], move(total, z=sign))
        ends.append(move(total, z=sign))
    return add(part[0], *ends)


def times_left(at, pieces, left):
    flat = [(d, i, x) for d, xs in zip(YX, pieces) for i, x in enumerate(xs)]
    n = len(flat)

    def body(at, *rest):
        blocks, left, top, bottom, stack, sems = rest[:n], *rest[n:]
        pairs = []
        for ((dy, p), i, _), block in zip(flat, blocks):
            cols = pl.ds(pl.multiple_of(chip_at(at, dy, p) * W, 128), W)
            pairs.append((block, stack.at[STEP * i : STEP * i + block.shape[0], cols]))
        copies(pairs, sems)
        total = lax.dot_general(stack[...], left[...], (((1,), (1,)), ((), ())), preferred_element_type=F32).astype(BF)
        top[...] = total[:STEP]
        bottom[...] = total[STEP:]

    return call(
        body,
        [far_sds((STEP, W))] * 2,
        at,
        out_spec=pl.BlockSpec(),
        apart=[x for _, _, x in flat],
        vmem=[left],
        scratch=[pltpu.VMEM((H, 16 * B), BF), pltpu.SemaphoreType.DMA((n,))],
        flops=2 * H * W * 16 * B,
        limit=24,
    )


def times_right(at, pieces, right, lo, wait_for=()):
    n = len(pieces[0])
    blocks = [x for chunk in pieces for x in chunk]

    def body(at, *rest):
        refs, rest = rest[: 2 * n], rest[2 * n + len(wait_for) :]
        right, keep, give, stack, total, sems = rest
        pairs = []
        for h in range(2):
            for i, d in enumerate(ZS):
                pairs.append((refs[h * n + i], stack.at[rows(ring_at(at, d) * H + STEP * h, STEP), :]))
        copies(pairs, sems)
        total[...] = jnp.dot(right[lo : lo + B, :], stack[...], preferred_element_type=F32)
        k = at[2]
        keep[...] = total[rows(H * k, H), :]
        give[...] = total[rows(H * (1 - k), H), :].astype(BF)

    return call(
        body,
        [sds((H, W), F32), sds((H, W))],
        at,
        apart=[*blocks, *wait_for],
        vmem=[right],
        scratch=[pltpu.VMEM((4 * B, W), BF), pltpu.VMEM((B, W), F32), pltpu.SemaphoreType.DMA((2 * n,))],
        flops=2 * B * W * 4 * B,
        limit=24,
    )


def left_piece(at, direction, left, d):
    cols = pl.ds(pl.multiple_of(chip_at(at, *d) * W, 128), W)
    return jnp.dot(direction, left[:, cols], preferred_element_type=F32).astype(BF)


EARLY = [(2, 1), (1, 1), (-1, 1)]
LATE = [(2, 0), (0, 1), (1, 0), (-1, 0), (0, 0)]


def moments(at, keep, near, far, avg, sq, left):
    def body(at, keep, near, far, avg, sq, left, new_avg, new_sq, direction, *outs):
        rotated = keep[...] + near[...].astype(F32) + far[...].astype(F32)
        a = 0.9 * avg[...] + 0.1 * rotated
        s = 0.95 * sq[...] + 0.05 * rotated * rotated
        new_avg[...] = a
        new_sq[...] = s
        direction[...] = (a / first_fix / (jnp.sqrt(s / second_fix) + 1e-08)).astype(BF)
        for d, out in zip(EARLY, outs):
            out[...] = left_piece(at, direction[...], left, d)

    out = [sds((H, W), F32), sds((H, W), F32), sds((H, W))] + [sds((H, W))] * 3
    a, s, direction, *parts = call(
        body, out, at, vmem=(keep, near, far, avg, sq, left), flops=2 * H * W * 3 * W, limit=24
    )
    return a, s, direction, dict(zip(EARLY, parts))


def left_back(at, direction, left):
    def body(at, direction, left, *outs):
        for d, out in zip(LATE, outs):
            out[...] = left_piece(at, direction[...], left, d)

    return dict(zip(LATE, call(body, [sds((H, W))] * 5, at, vmem=(direction, left), flops=2 * H * W * 5 * W, limit=24)))


def right_back(at, blocks, right, which, wait_for=()):
    def body(at, *rest):
        own, near, far, far_near, right = rest[len(wait_for) : len(wait_for) + 5]
        outs, stack = rest[len(wait_for) + 5 : -1], rest[-1]
        k = at[2]
        stack[rows(H * k, H), :] = own[...]
        stack[rows(H * (1 - k), H), :] = near[...]
        stack[rows(B + H * k, H), :] = far[...]
        stack[rows(B + H * (1 - k), H), :] = far_near[...]
        chosen = jnp.concatenate([right[rows(ring_at(at, d) * H, H), :] for d in which], 0)
        total = jnp.dot(chosen, stack[...], preferred_element_type=F32).astype(BF)
        for i in range(2 * len(which)):
            outs[i][...] = total[STEP * i : STEP * i + STEP]

    n = len(which)
    outs = call(
        body,
        [sds((STEP, W))] * (2 * n),
        at,
        apart=wait_for,
        vmem=(*blocks, right),
        scratch=[pltpu.VMEM((W, W), BF)],
        flops=2 * n * H * W * W,
        limit=24,
    )
    return [dict(zip(which, outs[h::2])) for h in range(2)]


def per_device(gradient, left_basis, right_basis, exp_avg, exp_avg_sq):
    row, col = lax.axis_index("row"), lax.axis_index("col")
    k, xh = row % 2, col // 8
    at = jnp.stack([row // 4, row // 2 % 2, k, xh, col % 8]).astype(jnp.int32)

    x, top, bottom = to_half(at, gradient, move(gradient, k=1), [(0, H), (0, STEP), (STEP, STEP)], far_sds)
    pieces = gather_yx(x, top, bottom)
    own_left = after(left_basis.T, pieces[1][0], pieces[2][0], pieces[3][0], *pieces[6])
    own_right = right_basis.T
    half = 4 * B
    sent = lax.dynamic_slice(own_right, (0, (1 - xh) * 2 * half + k * half), (B, half))
    got = move(sent, xh=1, xl=1)
    kept = lax.dynamic_slice(own_right, (0, xh * 2 * half), (B, 2 * half))
    left = both_left(at, own_left, move(own_left, k=1))

    x = times_left(at, pieces, left)
    pieces = [gather_z(x[0], True), gather_z(x[1], False)]
    got = after(got, *pieces[0][3:5], *pieces[1][3:5])
    right_turned, right = right_parts(at, kept, got, move(got, k=1))
    exp_avg, exp_avg_sq = after(exp_avg, x[0]), after(exp_avg_sq, x[0])
    (avg,) = to_half(at, exp_avg, move(exp_avg, k=1), [(0, H)])
    (sq,) = to_half(at, exp_avg_sq, move(exp_avg_sq, k=1), [(0, H)])
    far, give = times_right(at, pieces, right_turned, B, (avg, sq))
    far = move(add(far, move(give, k=1)), xh=1)
    keep, give = times_right(at, pieces, right_turned, 0)
    a, s, direction, part = moments(at, keep, move(give, k=1), far, avg, sq, left)
    part |= left_back(at, direction, left)
    new_avg = from_half(at, [a], [move(a, k=1)])
    new_sq = from_half(at, [s], [move(s, k=1)])

    own = scatter_yx(part)
    far = move(own, xh=1)
    blocks = (own, move(own, k=1), far, move(far, k=1))
    early = right_back(at, blocks, right, [-3, 3, 4], (new_avg, new_sq))
    late = right_back(at, blocks, right, [-2, 2, -1, 1, 0])
    ends = [scatter_z(early[h] | late[h], h == 0) for h in range(2)]
    update = from_half(at, ends, [move(e, k=1) for e in ends])
    return (new_avg, new_sq, update)


def solution(mesh):
    placed = (P("row", "col"), P(None, "row"), P(None, "col"), P("row", "col"), P("row", "col"))
    return jax.shard_map(
        per_device,
        mesh=mesh,
        in_specs=placed,
        out_specs=(P("row", "col"), P("row", "col"), P("row", "col")),
        check_vma=False,
    )
```

```python
import jax
import jax.numpy as jnp
import numpy as np
from jax import lax
from jax.experimental import pallas as pl
from jax.experimental.pallas import tpu as pltpu
from jax.sharding import PartitionSpec as P

first_fix = 0.9999734386
second_fix = 0.9940794709

AXES = ("row", "col")
SIZES = {"y": 4, "xl": 2, "k": 2, "xh": 2, "z": 8}
BF, F32 = jnp.bfloat16, jnp.float32
B, H, W = 320, 160, 640
YX = [(0, 0), (-1, 0), (1, 0), (0, 1), (-1, 1), (1, 1), (2, 0), (2, 1)]
ZS = [0, -1, 1, -2, 2, -3, 3, 4]
STEP = 80
C = 384


def place(i):
    r, c = divmod(i, 16)
    return {"y": r // 4, "xl": r // 2 % 2, "k": r % 2, "xh": c // 8, "z": c % 8}


def move(x, **steps):
    pairs = []
    for i in range(256):
        d = place(i)
        for name, step in steps.items():
            d[name] = (d[name] + step) % SIZES[name]
        pairs.append((i, (d["y"] * 4 + d["xl"] * 2 + d["k"]) * 16 + d["xh"] * 8 + d["z"]))
    return lax.ppermute(x, AXES, pairs)


ANY = pl.BlockSpec(memory_space=pl.ANY)
VMEM = pl.BlockSpec(memory_space=pltpu.VMEM)
SMEM = pl.BlockSpec(memory_space=pltpu.SMEM)


def call(body, out, at, apart=(), vmem=(), scratch=(), limit=40, flops=0, out_spec=None):
    args = [at, *apart, *vmem]
    size = sum(a.size * a.dtype.itemsize for a in args) + sum(
        int(np.prod(o.shape)) * jnp.dtype(o.dtype).itemsize for o in out
    )
    return pl.pallas_call(
        body,
        out_shape=list(out),
        in_specs=[SMEM] + [ANY] * len(apart) + [VMEM] * len(vmem),
        out_specs=[out_spec or VMEM] * len(out),
        scratch_shapes=list(scratch),
        compiler_params=pltpu.CompilerParams(vmem_limit_bytes=limit << 20),
        cost_estimate=pl.CostEstimate(flops=flops, bytes_accessed=size, transcendentals=0),
    )(*args)


def sds(shape, dtype=BF):
    return jax.ShapeDtypeStruct(shape, dtype)


def far_sds(shape, dtype=BF):
    return pltpu.HBM(shape, dtype)


def in_hbm(x):
    return pltpu.with_memory_space_constraint(x, pltpu.HBM)


def after(x, *others):
    return lax.optimization_barrier((x, *others))[0]


def chip_at(at, dy, p):
    return lax.rem(at[0] + dy + 4, 4) * 2 + lax.rem(at[1] + p, 2)


def ring_at(at, d):
    return lax.rem(at[4] + d + 8, 8)


def copies(pairs, sems):
    started = []
    for n, (a, b) in enumerate(pairs):
        c = pltpu.make_async_copy(a, b, sems.at[n])
        c.start()
        started.append(c)
    for c in started:
        c.wait()


def rows(i, n):
    return pl.ds(pl.multiple_of(i, 16), n)


def to_half(at, own, other, parts, shape=sds):
    dt = own.dtype

    def body(at, own, other, *rest):
        outs, (stack, turned) = rest[: len(parts)], rest[len(parts) :]
        k = at[2]
        stack[rows(B * k, B), 0:B] = own[...]
        stack[rows(B * (1 - k), B), 0:B] = other[...]
        turned[...] = jnp.transpose(stack[...])
        for out, (lo, n) in zip(outs, parts):
            out[...] = turned[rows(H * k + lo, n), :]

    return call(
        body,
        [shape((n, W), dt) for _, n in parts],
        at,
        vmem=(own, other),
        scratch=[pltpu.VMEM((W, 384), dt), pltpu.VMEM((384, W), dt)],
        limit=16,
        out_spec=pl.BlockSpec() if shape is far_sds else None,
    )


def from_half(at, own, other):
    n = len(own)
    dt = own[0].dtype

    def body(at, *rest):
        mine, theirs, (out, stack, turned) = rest[:n], rest[n : 2 * n], rest[2 * n :]
        k = at[2]
        lo = 0
        for a, b in zip(mine, theirs):
            h = a.shape[0]
            stack[rows(H * k + lo, h), :] = a[...]
            stack[rows(H * (1 - k) + lo, h), :] = b[...]
            lo += h
        turned[...] = jnp.transpose(stack[...])
        out[...] = turned[rows(B * k, B), 0:B]

    return call(
        body,
        [sds((B, B), dt)],
        at,
        vmem=(*own, *other),
        scratch=[pltpu.VMEM((384, W), dt), pltpu.VMEM((W, 384), dt)],
        limit=16,
    )[0]


def both_left(at, own, other):
    def body(at, own, other, out, sems):
        k = at[2]
        copies([(own, out.at[rows(B * k, B), :]), (other, out.at[rows(B * (1 - k), B), :])], sems)

    return call(
        body, [sds((W, 16 * B))], at, apart=(own, other), scratch=[pltpu.SemaphoreType.DMA((2,))], limit=4, out_spec=ANY
    )[0]


def right_parts(at, own, got, passed):
    def body(at, own, got, passed, flat, stack, turned):
        k = at[2]
        stack[B:C, :] = jnp.zeros((C - B, 8 * B), BF)
        stack[C + B :, :] = jnp.zeros((C - B, 8 * B), BF)
        stack[0:B, :] = own[...]
        wide = 4 * B
        stack[C : C + B, pl.ds(pl.multiple_of(wide * k, 128), wide)] = got[...]
        stack[C : C + B, pl.ds(pl.multiple_of(wide * (1 - k), 128), wide)] = passed[...]
        for t in range(20):
            turned[128 * t : 128 * t + 128, :] = jnp.transpose(stack[:, 128 * t : 128 * t + 128])
        for z in range(8):
            flat[H * z : H * z + H, :] = turned[rows(B * z + H * k, H), :]

    return call(
        body,
        [sds((4 * B, 2 * C))],
        at,
        vmem=(own, got, passed),
        scratch=[pltpu.VMEM((2 * C, 8 * B), BF), pltpu.VMEM((8 * B, 2 * C), BF)],
        limit=24,
    )[0]


def gather_yx(x, top, bottom):
    side = move(x, xl=1)
    behind, ahead = move(x, y=1), move(x, y=-1)
    far = [move(top, y=2), move(bottom, y=-2)]
    side_behind, side_ahead = move(side, y=1), move(side, y=-1)
    side_far = [move(f, xl=1) for f in far]
    return [[x], [behind], [ahead], [side], [side_behind], [side_ahead], far, side_far]


def add(*xs):
    total = xs[0].astype(F32)
    for x in xs[1:]:
        total = total + x.astype(F32)
    return total.astype(BF)


def scatter_yx(part):
    far = add(part[2, 0], move(part[2, 1], xl=1))
    side = add(part[0, 1], move(part[1, 1], y=1), move(part[-1, 1], y=-1))
    near = [move(part[1, 0], y=1), move(part[-1, 0], y=-1)]
    far = jnp.concatenate([move(far[:STEP], y=2), move(far[STEP:], y=-2)], 0)
    return add(part[0, 0], *near, far, move(side, xl=1))


def gather_z(x):
    plus = minus = x
    got = [[x]]
    for _ in range(3):
        plus, minus = move(plus, z=1), move(minus, z=-1)
        got += [[plus], [minus]]
        plus, minus = lax.optimization_barrier((plus, minus))
    return got + [[move(plus[:STEP], z=1), move(minus[STEP:], z=-1)]]


def scatter_z(part):
    plus, minus = move(part[4][:STEP], z=1), move(part[4][STEP:], z=-1)
    plus = jnp.concatenate([add(part[3][:STEP], plus), part[3][STEP:]], 0)
    minus = jnp.concatenate([part[-3][:STEP], add(part[-3][STEP:], minus)], 0)
    for s in (2, 1, 0):
        plus, minus = lax.optimization_barrier((plus, minus))
        plus, minus = move(plus, z=1), move(minus, z=-1)
        if s:
            plus, minus = add(part[s], plus), add(part[-s], minus)
    return add(part[0], plus, minus)


def times_left(at, which, pieces, left, before=None):
    flat = [(i, n, x) for i, xs in enumerate(pieces) for n, x in enumerate(xs)]
    n = len(flat)
    wide = len(which) * W

    def body(at, *rest):
        blocks, left, out, stack, sems = rest[:n], rest[n], *rest[-3:]
        copies([(r, stack.at[STEP * h : STEP * h + r.shape[0], W * i : W * i + W]) for (i, h, _), r in zip(flat, blocks)], sems)
        total = rest[n + 1][...] if before is not None else jnp.zeros((H, W), F32)
        for i, (dy, p) in enumerate(which):
            cols = pl.ds(pl.multiple_of(chip_at(at, dy, p) * W, 128), W)
            total += lax.dot_general(
                stack[:, W * i : W * i + W], left[:, cols], (((1,), (1,)), ((), ())), preferred_element_type=F32
            )
        out[...] = total.astype(out.dtype)

    last = before is not None
    return call(
        body,
        [far_sds((H, W)) if last else sds((H, W), F32)],
        at,
        apart=[x for _, _, x in flat],
        vmem=[left, before] if last else [left],
        scratch=[pltpu.VMEM((H, wide), BF), pltpu.SemaphoreType.DMA((n,))],
        flops=2 * H * W * wide,
        limit=24,
        out_spec=pl.BlockSpec() if last else None,
    )[0]


def times_right(at, which, pieces, right, lo, width, before=None):
    flat = [(i, h, x) for i, xs in enumerate(pieces) for h, x in enumerate(xs)]
    n = len(flat)
    deep = len(which) * H

    def body(at, *rest):
        blocks, right, stack, factor, sems = rest[:n], rest[n], *rest[-3:]
        copies([(r, stack.at[H * i + STEP * h : H * i + STEP * h + r.shape[0], :]) for (i, h, _), r in zip(flat, blocks)], sems)
        for i, d in enumerate(which):
            factor[H * i : H * i + H, :] = right[rows(ring_at(at, d) * H, H), lo : lo + width]
        part = lax.dot_general(stack[...], factor[...], (((0,), (0,)), ((), ())), preferred_element_type=F32)
        if before is None:
            rest[n + 1][...] = part
            return
        keep, give, total = rest[n + 2], rest[n + 3], rest[n + 4]
        total[...] = rest[n + 1][:, lo : lo + width] + part
        k = at[2]
        keep[...] = total[rows(B * k, B), 0:B]
        give[...] = total[rows(B * (1 - k), B), 0:B].astype(BF)

    scratch = [pltpu.VMEM((deep, W), BF), pltpu.VMEM((deep, width), BF), pltpu.SemaphoreType.DMA((n,))]
    flops = 2 * W * width * deep
    args = [x for _, _, x in flat]
    if before is None:
        return call(body, [sds((W, width), F32)], at, apart=args, vmem=[right], scratch=scratch, flops=flops, limit=24)[0]
    return call(
        body,
        [sds((B, B), F32), sds((B, B))],
        at,
        apart=args,
        vmem=[right, before],
        scratch=[pltpu.VMEM((W, width), F32), *scratch],
        flops=flops,
        limit=24,
    )


def left_piece(at, direction, left, d):
    cols = pl.ds(pl.multiple_of(chip_at(at, *d) * W, 128), W)
    return jnp.dot(direction, left[:, cols], preferred_element_type=F32).astype(BF)


EARLY = [(2, 1), (1, 1), (-1, 1)]
LATE = [(2, 0), (0, 1), (1, 0), (-1, 0), (0, 0)]


def moments(at, keep, near, far, avg, sq):
    def body(at, keep, near, far, avg, sq, new_avg, new_sq, direction):
        rotated = keep[...] + near[...].astype(F32) + far[...].astype(F32)
        a = 0.9 * avg[...] + 0.1 * rotated
        s = 0.95 * sq[...] + 0.05 * rotated * rotated
        new_avg[...] = a
        new_sq[...] = s
        direction[...] = (a / first_fix / (jnp.sqrt(s / second_fix) + 1e-08)).astype(BF)

    out = [sds((B, B), F32), sds((B, B), F32), sds((B, B))]
    return call(body, out, at, vmem=(keep, near, far, avg, sq), limit=16)


def left_early(at, own, other, left):
    def body(at, own, other, left, turned_out, *rest):
        outs, (stack, turned) = rest[:3], rest[3:]
        k = at[2]
        stack[rows(B * k, B), 0:B] = own[...]
        stack[rows(B * (1 - k), B), 0:B] = other[...]
        turned[...] = jnp.transpose(stack[...])
        direction = turned[rows(H * k, H), :]
        turned_out[...] = direction
        for d, out in zip(EARLY, outs):
            out[...] = left_piece(at, direction, left, d)

    direction, *parts = call(
        body,
        [sds((H, W))] * 4,
        at,
        vmem=(own, other, left),
        scratch=[pltpu.VMEM((W, C), BF), pltpu.VMEM((C, W), BF)],
        flops=2 * H * W * 3 * W,
        limit=24,
    )
    return direction, dict(zip(EARLY, parts))


def left_back(at, direction, left):
    def body(at, direction, left, *outs):
        for d, out in zip(LATE, outs):
            out[...] = left_piece(at, direction[...], left, d)

    return dict(zip(LATE, call(body, [sds((H, W))] * 5, at, vmem=(direction, left), flops=2 * H * W * 5 * W, limit=24)))


def right_back(at, blocks, right, which):
    def body(at, *rest):
        own, near, far, far_near, right = rest[:5]
        outs, stack = rest[5:-1], rest[-1]
        k = at[2]
        stack[B:C, :] = jnp.zeros((C - B, W), BF)
        stack[C + B :, :] = jnp.zeros((C - B, W), BF)
        stack[rows(H * k, H), :] = own[...]
        stack[rows(H * (1 - k), H), :] = near[...]
        stack[rows(C + H * k, H), :] = far[...]
        stack[rows(C + H * (1 - k), H), :] = far_near[...]
        chosen = jnp.concatenate([right[rows(ring_at(at, d) * H, H), :] for d in which], 0)
        total = jnp.dot(chosen, stack[...], preferred_element_type=F32).astype(BF)
        for i in range(len(which)):
            outs[i][...] = total[H * i : H * i + H]

    n = len(which)
    outs = call(
        body,
        [sds((H, W))] * n,
        at,
        vmem=(*blocks, right),
        scratch=[pltpu.VMEM((2 * C, W), BF)],
        flops=2 * n * H * W * W,
        limit=24,
    )
    return dict(zip(which, outs))


def per_device(gradient, left_basis, right_basis, exp_avg, exp_avg_sq):
    row, col = lax.axis_index("row"), lax.axis_index("col")
    k, xh = row % 2, col // 8
    at = jnp.stack([row // 4, row // 2 % 2, k, xh, col % 8]).astype(jnp.int32)

    gradient_far = move(gradient, k=1)
    own_left = after(left_basis.T, gradient_far)
    far_left = move(own_left, k=1)
    left = both_left(at, in_hbm(own_left), in_hbm(far_left))
    x, top, bottom = to_half(at, gradient, gradient_far, [(0, H), (0, STEP), (STEP, STEP)], far_sds)
    pieces = gather_yx(x, top, after(bottom, far_left))
    half = 4 * B
    sent = lax.dynamic_slice(right_basis.T, (0, (1 - xh) * 2 * half + k * half), (B, half))
    got = move(after(sent, pieces[1][0], pieces[2][0], pieces[3][0], *pieces[6]), xh=1, xl=1)
    kept = lax.dynamic_slice(right_basis.T, (0, xh * 2 * half), (B, 2 * half))

    part = times_left(at, YX[:4], pieces[:4], left)
    x = times_left(at, YX[4:], pieces[4:], left, part)
    pieces = gather_z(x)
    got = after(got, *pieces[3], *pieces[4])
    right = right_parts(at, kept, got, move(got, k=1))
    part = times_right(at, ZS[:5], pieces[:5], right, 0, 2 * C)
    far, give = times_right(at, ZS[5:], pieces[5:], right, C, C, part)
    far = move(add(far, move(give, k=1)), xh=1)
    keep, give = times_right(at, ZS[5:], pieces[5:], right, 0, C, part)
    new_avg, new_sq, direction = moments(at, keep, move(give, k=1), far, exp_avg, exp_avg_sq)
    direction, part = left_early(at, direction, move(direction, k=1), left)
    part |= left_back(at, direction, left)

    own = scatter_yx(part)
    far = move(own, xh=1)
    blocks = (own, move(own, k=1), far, move(far, k=1))
    part = right_back(at, blocks, right, [3, -3, 4]) | right_back(at, blocks, right, [-2, 2, -1, 1, 0])
    end = scatter_z(part)
    update = from_half(at, [end], [move(end, k=1)])
    return (new_avg, new_sq, update)


def solution(mesh):
    placed = (P("row", "col"), P(None, "row"), P(None, "col"), P("row", "col"), P("row", "col"))
    return jax.shard_map(
        per_device,
        mesh=mesh,
        in_specs=placed,
        out_specs=(P("row", "col"), P("row", "col"), P("row", "col")),
        check_vma=False,
    )
```

```python
import jax
import jax.numpy as jnp
import numpy as np
from jax import lax
from jax.experimental import pallas as pl
from jax.experimental.pallas import tpu as pltpu
from jax.sharding import PartitionSpec as P

first_fix = 0.9999734386
second_fix = 0.9940794709

AXES = ("row", "col")
SIZES = {"y": 4, "xl": 2, "k": 2, "xh": 2, "z": 8}
BF, F32 = jnp.bfloat16, jnp.float32
B, H, W = 320, 160, 640
YX = [(0, 0), (-1, 0), (1, 0), (0, 1), (-1, 1), (1, 1), (2, 0), (2, 1)]
ZS = [0, -1, 1, -2, 2, -3, 3, 4]
STEP = 80
C = 384


def place(i):
    r, c = divmod(i, 16)
    return {"y": r // 4, "xl": r // 2 % 2, "k": r % 2, "xh": c // 8, "z": c % 8}


def move(x, **steps):
    pairs = []
    for i in range(256):
        d = place(i)
        for name, step in steps.items():
            d[name] = (d[name] + step) % SIZES[name]
        pairs.append((i, (d["y"] * 4 + d["xl"] * 2 + d["k"]) * 16 + d["xh"] * 8 + d["z"]))
    return lax.ppermute(x, AXES, pairs)


ANY = pl.BlockSpec(memory_space=pl.ANY)
VMEM = pl.BlockSpec(memory_space=pltpu.VMEM)
SMEM = pl.BlockSpec(memory_space=pltpu.SMEM)


def call(body, out, at, apart=(), vmem=(), scratch=(), limit=40, flops=0, out_spec=None):
    args = [at, *apart, *vmem]
    size = sum(a.size * a.dtype.itemsize for a in args) + sum(
        int(np.prod(o.shape)) * jnp.dtype(o.dtype).itemsize for o in out
    )
    return pl.pallas_call(
        body,
        out_shape=list(out),
        in_specs=[SMEM] + [ANY] * len(apart) + [VMEM] * len(vmem),
        out_specs=[out_spec or VMEM] * len(out),
        scratch_shapes=list(scratch),
        compiler_params=pltpu.CompilerParams(vmem_limit_bytes=limit << 20),
        cost_estimate=pl.CostEstimate(flops=flops, bytes_accessed=size, transcendentals=0),
    )(*args)


def sds(shape, dtype=BF):
    return jax.ShapeDtypeStruct(shape, dtype)


def far_sds(shape, dtype=BF):
    return pltpu.HBM(shape, dtype)


def in_hbm(x):
    return pltpu.with_memory_space_constraint(x, pltpu.HBM)


def in_vmem(x):
    return pltpu.with_memory_space_constraint(x, pltpu.VMEM)


def after(x, *others):
    return lax.optimization_barrier((x, *others))[0]


def chip_at(at, dy, p):
    return lax.rem(at[0] + dy + 4, 4) * 2 + lax.rem(at[1] + p, 2)


def ring_at(at, d):
    return lax.rem(at[4] + d + 8, 8)


def copies(pairs, sems):
    started = []
    for n, (a, b) in enumerate(pairs):
        c = pltpu.make_async_copy(a, b, sems.at[n])
        c.start()
        started.append(c)
    for c in started:
        c.wait()


def rows(i, n):
    return pl.ds(pl.multiple_of(i, 16), n)


def to_half(at, own, other, parts, shape=sds):
    dt = own.dtype

    def body(at, own, other, *rest):
        outs, (stack, turned, mine, sems) = rest[: len(parts)], rest[len(parts) :]
        k = at[2]
        copy = pltpu.make_async_copy(own, mine, sems.at[0])
        copy.start()
        stack[rows(B * (1 - k), B), 0:B] = other[...]
        copy.wait()
        stack[rows(B * k, B), 0:B] = mine[...]
        turned[...] = jnp.transpose(stack[...])
        for out, (lo, n) in zip(outs, parts):
            out[...] = turned[rows(H * k + lo, n), :]

    return call(
        body,
        [shape((n, W), dt) for _, n in parts],
        at,
        apart=[in_hbm(own)],
        vmem=[other],
        scratch=[pltpu.VMEM((W, C), dt), pltpu.VMEM((C, W), dt), pltpu.VMEM((B, B), dt), pltpu.SemaphoreType.DMA((1,))],
        limit=16,
        out_spec=pl.BlockSpec() if shape is far_sds else None,
    )


def from_half(at, own, other):
    n = len(own)
    dt = own[0].dtype

    def body(at, *rest):
        mine, theirs, (out, stack, turned) = rest[:n], rest[n : 2 * n], rest[2 * n :]
        k = at[2]
        lo = 0
        for a, b in zip(mine, theirs):
            h = a.shape[0]
            stack[rows(H * k + lo, h), :] = a[...]
            stack[rows(H * (1 - k) + lo, h), :] = b[...]
            lo += h
        turned[...] = jnp.transpose(stack[...])
        out[...] = turned[rows(B * k, B), 0:B]

    return call(
        body,
        [sds((B, B), dt)],
        at,
        vmem=(*own, *other),
        scratch=[pltpu.VMEM((384, W), dt), pltpu.VMEM((W, 384), dt)],
        limit=16,
    )[0]


def both_left(at, own, other):
    def body(at, own, other, out, sems):
        k = at[2]
        pairs = []
        for i in range(5):
            part = slice(64 * i, 64 * i + 64)
            pairs.append((own.at[part, :], out.at[rows(B * k + 64 * i, 64), :]))
            pairs.append((other.at[part, :], out.at[rows(B * (1 - k) + 64 * i, 64), :]))
        copies(pairs, sems)

    return in_vmem(
        call(
            body,
            [sds((W, 16 * B))],
            at,
            apart=(own, other),
            scratch=[pltpu.SemaphoreType.DMA((10,))],
            limit=4,
            out_spec=ANY,
        )[0]
    )


def right_half(at, parts):
    def body(at, *rest):
        parts, (out, stack, turned) = rest[:-3], rest[-3:]
        k = at[2]
        stack[B:, :] = jnp.zeros((C - B, 8 * B), BF)
        wide = parts[0].shape[1]
        for part, i in zip(parts, (k, 1 - k)):
            to = pl.ds(pl.multiple_of(wide * i, 128), wide) if len(parts) > 1 else slice(None)
            stack[0:B, to] = part[...]
        for t in range(20):
            turned[128 * t : 128 * t + 128, :] = jnp.transpose(stack[:, 128 * t : 128 * t + 128])
        for z in range(8):
            out[H * z : H * z + H, :] = turned[rows(B * z + H * k, H), :]

    return call(
        body,
        [sds((4 * B, C))],
        at,
        vmem=parts,
        scratch=[pltpu.VMEM((C, 8 * B), BF), pltpu.VMEM((8 * B, C), BF)],
        limit=24,
    )[0]


def add(*xs):
    total = xs[0].astype(F32)
    for x in xs[1:]:
        total = total + x.astype(F32)
    return total.astype(BF)


def scatter_yx(part):
    far = add(part[2, 0], move(part[2, 1], xl=1))
    side = add(part[0, 1], move(part[1, 1], y=1), move(part[-1, 1], y=-1))
    near = [move(part[1, 0], y=1), move(part[-1, 0], y=-1)]
    far = jnp.concatenate([move(far[:STEP], y=2), move(far[STEP:], y=-2)], 0)
    return add(part[0, 0], *near, far, move(side, xl=1))


def gather_z(x):
    plus = minus = x
    got = [[x]]
    for _ in range(3):
        plus, minus = move(plus, z=1), move(minus, z=-1)
        got += [[plus], [minus]]
        plus, minus = lax.optimization_barrier((plus, minus))
    return got + [[move(plus[:STEP], z=1), move(minus[STEP:], z=-1)]]


def scatter_z(part):
    plus, minus = move(part[4][:STEP], z=1), move(part[4][STEP:], z=-1)
    plus = jnp.concatenate([add(part[3][:STEP], plus), part[3][STEP:]], 0)
    minus = jnp.concatenate([part[-3][:STEP], add(part[-3][STEP:], minus)], 0)
    for s in (2, 1, 0):
        plus, minus = lax.optimization_barrier((plus, minus))
        plus, minus = move(plus, z=1), move(minus, z=-1)
        if s:
            plus, minus = add(part[s], plus), add(part[-s], minus)
    return add(part[0], plus, minus)


def times_left(at, which, pieces, left, before=None):
    flat = [(i, n, x) for i, xs in enumerate(pieces) for n, x in enumerate(xs)]
    n = len(flat)
    wide = len(which) * W

    def body(at, *rest):
        blocks, left, out, stack, sems = rest[:n], rest[n], *rest[-3:]
        waits = [[] for _ in which]
        for m, ((i, h, _), r) in enumerate(zip(flat, blocks)):
            to = stack.at[STEP * h : STEP * h + r.shape[0], W * i : W * i + W]
            copy = pltpu.make_async_copy(r, to, sems.at[m])
            copy.start()
            waits[i].append(copy)
        total = rest[n + 1][...] if before is not None else jnp.zeros((H, W), F32)
        for i, (dy, p) in enumerate(which):
            for copy in waits[i]:
                copy.wait()
            cols = pl.ds(pl.multiple_of(chip_at(at, dy, p) * W, 128), W)
            total += lax.dot_general(
                stack[:, W * i : W * i + W], left[:, cols], (((1,), (1,)), ((), ())), preferred_element_type=F32
            )
        out[...] = total.astype(out.dtype)

    last = before is not None
    return call(
        body,
        [far_sds((H, W)) if last else sds((H, W), F32)],
        at,
        apart=[x for _, _, x in flat],
        vmem=[left, before] if last else [left],
        scratch=[pltpu.VMEM((H, wide), BF), pltpu.SemaphoreType.DMA((n,))],
        flops=2 * H * W * wide,
        limit=24,
        out_spec=pl.BlockSpec() if last else None,
    )[0]


def times_right(at, which, pieces, right, before=None):
    flat = [(i, h, x) for i, xs in enumerate(pieces) for h, x in enumerate(xs)]
    n = len(flat)
    deep = len(which) * H

    def body(at, *rest):
        blocks, right, stack, factor, sems = rest[:n], rest[n : n + 2], *rest[-3:]
        started = []
        for m, ((i, h, _), r) in enumerate(zip(flat, blocks)):
            to = stack.at[H * i + STEP * h : H * i + STEP * h + r.shape[0], :]
            started.append(pltpu.make_async_copy(r, to, sems.at[m]))
            started[-1].start()
        for i, d in enumerate(which):
            for side in range(2):
                factor[H * i : H * i + H, C * side : C * side + C] = right[side][rows(ring_at(at, d) * H, H), :]
        for copy in started:
            copy.wait()
        part = lax.dot_general(stack[...], factor[...], (((0,), (0,)), ((), ())), preferred_element_type=F32)
        if before is None:
            rest[n + 2][...] = part
            return
        keep, far, give, total = rest[n + 3 : n + 7]
        total[...] = rest[n + 2][...] + part
        mine, theirs = rows(B * at[2], B), rows(B * (1 - at[2]), B)
        keep[...] = total[mine, 0:B]
        far[...] = total[mine, C : C + B]
        give[0:B, :] = total[theirs, 0:B].astype(BF)
        give[B:, :] = total[theirs, C : C + B].astype(BF)

    scratch = [pltpu.VMEM((deep, W), BF), pltpu.VMEM((deep, 2 * C), BF), pltpu.SemaphoreType.DMA((n,))]
    flops = 2 * W * 2 * C * deep
    args = [x for _, _, x in flat]
    if before is None:
        return call(body, [sds((W, 2 * C), F32)], at, apart=args, vmem=right, scratch=scratch, flops=flops, limit=24)[0]
    return call(
        body,
        [sds((B, B), F32), sds((B, B), F32), sds((W, B))],
        at,
        apart=args,
        vmem=[*right, before],
        scratch=[pltpu.VMEM((W, 2 * C), F32), *scratch],
        flops=flops,
        limit=24,
    )


def left_piece(at, direction, left, d):
    cols = pl.ds(pl.multiple_of(chip_at(at, *d) * W, 128), W)
    return jnp.dot(direction, left[:, cols], preferred_element_type=F32).astype(BF)


EARLY = [(2, 1), (1, 1), (-1, 1)]
LATE = [(2, 0), (0, 1), (1, 0), (-1, 0), (0, 0)]


def moments(at, keep, near, far, avg, sq):
    def body(at, keep, near, far, avg, sq, new_avg, new_sq, direction):
        rotated = keep[...] + near[0:B, :].astype(F32) + far[...].astype(F32)
        a = 0.9 * avg[...] + 0.1 * rotated
        s = 0.95 * sq[...] + 0.05 * rotated * rotated
        new_avg[...] = a
        new_sq[...] = s
        direction[...] = (a / first_fix / (jnp.sqrt(s / second_fix) + 1e-08)).astype(BF)

    out = [sds((B, B), F32), sds((B, B), F32), sds((B, B))]
    return call(body, out, at, vmem=(keep, near, far, avg, sq), limit=16)


def left_early(at, own, other, left):
    def body(at, own, other, left, turned_out, *rest):
        outs, (stack, turned) = rest[:3], rest[3:]
        k = at[2]
        stack[rows(B * k, B), 0:B] = own[...]
        stack[rows(B * (1 - k), B), 0:B] = other[...]
        turned[...] = jnp.transpose(stack[...])
        direction = turned[rows(H * k, H), :]
        turned_out[...] = direction
        for d, out in zip(EARLY, outs):
            out[...] = left_piece(at, direction, left, d)

    direction, *parts = call(
        body,
        [sds((H, W))] * 4,
        at,
        vmem=(own, other, left),
        scratch=[pltpu.VMEM((W, C), BF), pltpu.VMEM((C, W), BF)],
        flops=2 * H * W * 3 * W,
        limit=24,
    )
    return direction, dict(zip(EARLY, parts))


def left_back(at, direction, left):
    def body(at, direction, left, *outs):
        for d, out in zip(LATE, outs):
            out[...] = left_piece(at, direction[...], left, d)

    return dict(zip(LATE, call(body, [sds((H, W))] * 5, at, vmem=(direction, left), flops=2 * H * W * 5 * W, limit=24)))


def right_back(at, blocks, right, which):
    def body(at, *rest):
        own, near, far, far_near, right, right_far = rest[:6]
        outs, stack, chosen = rest[6:-2], rest[-2], rest[-1]
        k = at[2]
        stack[B:C, :] = jnp.zeros((C - B, W), BF)
        stack[C + B :, :] = jnp.zeros((C - B, W), BF)
        stack[rows(H * k, H), :] = own[...]
        stack[rows(H * (1 - k), H), :] = near[...]
        stack[rows(C + H * k, H), :] = far[...]
        stack[rows(C + H * (1 - k), H), :] = far_near[...]
        for i, d in enumerate(which):
            chosen[H * i : H * i + H, :C] = right[rows(ring_at(at, d) * H, H), :]
            chosen[H * i : H * i + H, C:] = right_far[rows(ring_at(at, d) * H, H), :]
        total = jnp.dot(chosen[...], stack[...], preferred_element_type=F32).astype(BF)
        for i in range(len(which)):
            outs[i][...] = total[H * i : H * i + H]

    n = len(which)
    outs = call(
        body,
        [sds((H, W))] * n,
        at,
        vmem=(*blocks, *right),
        scratch=[pltpu.VMEM((2 * C, W), BF), pltpu.VMEM((n * H, 2 * C), BF)],
        flops=2 * n * H * W * W,
        limit=24,
    )
    return dict(zip(which, outs))


def per_device(gradient, left_basis, right_basis, exp_avg, exp_avg_sq):
    row, col = lax.axis_index("row"), lax.axis_index("col")
    k, xh = row % 2, col // 8
    at = jnp.stack([row // 4, row // 2 % 2, k, xh, col % 8]).astype(jnp.int32)

    gradient_far = move(gradient, k=1)
    half = 4 * B
    own_left = after(left_basis.T, gradient_far)
    far_left = move(own_left, k=1)
    left = both_left(at, in_hbm(own_left), in_hbm(far_left))
    x, top, bottom = to_half(at, gradient, gradient_far, [(0, H), (0, STEP), (STEP, STEP)], far_sds)
    side = move(x, xl=1)
    behind, ahead = move(x, y=1), move(x, y=-1)
    bottom = after(bottom, far_left)
    far = [move(top, y=2), move(bottom, y=-2)]
    whole = after(right_basis.T, x)
    sent = lax.dynamic_slice(whole, (0, (1 - xh) * 2 * half + k * half), (B, half))
    kept = lax.dynamic_slice(whole, (0, xh * 2 * half), (B, 2 * half))
    own_right = right_half(at, [kept])
    got = move(after(sent, left, own_right, side, behind, ahead, *far), xh=1, xl=1)
    side_in = after(side, left)
    side_behind, side_ahead = move(side_in, y=1), move(side_in, y=-1)
    side_far = [move(f, xl=1) for f in far]

    part = times_left(at, YX[:4], [[x], [behind], [ahead], [side]], left)
    x = times_left(at, YX[4:], [[side_behind], [side_ahead], far, side_far], left, part)
    pieces = gather_z(x)
    got = after(got, *pieces[3], *pieces[4])
    right = (own_right, right_half(at, [got, move(got, k=1)]))
    part = times_right(at, ZS[:5], pieces[:5], right)
    keep, far, give = times_right(at, ZS[5:], pieces[5:], right, part)
    near = move(give, k=1)
    far = move(add(far, near[B:]), xh=1)
    new_avg, new_sq, direction = moments(at, keep, near, far, exp_avg, exp_avg_sq)
    direction, part = left_early(at, direction, move(direction, k=1), left)
    part |= left_back(at, direction, left)

    own = scatter_yx(part)
    far = move(own, xh=1)
    blocks = (own, move(own, k=1), far, move(far, k=1))
    end = scatter_z(right_back(at, blocks, right, ZS))
    update = from_half(at, [end], [move(end, k=1)])
    return (new_avg, new_sq, update)


def solution(mesh):
    placed = (P("row", "col"), P(None, "row"), P(None, "col"), P("row", "col"), P("row", "col"))
    return jax.shard_map(
        per_device,
        mesh=mesh,
        in_specs=placed,
        out_specs=(P("row", "col"), P("row", "col"), P("row", "col")),
        check_vma=False,
    )
```

```python
import jax
import jax.numpy as jnp
import numpy as np
from jax import lax
from jax.experimental import pallas as pl
from jax.experimental.pallas import tpu as pltpu
from jax.sharding import PartitionSpec as P

first_fix = 0.9999734386
second_fix = 0.9940794709

AXES = ("row", "col")
SIZES = {"y": 4, "xl": 2, "k": 2, "xh": 2, "z": 8}
BF, F32 = jnp.bfloat16, jnp.float32
B, H, W = 320, 160, 640
YX = [(0, 0), (-1, 0), (1, 0), (0, 1), (-1, 1), (1, 1), (2, 0), (2, 1)]
STEP = 80
FIRST = 512
C = 384


def place(i):
    r, c = divmod(i, 16)
    return {"y": r // 4, "xl": r // 2 % 2, "k": r % 2, "xh": c // 8, "z": c % 8}


def move(x, **steps):
    pairs = []
    for i in range(256):
        d = place(i)
        k = d["k"]
        for name, step in steps.items():
            d[name] = (d[name] + (step[k] if isinstance(step, tuple) else step)) % SIZES[name]
        pairs.append((i, (d["y"] * 4 + d["xl"] * 2 + d["k"]) * 16 + d["xh"] * 8 + d["z"]))
    return lax.ppermute(x, AXES, pairs)


ANY = pl.BlockSpec(memory_space=pl.ANY)
VMEM = pl.BlockSpec(memory_space=pltpu.VMEM)
SMEM = pl.BlockSpec(memory_space=pltpu.SMEM)


def call(body, out, at, apart=(), vmem=(), scratch=(), limit=40, flops=0, out_spec=None):
    args = [at, *apart, *vmem]
    size = sum(a.size * a.dtype.itemsize for a in args) + sum(
        int(np.prod(o.shape)) * jnp.dtype(o.dtype).itemsize for o in out
    )
    return pl.pallas_call(
        body,
        out_shape=list(out),
        in_specs=[SMEM] + [ANY] * len(apart) + [VMEM] * len(vmem),
        out_specs=[out_spec or VMEM] * len(out),
        scratch_shapes=list(scratch),
        compiler_params=pltpu.CompilerParams(vmem_limit_bytes=limit << 20),
        cost_estimate=pl.CostEstimate(flops=flops, bytes_accessed=size, transcendentals=0),
    )(*args)


def sds(shape, dtype=BF):
    return jax.ShapeDtypeStruct(shape, dtype)


def far_sds(shape, dtype=BF):
    return pltpu.HBM(shape, dtype)


def in_hbm(x):
    return pltpu.with_memory_space_constraint(x, pltpu.HBM)


def in_vmem(x):
    return pltpu.with_memory_space_constraint(x, pltpu.VMEM)


def after(x, *others):
    return lax.optimization_barrier((x, *others))[0]


def chip_at(at, dy, p):
    return lax.rem(at[0] + dy + 4, 4) * 2 + lax.rem(at[1] + p, 2)


RING = (1, -1)


def ring_rows(at, d, full):
    start = lax.rem(at[4] + (1 - 2 * at[2]) * d + 8, 8) * B
    k = at[2]
    return [rows(start + H * k, H)] + ([rows(start + H * (1 - k), H)] if full else [])


def copies(pairs, sems):
    started = []
    for n, (a, b) in enumerate(pairs):
        c = pltpu.make_async_copy(a, b, sems.at[n])
        c.start()
        started.append(c)
    for c in started:
        c.wait()


def rows(i, n):
    return pl.ds(pl.multiple_of(i, 16), n)


def to_half(at, own, other, parts, shape=sds):
    dt = own.dtype

    def body(at, own, other, *rest):
        outs, (stack, turned, mine, sems) = rest[: len(parts)], rest[len(parts) :]
        k = at[2]
        copy = pltpu.make_async_copy(own, mine, sems.at[0])
        copy.start()
        stack[rows(B * (1 - k), B), 0:B] = other[...]
        copy.wait()
        stack[rows(B * k, B), 0:B] = mine[...]
        turned[...] = jnp.transpose(stack[...])
        for out, (lo, n) in zip(outs, parts):
            out[...] = turned[rows(H * k + lo, n), :]

    return call(
        body,
        [shape((n, W), dt) for _, n in parts],
        at,
        apart=[in_hbm(own)],
        vmem=[other],
        scratch=[pltpu.VMEM((W, C), dt), pltpu.VMEM((C, W), dt), pltpu.VMEM((B, B), dt), pltpu.SemaphoreType.DMA((1,))],
        limit=16,
        out_spec=pl.BlockSpec() if shape is far_sds else None,
    )


def finish(at, own, other):
    def body(at, own, other, out, stack, turned):
        k = at[2]
        stack[rows(H * k, H), :] = (own[:H, :].astype(F32) + other[H:, :].astype(F32)).astype(BF)
        stack[rows(H * (1 - k), H), :] = (own[H:, :].astype(F32) + other[:H, :].astype(F32)).astype(BF)
        turned[...] = jnp.transpose(stack[...])
        out[...] = turned[rows(B * k, B), 0:B]

    return call(
        body,
        [sds((B, B))],
        at,
        vmem=(own, other),
        scratch=[pltpu.VMEM((C, W), BF), pltpu.VMEM((W, C), BF)],
        limit=16,
    )[0]


def both_left(at, own, other):
    def body(at, own, other, out, sems):
        k = at[2]
        pairs = []
        for i in range(5):
            part = slice(64 * i, 64 * i + 64)
            pairs.append((own.at[part, :], out.at[rows(B * k + 64 * i, 64), :]))
            pairs.append((other.at[part, :], out.at[rows(B * (1 - k) + 64 * i, 64), :]))
        copies(pairs, sems)

    return in_vmem(
        call(
            body,
            [sds((W, 16 * B))],
            at,
            apart=(own, other),
            scratch=[pltpu.SemaphoreType.DMA((10,))],
            limit=4,
            out_spec=ANY,
        )[0]
    )


def right_half(at, mine, theirs=()):
    n = len(mine)

    def body(at, *rest):
        parts, (out, stack) = rest[:-2], rest[-2:]
        k = at[2]
        stack[B:, :] = jnp.zeros((C - B, 8 * B), BF)
        if n == 1:
            stack[0:B, :] = parts[0][...]
        else:
            for i, start in ((0, k), (n, 1 - k)):
                lo = 0
                for part in parts[i : i + n]:
                    wide = part.shape[1]
                    stack[0:B, pl.ds(pl.multiple_of(4 * B * start + lo, 128), wide)] = part[...]
                    lo += wide
        for t in range(20):
            out[128 * t : 128 * t + 128, :] = jnp.transpose(stack[:, 128 * t : 128 * t + 128])

    return call(body, [sds((8 * B, C))], at, vmem=(*mine, *theirs), scratch=[pltpu.VMEM((C, 8 * B), BF)], limit=24)[0]


def add(*xs):
    total = xs[0].astype(F32)
    for x in xs[1:]:
        total = total + x.astype(F32)
    return total.astype(BF)


def scatter_yx(part):
    far = add(part[2, 0], move(part[2, 1], xl=1))
    side = add(part[0, 1], move(part[1, 1], y=1), move(part[-1, 1], y=-1))
    near = [move(part[1, 0], y=1), move(part[-1, 0], y=-1)]
    far = jnp.concatenate([move(far[:STEP], y=2), move(far[STEP:], y=-2)], 0)
    return add(part[0, 0], *near, far, move(side, xl=1))


def gather_z(x):
    got = [x, jnp.concatenate([x, move(x, k=1)], 0)]
    for _ in range(3):
        got.append(move(got[-1], z=RING))
    got.append(move(got[-1][:H], z=RING))
    return [got[0], *got[2:]]


def scatter_z(part):
    own, *near, far = part
    total = move(far, z=RING)
    total = jnp.concatenate([add(near[2][:H], total), near[2][H:]], 0)
    total = add(near[1], move(total, z=RING))
    total = add(near[0], move(total, z=RING))
    total = move(total, z=RING)
    return jnp.concatenate([add(own, total[:H]), total[H:]], 0)


def times_left(at, which, pieces, left, before=None):
    flat = [(i, n, x) for i, xs in enumerate(pieces) for n, x in enumerate(xs)]
    n = len(flat)
    wide = len(which) * W

    def body(at, *rest):
        blocks, left, out, stack, sems = rest[:n], rest[n], *rest[-3:]
        waits = [[] for _ in which]
        for m, ((i, h, _), r) in enumerate(zip(flat, blocks)):
            to = stack.at[STEP * h : STEP * h + r.shape[0], W * i : W * i + W]
            copy = pltpu.make_async_copy(r, to, sems.at[m])
            copy.start()
            waits[i].append(copy)
        total = rest[n + 1][...] if before is not None else jnp.zeros((H, W), F32)
        for i, (dy, p) in enumerate(which):
            for copy in waits[i]:
                copy.wait()
            cols = pl.ds(pl.multiple_of(chip_at(at, dy, p) * W, 128), W)
            total += lax.dot_general(
                stack[:, W * i : W * i + W], left[:, cols], (((1,), (1,)), ((), ())), preferred_element_type=F32
            )
        out[...] = total.astype(out.dtype)

    last = before is not None
    return call(
        body,
        [sds((H, W), BF if last else F32)],
        at,
        apart=[x for _, _, x in flat],
        vmem=[left, before] if last else [left],
        scratch=[pltpu.VMEM((H, wide), BF), pltpu.SemaphoreType.DMA((n,))],
        flops=2 * H * W * wide,
        limit=24,
    )[0]


def times_right(at, which, pieces, right, before=None):
    n = len(pieces)
    deep = sum(x.shape[0] for x in pieces)

    def body(at, *rest):
        blocks, right, stack, factor, sems = rest[:n], rest[n : n + 2], *rest[-3:]
        started = []
        lo = 0
        for m, r in enumerate(blocks):
            started.append(pltpu.make_async_copy(r, stack.at[lo : lo + r.shape[0], :], sems.at[m]))
            started[-1].start()
            lo += r.shape[0]
        lo = 0
        for d, r in zip(which, blocks):
            for at_rows in ring_rows(at, -d, r.shape[0] == B):
                for side in range(2):
                    factor[lo : lo + H, C * side : C * side + C] = right[side][at_rows, :]
                lo += H
        for copy in started:
            copy.wait()
        part = lax.dot_general(stack[...], factor[...], (((0,), (0,)), ((), ())), preferred_element_type=F32)
        if before is None:
            rest[n + 2][...] = part
            return
        keep, far, give, total = rest[n + 3 : n + 7]
        total[...] = rest[n + 2][...] + part
        mine, theirs = rows(B * at[2], B), rows(B * (1 - at[2]), B)
        keep[...] = total[mine, 0:B]
        far[...] = total[mine, C : C + B]
        give[0:B, :] = total[theirs, 0:B].astype(BF)
        give[B:, :] = total[theirs, C : C + B].astype(BF)

    scratch = [pltpu.VMEM((deep, W), BF), pltpu.VMEM((deep, 2 * C), BF), pltpu.SemaphoreType.DMA((n,))]
    flops = 2 * W * 2 * C * deep
    args = pieces
    if before is None:
        return call(body, [sds((W, 2 * C), F32)], at, apart=args, vmem=right, scratch=scratch, flops=flops, limit=24)
    return call(
        body,
        [sds((B, B), F32), sds((B, B), F32), sds((W, B))],
        at,
        apart=args,
        vmem=[*right, before],
        scratch=[pltpu.VMEM((W, 2 * C), F32), *scratch],
        flops=flops,
        limit=24,
    )


def left_piece(at, direction, left, d):
    cols = pl.ds(pl.multiple_of(chip_at(at, *d) * W, 128), W)
    return jnp.dot(direction, left[:, cols], preferred_element_type=F32).astype(BF)


EARLY = [(2, 1), (1, 1), (-1, 1)]
LATE = [(2, 0), (0, 1), (1, 0), (-1, 0), (0, 0)]


def moments(at, keep, near, far, avg, sq):
    def body(at, keep, near, far, avg, sq, new_avg, new_sq, direction):
        rotated = keep[...] + near[0:B, :].astype(F32) + far[...].astype(F32)
        a = 0.9 * avg[...] + 0.1 * rotated
        s = 0.95 * sq[...] + 0.05 * rotated * rotated
        new_avg[...] = a
        new_sq[...] = s
        direction[...] = (a / first_fix / (jnp.sqrt(s / second_fix) + 1e-08)).astype(BF)

    out = [sds((B, B), F32), sds((B, B), F32), sds((B, B))]
    return call(body, out, at, vmem=(keep, near, far, avg, sq), limit=16)


def left_early(at, own, other, left):
    def body(at, own, other, left, turned_out, *rest):
        outs, (stack, turned) = rest[:3], rest[3:]
        k = at[2]
        stack[rows(B * k, B), 0:B] = own[...]
        stack[rows(B * (1 - k), B), 0:B] = other[...]
        turned[...] = jnp.transpose(stack[...])
        direction = turned[rows(H * k, H), :]
        turned_out[...] = direction
        for d, out in zip(EARLY, outs):
            out[...] = left_piece(at, direction, left, d)

    direction, *parts = call(
        body,
        [sds((H, W))] * 4,
        at,
        vmem=(own, other, left),
        scratch=[pltpu.VMEM((W, C), BF), pltpu.VMEM((C, W), BF)],
        flops=2 * H * W * 3 * W,
        limit=24,
    )
    return direction, dict(zip(EARLY, parts))


def left_back(at, direction, left):
    def body(at, direction, left, *outs):
        for d, out in zip(LATE, outs):
            out[...] = left_piece(at, direction[...], left, d)

    return dict(zip(LATE, call(body, [sds((H, W))] * 5, at, vmem=(direction, left), flops=2 * H * W * 5 * W, limit=24)))


def right_back(at, blocks, right):
    which = [(0, H), (1, B), (2, B), (3, B), (4, H)]

    def body(at, *rest):
        own, near, far, far_near, right, right_far = rest[:6]
        outs, stack, chosen = rest[6:-2], rest[-2], rest[-1]
        k = at[2]
        stack[B:C, :] = jnp.zeros((C - B, W), BF)
        stack[C + B :, :] = jnp.zeros((C - B, W), BF)
        stack[rows(H * k, H), :] = own[...]
        stack[rows(H * (1 - k), H), :] = near[...]
        stack[rows(C + H * k, H), :] = far[...]
        stack[rows(C + H * (1 - k), H), :] = far_near[...]
        lo = 0
        for d, n in which:
            for at_rows in ring_rows(at, d, n == B):
                chosen[lo : lo + H, :C] = right[at_rows, :]
                chosen[lo : lo + H, C:] = right_far[at_rows, :]
                lo += H
        total = jnp.dot(chosen[...], stack[...], preferred_element_type=F32).astype(BF)
        lo = 0
        for (_, n), out in zip(which, outs):
            out[...] = total[lo : lo + n]
            lo += n

    return call(
        body,
        [sds((n, W)) for _, n in which],
        at,
        vmem=(*blocks, *right),
        scratch=[pltpu.VMEM((2 * C, W), BF), pltpu.VMEM((4 * B, 2 * C), BF)],
        flops=2 * 4 * B * W * 2 * C,
        limit=32,
    )


def per_device(gradient, left_basis, right_basis, exp_avg, exp_avg_sq):
    row, col = lax.axis_index("row"), lax.axis_index("col")
    k, xh = row % 2, col // 8
    at = jnp.stack([row // 4, row // 2 % 2, k, xh, col % 8]).astype(jnp.int32)

    gradient_far = move(gradient, k=1)
    half = 4 * B
    own_left = after(left_basis.T, gradient_far)
    far_left = move(own_left, k=1)
    left = both_left(at, in_hbm(own_left), in_hbm(far_left))
    x, top, bottom = to_half(at, gradient, gradient_far, [(0, H), (0, STEP), (STEP, STEP)], far_sds)
    side = move(x, xl=1)
    behind, ahead = move(x, y=1), move(x, y=-1)
    bottom = after(bottom, far_left)
    far = [move(top, y=2), move(bottom, y=-2)]
    whole = after(right_basis.T, x)
    sent = lax.dynamic_slice(whole, (0, (1 - xh) * 2 * half + k * half), (B, half))
    kept = lax.dynamic_slice(whole, (0, xh * 2 * half), (B, 2 * half))
    own_right = right_half(at, [kept])
    got = [move(after(sent[:, :FIRST], left, own_right, side, behind, ahead, *far), xh=1, xl=1)]
    side_in = after(side, left)
    side_behind, side_ahead = move(side_in, y=1), move(side_in, y=-1)
    side_far = [move(f, xl=1) for f in far]

    part = times_left(at, YX[:4], [[x], [behind], [ahead], [side]], left)
    got.append(move(after(sent[:, FIRST:], got[0]), xh=1, xl=1))
    x = times_left(at, YX[4:], [[side_behind], [side_ahead], far, side_far], left, after(part, got[0]))
    pieces = gather_z(x)
    got = [got[0], after(got[1], pieces[1])]
    right = (own_right, right_half(at, got, [move(g, k=1) for g in got]))
    part = times_right(at, [0, 1, 2], pieces[:3], right)[0]
    keep, far, give = times_right(at, [3, 4], pieces[3:], right, part)
    near = move(give, k=1)
    far = move(add(far, near[B:]), xh=1)
    new_avg, new_sq, direction = moments(at, keep, near, far, exp_avg, exp_avg_sq)
    direction, part = left_early(at, direction, move(direction, k=1), left)
    part |= left_back(at, direction, left)

    own = scatter_yx(part)
    far = move(own, xh=1)
    blocks = (own, move(own, k=1), far, move(far, k=1))
    end = scatter_z(right_back(at, blocks, right))
    update = finish(at, end, move(end, k=1))
    return (new_avg, new_sq, update)


def solution(mesh):
    placed = (P("row", "col"), P(None, "row"), P(None, "col"), P("row", "col"), P("row", "col"))
    return jax.shard_map(
        per_device,
        mesh=mesh,
        in_specs=placed,
        out_specs=(P("row", "col"), P("row", "col"), P("row", "col")),
        check_vma=False,
    )
```

```python
import jax
import jax.numpy as jnp
import numpy as np
from jax import lax
from jax.experimental import pallas as pl
from jax.experimental.pallas import tpu as pltpu
from jax.sharding import PartitionSpec as P

first_fix = 0.9999734386
second_fix = 0.9940794709

AXES = ("row", "col")
SIZES = {"y": 4, "xl": 2, "k": 2, "xh": 2, "z": 8}
BF, F32 = jnp.bfloat16, jnp.float32
B, H, W = 320, 160, 640
YX = [(0, 0), (-1, 0), (1, 0), (0, 1), (-1, 1), (1, 1), (2, 0), (2, 1)]
ZS = [0, -1, 1, -2, 2, -3, 3, 4]
FIRST = 512
STEP = 80
C = 384


def place(i):
    r, c = divmod(i, 16)
    return {"y": r // 4, "xl": r // 2 % 2, "k": r % 2, "xh": c // 8, "z": c % 8}


def move(x, **steps):
    pairs = []
    for i in range(256):
        d = place(i)
        for name, step in steps.items():
            d[name] = (d[name] + step) % SIZES[name]
        pairs.append((i, (d["y"] * 4 + d["xl"] * 2 + d["k"]) * 16 + d["xh"] * 8 + d["z"]))
    return lax.ppermute(x, AXES, pairs)


ANY = pl.BlockSpec(memory_space=pl.ANY)
VMEM = pl.BlockSpec(memory_space=pltpu.VMEM)
SMEM = pl.BlockSpec(memory_space=pltpu.SMEM)


def call(body, out, at, apart=(), vmem=(), scratch=(), limit=40, flops=0, out_spec=None):
    args = [at, *apart, *vmem]
    size = sum(a.size * a.dtype.itemsize for a in args) + sum(
        int(np.prod(o.shape)) * jnp.dtype(o.dtype).itemsize for o in out
    )
    return pl.pallas_call(
        body,
        out_shape=list(out),
        in_specs=[SMEM] + [ANY] * len(apart) + [VMEM] * len(vmem),
        out_specs=[out_spec or VMEM] * len(out),
        scratch_shapes=list(scratch),
        compiler_params=pltpu.CompilerParams(vmem_limit_bytes=limit << 20),
        cost_estimate=pl.CostEstimate(flops=flops, bytes_accessed=size, transcendentals=0),
    )(*args)


def sds(shape, dtype=BF):
    return jax.ShapeDtypeStruct(shape, dtype)


def far_sds(shape, dtype=BF):
    return pltpu.HBM(shape, dtype)


def in_hbm(x):
    return pltpu.with_memory_space_constraint(x, pltpu.HBM)


def in_vmem(x):
    return pltpu.with_memory_space_constraint(x, pltpu.VMEM)


def after(x, *others):
    return lax.optimization_barrier((x, *others))[0]


def chip_at(at, dy, p):
    return lax.rem(at[0] + dy + 4, 4) * 2 + lax.rem(at[1] + p, 2)


def ring_at(at, d):
    return lax.rem(at[4] + d + 8, 8)


def copies(pairs, sems):
    started = []
    for n, (a, b) in enumerate(pairs):
        c = pltpu.make_async_copy(a, b, sems.at[n])
        c.start()
        started.append(c)
    for c in started:
        c.wait()


def rows(i, n):
    return pl.ds(pl.multiple_of(i, 16), n)


def to_half(at, own, other, parts, shape=sds):
    dt = own.dtype

    def body(at, own, other, *rest):
        outs, (stack, turned, mine, sems) = rest[: len(parts)], rest[len(parts) :]
        k = at[2]
        copy = pltpu.make_async_copy(own, mine, sems.at[0])
        copy.start()
        stack[rows(B * (1 - k), B), 0:B] = other[...]
        copy.wait()
        stack[rows(B * k, B), 0:B] = mine[...]
        turned[...] = jnp.transpose(stack[...])
        for out, (lo, n) in zip(outs, parts):
            out[...] = turned[rows(H * k + lo, n), :]

    return call(
        body,
        [shape((n, W), dt) for _, n in parts],
        at,
        apart=[in_hbm(own)],
        vmem=[other],
        scratch=[pltpu.VMEM((W, C), dt), pltpu.VMEM((C, W), dt), pltpu.VMEM((B, B), dt), pltpu.SemaphoreType.DMA((1,))],
        limit=16,
        out_spec=pl.BlockSpec() if shape is far_sds else None,
    )


def from_half(at, own, other):
    n = len(own)
    dt = own[0].dtype

    def body(at, *rest):
        mine, theirs, (out, stack, turned) = rest[:n], rest[n : 2 * n], rest[2 * n :]
        k = at[2]
        lo = 0
        for a, b in zip(mine, theirs):
            h = a.shape[0]
            stack[rows(H * k + lo, h), :] = a[...]
            stack[rows(H * (1 - k) + lo, h), :] = b[...]
            lo += h
        turned[...] = jnp.transpose(stack[...])
        out[...] = turned[rows(B * k, B), 0:B]

    return call(
        body,
        [sds((B, B), dt)],
        at,
        vmem=(*own, *other),
        scratch=[pltpu.VMEM((384, W), dt), pltpu.VMEM((W, 384), dt)],
        limit=16,
    )[0]


def both_left(at, own, other):
    def body(at, own, other, out, sems):
        k = at[2]
        pairs = []
        for i in range(5):
            part = slice(64 * i, 64 * i + 64)
            pairs.append((own.at[part, :], out.at[rows(B * k + 64 * i, 64), :]))
            pairs.append((other.at[part, :], out.at[rows(B * (1 - k) + 64 * i, 64), :]))
        copies(pairs, sems)

    return in_vmem(
        call(
            body,
            [sds((W, 16 * B))],
            at,
            apart=(own, other),
            scratch=[pltpu.SemaphoreType.DMA((10,))],
            limit=4,
            out_spec=ANY,
        )[0]
    )


def right_half(at, mine, theirs=()):
    n = len(mine)

    def body(at, *rest):
        parts, (out, stack, turned) = rest[:-3], rest[-3:]
        k = at[2]
        stack[B:, :] = jnp.zeros((C - B, 8 * B), BF)
        if n == 1:
            stack[0:B, :] = parts[0][...]
        else:
            for i, start in ((0, k), (n, 1 - k)):
                lo = 0
                for part in parts[i : i + n]:
                    wide = part.shape[1]
                    stack[0:B, pl.ds(pl.multiple_of(4 * B * start + lo, 128), wide)] = part[...]
                    lo += wide
        for t in range(20):
            turned[128 * t : 128 * t + 128, :] = jnp.transpose(stack[:, 128 * t : 128 * t + 128])
        for z in range(8):
            out[H * z : H * z + H, :] = turned[rows(B * z + H * k, H), :]

    return call(
        body,
        [sds((4 * B, C))],
        at,
        vmem=(*mine, *theirs),
        scratch=[pltpu.VMEM((C, 8 * B), BF), pltpu.VMEM((8 * B, C), BF)],
        limit=24,
    )[0]


def add(*xs):
    total = xs[0].astype(F32)
    for x in xs[1:]:
        total = total + x.astype(F32)
    return total.astype(BF)


def scatter_yx(part):
    far = add(part[2, 0], move(part[2, 1], xl=1))
    side = add(part[0, 1], move(part[1, 1], y=1), move(part[-1, 1], y=-1))
    near = [move(part[1, 0], y=1), move(part[-1, 0], y=-1)]
    far = jnp.concatenate([move(far[:STEP], y=2), move(far[STEP:], y=-2)], 0)
    return add(part[0, 0], *near, far, move(side, xl=1))


def gather_z(x):
    plus = minus = x
    got = [[x]]
    for _ in range(3):
        plus, minus = move(plus, z=1), move(minus, z=-1)
        got += [[plus], [minus]]
        plus, minus = lax.optimization_barrier((plus, minus))
    return got + [[move(plus[:STEP], z=1), move(minus[STEP:], z=-1)]]


def scatter_z(part):
    plus, minus = move(part[4][:STEP], z=1), move(part[4][STEP:], z=-1)
    plus = jnp.concatenate([add(part[3][:STEP], plus), part[3][STEP:]], 0)
    minus = jnp.concatenate([part[-3][:STEP], add(part[-3][STEP:], minus)], 0)
    for s in (2, 1, 0):
        plus, minus = lax.optimization_barrier((plus, minus))
        plus, minus = move(plus, z=1), move(minus, z=-1)
        if s:
            plus, minus = add(part[s], plus), add(part[-s], minus)
    return add(part[0], plus, minus)


def times_left(at, which, pieces, left, before=None):
    flat = [(i, n, x) for i, xs in enumerate(pieces) for n, x in enumerate(xs)]
    n = len(flat)
    wide = len(which) * W

    def body(at, *rest):
        blocks, left, out, stack, sems = rest[:n], rest[n], *rest[-3:]
        waits = [[] for _ in which]
        for m, ((i, h, _), r) in enumerate(zip(flat, blocks)):
            to = stack.at[STEP * h : STEP * h + r.shape[0], W * i : W * i + W]
            copy = pltpu.make_async_copy(r, to, sems.at[m])
            copy.start()
            waits[i].append(copy)
        total = rest[n + 1][...] if before is not None else jnp.zeros((H, W), F32)
        for i, (dy, p) in enumerate(which):
            for copy in waits[i]:
                copy.wait()
            cols = pl.ds(pl.multiple_of(chip_at(at, dy, p) * W, 128), W)
            total += lax.dot_general(
                stack[:, W * i : W * i + W], left[:, cols], (((1,), (1,)), ((), ())), preferred_element_type=F32
            )
        out[...] = total.astype(out.dtype)

    last = before is not None
    return call(
        body,
        [sds((H, W), BF if last else F32)],
        at,
        apart=[x for _, _, x in flat],
        vmem=[left, before] if last else [left],
        scratch=[pltpu.VMEM((H, wide), BF), pltpu.SemaphoreType.DMA((n,))],
        flops=2 * H * W * wide,
        limit=24,
    )[0]


def times_right(at, which, pieces, right, before=None):
    flat = [(i, h, x) for i, xs in enumerate(pieces) for h, x in enumerate(xs)]
    n = len(flat)
    deep = len(which) * H

    def body(at, *rest):
        blocks, right, stack, factor, sems = rest[:n], rest[n : n + 2], *rest[-3:]
        started = []
        for m, ((i, h, _), r) in enumerate(zip(flat, blocks)):
            to = stack.at[H * i + STEP * h : H * i + STEP * h + r.shape[0], :]
            started.append(pltpu.make_async_copy(r, to, sems.at[m]))
            started[-1].start()
        for i, d in enumerate(which):
            for side in range(2):
                factor[H * i : H * i + H, C * side : C * side + C] = right[side][rows(ring_at(at, d) * H, H), :]
        for copy in started:
            copy.wait()
        part = lax.dot_general(stack[...], factor[...], (((0,), (0,)), ((), ())), preferred_element_type=F32)
        if before is None:
            rest[n + 2][...] = part
            return
        keep, far, give, total = rest[n + 3 : n + 7]
        total[...] = rest[n + 2][...] + part
        mine, theirs = rows(B * at[2], B), rows(B * (1 - at[2]), B)
        for half in range(2):
            lo, to = H * half, slice(B * half, B * half + B)
            mine, theirs = rows(B * at[2] + lo, H), rows(B * (1 - at[2]) + lo, H)
            keep[:, to] = total[mine, 0:B]
            far[:, to] = total[mine, C : C + B]
            give[0:H, to] = total[theirs, 0:B].astype(BF)
            give[H:, to] = total[theirs, C : C + B].astype(BF)

    scratch = [pltpu.VMEM((deep, W), BF), pltpu.VMEM((deep, 2 * C), BF), pltpu.SemaphoreType.DMA((n,))]
    flops = 2 * W * 2 * C * deep
    args = [x for _, _, x in flat]
    if before is None:
        return call(body, [sds((W, 2 * C), F32)], at, apart=args, vmem=right, scratch=scratch, flops=flops, limit=24)[0]
    return call(
        body,
        [sds((H, W), F32), sds((H, W), F32), sds((B, W))],
        at,
        apart=args,
        vmem=[*right, before],
        scratch=[pltpu.VMEM((W, 2 * C), F32), *scratch],
        flops=flops,
        limit=24,
    )


def left_piece(at, direction, left, d):
    cols = pl.ds(pl.multiple_of(chip_at(at, *d) * W, 128), W)
    return jnp.dot(direction, left[:, cols], preferred_element_type=F32).astype(BF)


EARLY = [(2, 1), (1, 1), (-1, 1), (1, 0), (-1, 0)]
LATE = [(2, 0), (0, 1), (0, 0)]


def moments(at, keep, near, far, avg, sq):
    def body(at, keep, near, far, avg, sq, new_avg, new_sq, direction):
        packed = keep[...] + near[0:H, :].astype(F32) + far[...].astype(F32)
        for half in range(2):
            here = slice(H * half, H * half + H)
            rotated = packed[:, B * half : B * half + B]
            a = 0.9 * avg[here, :] + 0.1 * rotated
            s = 0.95 * sq[here, :] + 0.05 * rotated * rotated
            new_avg[here, :] = a
            new_sq[here, :] = s
            direction[here, :] = (a / first_fix / (jnp.sqrt(s / second_fix) + 1e-08)).astype(BF)

    out = [sds((B, B), F32), sds((B, B), F32), sds((B, B))]
    return call(body, out, at, vmem=(keep, near, far, avg, sq), limit=16)


def left_early(at, own, other, left):
    def body(at, own, other, left, turned_out, *rest):
        outs, (stack, turned) = rest[: len(EARLY)], rest[len(EARLY) :]
        k = at[2]
        stack[rows(B * k, B), 0:B] = own[...]
        stack[rows(B * (1 - k), B), 0:B] = other[...]
        turned[...] = jnp.transpose(stack[...])
        direction = turned[rows(H * k, H), :]
        turned_out[...] = direction
        for d, out in zip(EARLY, outs):
            out[...] = left_piece(at, direction, left, d)

    direction, *parts = call(
        body,
        [sds((H, W))] * (1 + len(EARLY)),
        at,
        vmem=(own, other, left),
        scratch=[pltpu.VMEM((W, C), BF), pltpu.VMEM((C, W), BF)],
        flops=2 * H * W * 5 * W,
        limit=24,
    )
    return direction, dict(zip(EARLY, parts))


def left_back(at, direction, left):
    def body(at, direction, left, *outs):
        for d, out in zip(LATE, outs):
            out[...] = left_piece(at, direction[...], left, d)

    return dict(zip(LATE, call(body, [sds((H, W))] * 3, at, vmem=(direction, left), flops=2 * H * W * 3 * W, limit=24)))


def right_back(at, blocks, right, which):
    def body(at, *rest):
        own, near, far, far_near, right, right_far = rest[:6]
        outs, stack, chosen = rest[6:-2], rest[-2], rest[-1]
        k = at[2]
        stack[B:C, :] = jnp.zeros((C - B, W), BF)
        stack[C + B :, :] = jnp.zeros((C - B, W), BF)
        stack[rows(H * k, H), :] = own[...]
        stack[rows(H * (1 - k), H), :] = near[...]
        stack[rows(C + H * k, H), :] = far[...]
        stack[rows(C + H * (1 - k), H), :] = far_near[...]
        for i, d in enumerate(which):
            chosen[H * i : H * i + H, :C] = right[rows(ring_at(at, d) * H, H), :]
            chosen[H * i : H * i + H, C:] = right_far[rows(ring_at(at, d) * H, H), :]
        total = jnp.dot(chosen[...], stack[...], preferred_element_type=F32).astype(BF)
        for i in range(len(which)):
            outs[i][...] = total[H * i : H * i + H]

    n = len(which)
    outs = call(
        body,
        [sds((H, W))] * n,
        at,
        vmem=(*blocks, *right),
        scratch=[pltpu.VMEM((2 * C, W), BF), pltpu.VMEM((n * H, 2 * C), BF)],
        flops=2 * n * H * W * W,
        limit=24,
    )
    return dict(zip(which, outs))


def per_device(gradient, left_basis, right_basis, exp_avg, exp_avg_sq):
    row, col = lax.axis_index("row"), lax.axis_index("col")
    k, xh = row % 2, col // 8
    at = jnp.stack([row // 4, row // 2 % 2, k, xh, col % 8]).astype(jnp.int32)

    gradient_far = move(gradient, k=1)
    half = 4 * B
    own_left = after(left_basis.T, gradient_far)
    far_left = move(own_left, k=1)
    x, top, bottom = to_half(at, gradient, gradient_far, [(0, H), (0, STEP), (STEP, STEP)], far_sds)
    side = move(x, xl=1)
    behind, ahead = move(x, y=1), move(x, y=-1)
    bottom = after(bottom, far_left)
    far = [move(top, y=2), move(bottom, y=-2)]
    whole = after(right_basis.T, x)
    start = (1 - xh) * 2 * half + k * half
    sent = [
        lax.dynamic_slice(whole, (0, start), (B, FIRST)),
        lax.dynamic_slice(whole, (0, start + FIRST), (B, half - FIRST)),
    ]
    kept = lax.dynamic_slice(whole, (0, xh * 2 * half), (B, 2 * half))
    own_right = right_half(at, [kept])
    left = both_left(at, in_hbm(after(own_left, *sent, own_right)), in_hbm(far_left))
    got = [move(after(sent[0], left, own_right, side, behind, ahead, *far), xh=1, xl=1)]
    side_in = after(side, left)
    side_behind, side_ahead = move(side_in, y=1), move(side_in, y=-1)
    side_far = [move(f, xl=1) for f in far]

    part = times_left(at, YX[:4], [[x], [behind], [ahead], [side]], left)
    got.append(move(after(sent[1], got[0], part), xh=1, xl=1))
    x = times_left(at, YX[4:], [[side_behind], [side_ahead], far, side_far], left, after(part, got[0]))
    pieces = gather_z(x)
    got = [got[0], after(got[1], *pieces[3], *pieces[4])]
    right = (own_right, right_half(at, got, [move(g, k=1) for g in got]))
    part = times_right(at, ZS[:5], pieces[:5], right)
    keep, far, give = times_right(at, ZS[5:], pieces[5:], right, part)
    near = move(give, k=1)
    far = move(add(far, near[H:]), xh=1)
    new_avg, new_sq, direction = moments(at, keep, near, far, exp_avg, exp_avg_sq)
    direction, part = left_early(at, direction, move(direction, k=1), left)
    part |= left_back(at, direction, left)

    own = scatter_yx(part)
    far = move(own, xh=1)
    blocks = (own, move(own, k=1), far, move(far, k=1))
    end = scatter_z(right_back(at, blocks, right, ZS))
    update = from_half(at, [end], [move(end, k=1)])
    return (new_avg, new_sq, update)


def solution(mesh):
    placed = (P("row", "col"), P(None, "row"), P(None, "col"), P("row", "col"), P("row", "col"))
    return jax.shard_map(
        per_device,
        mesh=mesh,
        in_specs=placed,
        out_specs=(P("row", "col"), P("row", "col"), P("row", "col")),
        check_vma=False,
    )
```

```python
import jax
import jax.numpy as jnp
import numpy as np
from jax import lax
from jax.experimental import pallas as pl
from jax.experimental.pallas import tpu as pltpu
from jax.sharding import PartitionSpec as P

first_fix = 0.9999734386
second_fix = 0.9940794709

AXES = ("row", "col")
SIZES = {"y": 4, "xl": 2, "k": 2, "xh": 2, "z": 8}
BF, F32 = jnp.bfloat16, jnp.float32
B, H, W = 320, 160, 640
YX = [(0, 0), (-1, 0), (1, 0), (0, 1), (-1, 1), (1, 1), (2, 0), (2, 1)]
ZS = [0, -1, 1, -2, 2, -3, 3, 4]
FIRST = 512
STEP = 80
C = 384


def place(i):
    r, c = divmod(i, 16)
    return {"y": r // 4, "xl": r // 2 % 2, "k": r % 2, "xh": c // 8, "z": c % 8}


def move(x, **steps):
    pairs = []
    for i in range(256):
        d = place(i)
        for name, step in steps.items():
            d[name] = (d[name] + step) % SIZES[name]
        pairs.append((i, (d["y"] * 4 + d["xl"] * 2 + d["k"]) * 16 + d["xh"] * 8 + d["z"]))
    return lax.ppermute(x, AXES, pairs)


ANY = pl.BlockSpec(memory_space=pl.ANY)
VMEM = pl.BlockSpec(memory_space=pltpu.VMEM)
SMEM = pl.BlockSpec(memory_space=pltpu.SMEM)


def call(body, out, at, apart=(), vmem=(), scratch=(), limit=40, flops=0, out_spec=None):
    args = [at, *apart, *vmem]
    size = sum(a.size * a.dtype.itemsize for a in args) + sum(
        int(np.prod(o.shape)) * jnp.dtype(o.dtype).itemsize for o in out
    )
    return pl.pallas_call(
        body,
        out_shape=list(out),
        in_specs=[SMEM] + [ANY] * len(apart) + [VMEM] * len(vmem),
        out_specs=[out_spec or VMEM] * len(out),
        scratch_shapes=list(scratch),
        compiler_params=pltpu.CompilerParams(vmem_limit_bytes=limit << 20),
        cost_estimate=pl.CostEstimate(flops=flops, bytes_accessed=size, transcendentals=0),
    )(*args)


def sds(shape, dtype=BF):
    return jax.ShapeDtypeStruct(shape, dtype)


def far_sds(shape, dtype=BF):
    return pltpu.HBM(shape, dtype)


def in_hbm(x):
    return pltpu.with_memory_space_constraint(x, pltpu.HBM)


def in_vmem(x):
    return pltpu.with_memory_space_constraint(x, pltpu.VMEM)


def after(x, *others):
    return lax.optimization_barrier((x, *others))[0]


def chip_at(at, dy, p):
    return lax.rem(at[0] + dy + 4, 4) * 2 + lax.rem(at[1] + p, 2)


def ring_at(at, d):
    return lax.rem(at[4] + d + 8, 8)


def copies(pairs, sems):
    started = []
    for n, (a, b) in enumerate(pairs):
        c = pltpu.make_async_copy(a, b, sems.at[n])
        c.start()
        started.append(c)
    for c in started:
        c.wait()


def rows(i, n):
    return pl.ds(pl.multiple_of(i, 16), n)


def to_half(at, own, other, parts, shape=sds):
    dt = own.dtype

    def body(at, own, other, *rest):
        outs, (stack, turned, mine, sems) = rest[: len(parts)], rest[len(parts) :]
        k = at[2]
        copy = pltpu.make_async_copy(own, mine, sems.at[0])
        copy.start()
        stack[rows(B * (1 - k), B), 0:B] = other[...]
        copy.wait()
        stack[rows(B * k, B), 0:B] = mine[...]
        turned[...] = jnp.transpose(stack[...])
        for out, (lo, n) in zip(outs, parts):
            out[...] = turned[rows(H * k + lo, n), :]

    return call(
        body,
        [shape((n, W), dt) for _, n in parts],
        at,
        apart=[in_hbm(own)],
        vmem=[other],
        scratch=[pltpu.VMEM((W, C), dt), pltpu.VMEM((C, W), dt), pltpu.VMEM((B, B), dt), pltpu.SemaphoreType.DMA((1,))],
        limit=16,
        out_spec=pl.BlockSpec() if shape is far_sds else None,
    )


def from_half(at, own, other):
    n = len(own)
    dt = own[0].dtype

    def body(at, *rest):
        mine, theirs, (out, stack, turned) = rest[:n], rest[n : 2 * n], rest[2 * n :]
        k = at[2]
        lo = 0
        for a, b in zip(mine, theirs):
            h = a.shape[0]
            stack[rows(H * k + lo, h), :] = a[...]
            stack[rows(H * (1 - k) + lo, h), :] = b[...]
            lo += h
        turned[...] = jnp.transpose(stack[...])
        out[...] = turned[rows(B * k, B), 0:B]

    return call(
        body,
        [sds((B, B), dt)],
        at,
        vmem=(*own, *other),
        scratch=[pltpu.VMEM((384, W), dt), pltpu.VMEM((W, 384), dt)],
        limit=16,
    )[0]


def both_left(at, own, other):
    def body(at, own, other, out, sems):
        k = at[2]
        pairs = []
        for i in range(5):
            part = slice(64 * i, 64 * i + 64)
            pairs.append((own.at[part, :], out.at[rows(B * k + 64 * i, 64), :]))
            pairs.append((other.at[part, :], out.at[rows(B * (1 - k) + 64 * i, 64), :]))
        copies(pairs, sems)

    return in_vmem(
        call(
            body,
            [sds((W, 16 * B))],
            at,
            apart=(own, other),
            scratch=[pltpu.SemaphoreType.DMA((10,))],
            limit=4,
            out_spec=ANY,
        )[0]
    )


def right_half(at, mine, theirs=()):
    n = len(mine)

    def body(at, *rest):
        parts, (out, stack, turned) = rest[:-3], rest[-3:]
        k = at[2]
        stack[B:, :] = jnp.zeros((C - B, 8 * B), BF)
        if n == 1:
            stack[0:B, :] = parts[0][...]
        else:
            for i, start in ((0, k), (n, 1 - k)):
                lo = 0
                for part in parts[i : i + n]:
                    wide = part.shape[1]
                    stack[0:B, pl.ds(pl.multiple_of(4 * B * start + lo, 128), wide)] = part[...]
                    lo += wide
        for t in range(20):
            turned[128 * t : 128 * t + 128, :] = jnp.transpose(stack[:, 128 * t : 128 * t + 128])
        for z in range(8):
            out[H * z : H * z + H, :] = turned[rows(B * z + H * k, H), :]

    return call(
        body,
        [sds((4 * B, C))],
        at,
        vmem=(*mine, *theirs),
        scratch=[pltpu.VMEM((C, 8 * B), BF), pltpu.VMEM((8 * B, C), BF)],
        limit=24,
    )[0]


def add(*xs):
    total = xs[0].astype(F32)
    for x in xs[1:]:
        total = total + x.astype(F32)
    return total.astype(BF)


def scatter_yx(part):
    far = add(part[2, 0], move(part[2, 1], xl=1))
    side = add(part[0, 1], move(part[1, 1], y=1), move(part[-1, 1], y=-1))
    near = [move(part[1, 0], y=1), move(part[-1, 0], y=-1)]
    far = jnp.concatenate([move(far[:STEP], y=2), move(far[STEP:], y=-2)], 0)
    return add(part[0, 0], *near, far, move(side, xl=1))


def gather_z(x, early):
    plus = minus = x
    got = [[x]]
    for step in range(3):
        plus, minus = move(plus, z=1), move(minus, z=-1)
        got += [[plus], [minus]]
        plus, minus, *_ = lax.optimization_barrier((plus, minus, *([early] if step == 0 else [])))
    return got, plus, minus


def gather_last(plus, minus):
    return [move(plus[:STEP], z=1), move(minus[STEP:], z=-1)]


def scatter_z(part):
    plus, minus = move(part[4][:STEP], z=1), move(part[4][STEP:], z=-1)
    plus = jnp.concatenate([add(part[3][:STEP], plus), part[3][STEP:]], 0)
    minus = jnp.concatenate([part[-3][:STEP], add(part[-3][STEP:], minus)], 0)
    for s in (2, 1, 0):
        plus, minus, part[0] = lax.optimization_barrier((plus, minus, part[0]))
        plus, minus = move(plus, z=1), move(minus, z=-1)
        if s:
            plus, minus = add(part[s], plus), add(part[-s], minus)
    return add(part[0], plus, minus)


def times_left(at, which, pieces, left, before=None):
    flat = [(i, n, x) for i, xs in enumerate(pieces) for n, x in enumerate(xs)]
    n = len(flat)
    wide = len(which) * W

    def body(at, *rest):
        blocks, left, out, stack, sems = rest[:n], rest[n], *rest[-3:]
        waits = [[] for _ in which]
        for m, ((i, h, _), r) in enumerate(zip(flat, blocks)):
            to = stack.at[STEP * h : STEP * h + r.shape[0], W * i : W * i + W]
            copy = pltpu.make_async_copy(r, to, sems.at[m])
            copy.start()
            waits[i].append(copy)
        total = rest[n + 1][...] if before is not None else jnp.zeros((H, W), F32)
        for i, (dy, p) in enumerate(which):
            for copy in waits[i]:
                copy.wait()
            cols = pl.ds(pl.multiple_of(chip_at(at, dy, p) * W, 128), W)
            total += lax.dot_general(
                stack[:, W * i : W * i + W], left[:, cols], (((1,), (1,)), ((), ())), preferred_element_type=F32
            )
        out[...] = total.astype(out.dtype)

    last = before is not None
    return call(
        body,
        [sds((H, W), BF if last else F32)],
        at,
        apart=[x for _, _, x in flat],
        vmem=[left, before] if last else [left],
        scratch=[pltpu.VMEM((H, wide), BF), pltpu.SemaphoreType.DMA((n,))],
        flops=2 * H * W * wide,
        limit=24,
    )[0]


def times_right(at, which, pieces, right, before=()):
    sides = len(right)
    flat = [(i, h, x) for i, xs in enumerate(pieces) for h, x in enumerate(xs)]
    n = len(flat)
    deep = len(which) * H

    def body(at, *rest):
        blocks, right, stack, factor, sems = rest[:n], rest[n : n + sides], *rest[-3:]
        started = []
        for m, ((i, h, _), r) in enumerate(zip(flat, blocks)):
            to = stack.at[H * i + STEP * h : H * i + STEP * h + r.shape[0], :]
            started.append(pltpu.make_async_copy(r, to, sems.at[m]))
            started[-1].start()
        for i, d in enumerate(which):
            for side in range(sides):
                factor[H * i : H * i + H, C * side : C * side + C] = right[side][rows(ring_at(at, d) * H, H), :]
        for copy in started:
            copy.wait()
        part = lax.dot_general(stack[...], factor[...], (((0,), (0,)), ((), ())), preferred_element_type=F32)
        if not before:
            rest[n + sides][...] = part
            return
        keep, far, give, total = rest[n + 2 * sides : n + 2 * sides + 4]
        for side in range(sides):
            cols = slice(C * side, C * side + C)
            total[:, cols] = rest[n + sides + side][...] + part[:, cols]
        for half in range(2):
            lo, to = H * half, slice(B * half, B * half + B)
            mine, theirs = rows(B * at[2] + lo, H), rows(B * (1 - at[2]) + lo, H)
            keep[:, to] = total[mine, 0:B]
            far[:, to] = total[mine, C : C + B]
            give[0:H, to] = total[theirs, 0:B].astype(BF)
            give[H:, to] = total[theirs, C : C + B].astype(BF)

    scratch = [pltpu.VMEM((deep, W), BF), pltpu.VMEM((deep, sides * C), BF), pltpu.SemaphoreType.DMA((n,))]
    flops = 2 * W * sides * C * deep
    args = [x for _, _, x in flat]
    if not before:
        return call(body, [sds((W, sides * C), F32)], at, apart=args, vmem=right, scratch=scratch, flops=flops, limit=24)[0]
    return call(
        body,
        [sds((H, W), F32), sds((H, W), F32), sds((B, W))],
        at,
        apart=args,
        vmem=[*right, *before],
        scratch=[pltpu.VMEM((W, 2 * C), F32), *scratch],
        flops=flops,
        limit=24,
    )


def left_piece(at, direction, left, d):
    cols = pl.ds(pl.multiple_of(chip_at(at, *d) * W, 128), W)
    return jnp.dot(direction, left[:, cols], preferred_element_type=F32).astype(BF)


EARLY = [(2, 1), (1, 1), (-1, 1), (1, 0), (-1, 0)]
LATE = [(2, 0), (0, 1), (0, 0)]


def moments(at, keep, near, far, avg, sq):
    def body(at, keep, near, far, avg, sq, new_avg, new_sq, direction):
        packed = keep[...] + near[0:H, :].astype(F32) + far[...].astype(F32)
        for half in range(2):
            here = slice(H * half, H * half + H)
            rotated = packed[:, B * half : B * half + B]
            a = 0.9 * avg[here, :] + 0.1 * rotated
            s = 0.95 * sq[here, :] + 0.05 * rotated * rotated
            new_avg[here, :] = a
            new_sq[here, :] = s
            direction[here, :] = (a / first_fix / (jnp.sqrt(s / second_fix) + 1e-08)).astype(BF)

    out = [sds((B, B), F32), sds((B, B), F32), sds((B, B))]
    return call(body, out, at, vmem=(keep, near, far, avg, sq), limit=16)


def left_early(at, own, other, left):
    def body(at, own, other, left, turned_out, *rest):
        outs, (stack, turned) = rest[: len(EARLY)], rest[len(EARLY) :]
        k = at[2]
        stack[rows(B * k, B), 0:B] = own[...]
        stack[rows(B * (1 - k), B), 0:B] = other[...]
        turned[...] = jnp.transpose(stack[...])
        direction = turned[rows(H * k, H), :]
        turned_out[...] = direction
        for d, out in zip(EARLY, outs):
            out[...] = left_piece(at, direction, left, d)

    direction, *parts = call(
        body,
        [sds((H, W))] * (1 + len(EARLY)),
        at,
        vmem=(own, other, left),
        scratch=[pltpu.VMEM((W, C), BF), pltpu.VMEM((C, W), BF)],
        flops=2 * H * W * 5 * W,
        limit=24,
    )
    return direction, dict(zip(EARLY, parts))


def left_back(at, direction, left):
    def body(at, direction, left, *outs):
        for d, out in zip(LATE, outs):
            out[...] = left_piece(at, direction[...], left, d)

    return dict(zip(LATE, call(body, [sds((H, W))] * 3, at, vmem=(direction, left), flops=2 * H * W * 3 * W, limit=24)))


def right_back(at, blocks, right, which):
    def body(at, *rest):
        own, near, far, far_near, right, right_far = rest[:6]
        outs, stack, chosen = rest[6:-2], rest[-2], rest[-1]
        k = at[2]
        stack[B:C, :] = jnp.zeros((C - B, W), BF)
        stack[C + B :, :] = jnp.zeros((C - B, W), BF)
        stack[rows(H * k, H), :] = own[...]
        stack[rows(H * (1 - k), H), :] = near[...]
        stack[rows(C + H * k, H), :] = far[...]
        stack[rows(C + H * (1 - k), H), :] = far_near[...]
        for i, d in enumerate(which):
            chosen[H * i : H * i + H, :C] = right[rows(ring_at(at, d) * H, H), :]
            chosen[H * i : H * i + H, C:] = right_far[rows(ring_at(at, d) * H, H), :]
        total = jnp.dot(chosen[...], stack[...], preferred_element_type=F32).astype(BF)
        for i in range(len(which)):
            outs[i][...] = total[H * i : H * i + H]

    n = len(which)
    outs = call(
        body,
        [sds((H, W))] * n,
        at,
        vmem=(*blocks, *right),
        scratch=[pltpu.VMEM((2 * C, W), BF), pltpu.VMEM((n * H, 2 * C), BF)],
        flops=2 * n * H * W * W,
        limit=24,
    )
    return dict(zip(which, outs))


def per_device(gradient, left_basis, right_basis, exp_avg, exp_avg_sq):
    row, col = lax.axis_index("row"), lax.axis_index("col")
    k, xh = row % 2, col // 8
    at = jnp.stack([row // 4, row // 2 % 2, k, xh, col % 8]).astype(jnp.int32)

    gradient_far = move(gradient, k=1)
    half = 4 * B
    own_left = after(left_basis.T, gradient_far)
    far_left = move(own_left, k=1)
    x, top, bottom = to_half(at, gradient, gradient_far, [(0, H), (0, STEP), (STEP, STEP)], far_sds)
    side = move(x, xl=1)
    behind, ahead = move(x, y=1), move(x, y=-1)
    bottom = after(bottom, far_left)
    far = [move(top, y=2), move(bottom, y=-2)]
    whole = after(right_basis.T, x)
    start = (1 - xh) * 2 * half + k * half
    sent = [
        lax.dynamic_slice(whole, (0, start), (B, FIRST)),
        lax.dynamic_slice(whole, (0, start + FIRST), (B, half - FIRST)),
    ]
    kept = lax.dynamic_slice(whole, (0, xh * 2 * half), (B, 2 * half))
    left = both_left(at, in_hbm(after(own_left, *sent, kept)), in_hbm(far_left))
    got = [move(after(sent[0], left, side, behind, ahead, *far), xh=1, xl=1)]
    side_in = after(side, left)
    side_behind, side_ahead = move(side_in, y=1), move(side_in, y=-1)
    side_far = [move(f, xl=1) for f in far]

    part = times_left(at, YX[:4], [[x], [behind], [ahead], [side]], left)
    x = times_left(at, YX[4:], [[side_behind], [side_ahead], far, side_far], left, after(part, got[0]))
    own_right = right_half(at, [after(kept, x)])
    got.append(move(after(sent[1], got[0], own_right), xh=1, xl=1))
    pieces, plus, minus = gather_z(x, own_right)
    own_part = times_right(at, ZS[:5], pieces[:5], [own_right])
    got = [after(g, own_part, *pieces[5], *pieces[6]) for g in got]
    far_right = right_half(at, got, [move(g, k=1) for g in got])
    pieces.append(gather_last(after(plus, own_part), after(minus, own_part)))
    far_part = times_right(at, ZS[:5], pieces[:5], [far_right])
    right = (own_right, far_right)
    keep, far, give = times_right(at, ZS[5:], pieces[5:], right, (own_part, far_part))
    near = move(give, k=1)
    far = move(add(far, near[H:]), xh=1)
    new_avg, new_sq, direction = moments(at, keep, near, far, exp_avg, exp_avg_sq)
    direction, part = left_early(at, direction, move(direction, k=1), left)
    part |= left_back(at, direction, left)

    own = scatter_yx(part)
    far = move(own, xh=1)
    blocks = (own, move(own, k=1), far, move(far, k=1))
    end = scatter_z(right_back(at, blocks, right, [4, 3, -3]) | right_back(at, blocks, right, [0, 2, -2, 1, -1]))
    update = from_half(at, [end], [move(end, k=1)])
    return (new_avg, new_sq, update)


def solution(mesh):
    placed = (P("row", "col"), P(None, "row"), P(None, "col"), P("row", "col"), P("row", "col"))
    return jax.shard_map(
        per_device,
        mesh=mesh,
        in_specs=placed,
        out_specs=(P("row", "col"), P("row", "col"), P("row", "col")),
        check_vma=False,
    )
```

```python
import jax
import jax.numpy as jnp
import numpy as np
from jax import lax
from jax.experimental import pallas as pl
from jax.experimental.pallas import tpu as pltpu
from jax.sharding import PartitionSpec as P

first_fix = 0.9999734386
second_fix = 0.9940794709

AXES = ("row", "col")
SIZES = {"y": 4, "xl": 2, "k": 2, "xh": 2, "z": 8}
BF, F32 = jnp.bfloat16, jnp.float32
B, H, W = 320, 160, 640
YX = [(0, 0), (-1, 0), (1, 0), (0, 1), (-1, 1), (1, 1), (2, 0), (2, 1)]
ZS = [0, -1, 1, -2, 2, -3, 3, 4]
STEP = 80
C = 384


def place(i):
    r, c = divmod(i, 16)
    return {"y": r // 4, "xl": r // 2 % 2, "k": r % 2, "xh": c // 8, "z": c % 8}


def move(x, **steps):
    pairs = []
    for i in range(256):
        d = place(i)
        for name, step in steps.items():
            d[name] = (d[name] + step) % SIZES[name]
        pairs.append((i, (d["y"] * 4 + d["xl"] * 2 + d["k"]) * 16 + d["xh"] * 8 + d["z"]))
    return lax.ppermute(x, AXES, pairs)


ANY = pl.BlockSpec(memory_space=pl.ANY)
VMEM = pl.BlockSpec(memory_space=pltpu.VMEM)
SMEM = pl.BlockSpec(memory_space=pltpu.SMEM)


def call(body, out, at, apart=(), vmem=(), scratch=(), limit=40, flops=0, out_spec=None):
    args = [at, *apart, *vmem]
    size = sum(a.size * a.dtype.itemsize for a in args) + sum(
        int(np.prod(o.shape)) * jnp.dtype(o.dtype).itemsize for o in out
    )
    return pl.pallas_call(
        body,
        out_shape=list(out),
        in_specs=[SMEM] + [ANY] * len(apart) + [VMEM] * len(vmem),
        out_specs=[out_spec or VMEM] * len(out),
        scratch_shapes=list(scratch),
        compiler_params=pltpu.CompilerParams(vmem_limit_bytes=limit << 20),
        cost_estimate=pl.CostEstimate(flops=flops, bytes_accessed=size, transcendentals=0),
    )(*args)


def sds(shape, dtype=BF):
    return jax.ShapeDtypeStruct(shape, dtype)


def far_sds(shape, dtype=BF):
    return pltpu.HBM(shape, dtype)


def in_hbm(x):
    return pltpu.with_memory_space_constraint(x, pltpu.HBM)


def in_vmem(x):
    return pltpu.with_memory_space_constraint(x, pltpu.VMEM)


def after(x, *others):
    return lax.optimization_barrier((x, *others))[0]


def chip_at(at, dy, p):
    return lax.rem(at[0] + dy + 4, 4) * 2 + lax.rem(at[1] + p, 2)


def ring_at(at, d):
    return lax.rem(at[4] + d + 8, 8)


def copies(pairs, sems):
    started = []
    for n, (a, b) in enumerate(pairs):
        c = pltpu.make_async_copy(a, b, sems.at[n])
        c.start()
        started.append(c)
    for c in started:
        c.wait()


def rows(i, n):
    return pl.ds(pl.multiple_of(i, 16), n)


def to_half(at, own, other, parts, shape=sds):
    dt = own.dtype

    def body(at, own, other, *rest):
        outs, (stack, turned, mine, sems) = rest[: len(parts)], rest[len(parts) :]
        k = at[2]
        copy = pltpu.make_async_copy(own, mine, sems.at[0])
        copy.start()
        stack[rows(B * (1 - k), B), 0:B] = other[...]
        copy.wait()
        stack[rows(B * k, B), 0:B] = mine[...]
        turned[...] = jnp.transpose(stack[...])
        for out, (lo, n) in zip(outs, parts):
            out[...] = turned[rows(H * k + lo, n), :]

    return call(
        body,
        [shape((n, W), dt) for _, n in parts],
        at,
        apart=[in_hbm(own)],
        vmem=[other],
        scratch=[pltpu.VMEM((W, C), dt), pltpu.VMEM((C, W), dt), pltpu.VMEM((B, B), dt), pltpu.SemaphoreType.DMA((1,))],
        limit=16,
        out_spec=pl.BlockSpec() if shape is far_sds else None,
    )


def from_half(at, own, other):
    n = len(own)
    dt = own[0].dtype

    def body(at, *rest):
        mine, theirs, (out, stack, turned) = rest[:n], rest[n : 2 * n], rest[2 * n :]
        k = at[2]
        lo = 0
        for a, b in zip(mine, theirs):
            h = a.shape[0]
            stack[rows(H * k + lo, h), :] = a[...]
            stack[rows(H * (1 - k) + lo, h), :] = b[...]
            lo += h
        turned[...] = jnp.transpose(stack[...])
        out[...] = turned[rows(B * k, B), 0:B]

    return call(
        body,
        [sds((B, B), dt)],
        at,
        vmem=(*own, *other),
        scratch=[pltpu.VMEM((384, W), dt), pltpu.VMEM((W, 384), dt)],
        limit=16,
    )[0]


def both_left(at, own, other):
    def body(at, own, other, out, sems):
        k = at[2]
        pairs = []
        for i in range(5):
            part = slice(64 * i, 64 * i + 64)
            pairs.append((own.at[part, :], out.at[rows(B * k + 64 * i, 64), :]))
            pairs.append((other.at[part, :], out.at[rows(B * (1 - k) + 64 * i, 64), :]))
        copies(pairs, sems)

    return in_vmem(
        call(
            body,
            [sds((W, 16 * B))],
            at,
            apart=(own, other),
            scratch=[pltpu.SemaphoreType.DMA((10,))],
            limit=4,
            out_spec=ANY,
        )[0]
    )


def right_half(at, columns):
    def body(at, columns, out, stack, turned):
        k = at[2]
        stack[B:, :] = jnp.zeros((C - B, 8 * B), BF)
        stack[0:B, :] = columns[...]
        for t in range(20):
            turned[128 * t : 128 * t + 128, :] = jnp.transpose(stack[:, 128 * t : 128 * t + 128])
        for z in range(8):
            out[H * z : H * z + H, :] = turned[rows(B * z + H * k, H), :]

    return call(
        body,
        [sds((4 * B, C))],
        at,
        vmem=[columns],
        scratch=[pltpu.VMEM((C, 8 * B), BF), pltpu.VMEM((8 * B, C), BF)],
        limit=24,
    )[0]


def add(*xs):
    total = xs[0].astype(F32)
    for x in xs[1:]:
        total = total + x.astype(F32)
    return total.astype(BF)


def scatter_yx(part):
    far = add(part[2, 0], move(part[2, 1], xl=1))
    side = add(part[0, 1], move(part[1, 1], y=1), move(part[-1, 1], y=-1))
    near = [move(part[1, 0], y=1), move(part[-1, 0], y=-1)]
    far = jnp.concatenate([move(far[:STEP], y=2), move(far[STEP:], y=-2)], 0)
    return add(part[0, 0], *near, far, move(side, xl=1))


def gather_z(x, early):
    plus = minus = x
    got = [[x]]
    for step in range(3):
        plus, minus = move(plus, z=1), move(minus, z=-1)
        got += [[plus], [minus]]
        plus, minus, *_ = lax.optimization_barrier((plus, minus, *([early] if step == 0 else [])))
    return got, plus, minus


def gather_last(plus, minus):
    return [move(plus[:STEP], z=1), move(minus[STEP:], z=-1)]


def scatter_z(part):
    plus, minus = move(part[4][:STEP], z=1), move(part[4][STEP:], z=-1)
    plus = jnp.concatenate([add(part[3][:STEP], plus), part[3][STEP:]], 0)
    minus = jnp.concatenate([part[-3][:STEP], add(part[-3][STEP:], minus)], 0)
    for s in (2, 1, 0):
        plus, minus, part[0] = lax.optimization_barrier((plus, minus, part[0]))
        plus, minus = move(plus, z=1), move(minus, z=-1)
        if s:
            plus, minus = add(part[s], plus), add(part[-s], minus)
    return add(part[0], plus, minus)


def times_left(at, which, pieces, left, before=None):
    flat = [(i, n, x) for i, xs in enumerate(pieces) for n, x in enumerate(xs)]
    n = len(flat)
    wide = len(which) * W

    def body(at, *rest):
        blocks, left, out, stack, sems = rest[:n], rest[n], *rest[-3:]
        waits = [[] for _ in which]
        for m, ((i, h, _), r) in enumerate(zip(flat, blocks)):
            to = stack.at[STEP * h : STEP * h + r.shape[0], W * i : W * i + W]
            copy = pltpu.make_async_copy(r, to, sems.at[m])
            copy.start()
            waits[i].append(copy)
        total = rest[n + 1][...] if before is not None else jnp.zeros((H, W), F32)
        for i, (dy, p) in enumerate(which):
            for copy in waits[i]:
                copy.wait()
            cols = pl.ds(pl.multiple_of(chip_at(at, dy, p) * W, 128), W)
            total += lax.dot_general(
                stack[:, W * i : W * i + W], left[:, cols], (((1,), (1,)), ((), ())), preferred_element_type=F32
            )
        out[...] = total.astype(out.dtype)

    last = before is not None
    return call(
        body,
        [sds((H, W), BF if last else F32)],
        at,
        apart=[x for _, _, x in flat],
        vmem=[left, before] if last else [left],
        scratch=[pltpu.VMEM((H, wide), BF), pltpu.SemaphoreType.DMA((n,))],
        flops=2 * H * W * wide,
        limit=24,
    )[0]


def times_right(at, which, pieces, right, before=()):
    sides = len(right)
    flat = [(i, h, x) for i, xs in enumerate(pieces) for h, x in enumerate(xs)]
    n = len(flat)
    deep = len(which) * H

    def body(at, *rest):
        blocks, right, stack, factor, sems = rest[:n], rest[n : n + sides], *rest[-3:]
        started = []
        for m, ((i, h, _), r) in enumerate(zip(flat, blocks)):
            to = stack.at[H * i + STEP * h : H * i + STEP * h + r.shape[0], :]
            started.append(pltpu.make_async_copy(r, to, sems.at[m]))
            started[-1].start()
        for i, d in enumerate(which):
            for side in range(sides):
                factor[H * i : H * i + H, C * side : C * side + C] = right[side][rows(ring_at(at, d) * H, H), :]
        for copy in started:
            copy.wait()
        part = lax.dot_general(stack[...], factor[...], (((0,), (0,)), ((), ())), preferred_element_type=F32)
        if not before:
            rest[n + sides][...] = part
            return
        keep, far, give, total = rest[n + 2 * sides : n + 2 * sides + 4]
        for side in range(sides):
            cols = slice(C * side, C * side + C)
            total[:, cols] = rest[n + sides + side][...] + part[:, cols]
        for half in range(2):
            lo, to = H * half, slice(B * half, B * half + B)
            mine, theirs = rows(B * at[2] + lo, H), rows(B * (1 - at[2]) + lo, H)
            keep[:, to] = total[mine, 0:B]
            far[:, to] = total[mine, C : C + B]
            give[0:H, to] = total[theirs, 0:B].astype(BF)
            give[H:, to] = total[theirs, C : C + B].astype(BF)

    scratch = [pltpu.VMEM((deep, W), BF), pltpu.VMEM((deep, sides * C), BF), pltpu.SemaphoreType.DMA((n,))]
    flops = 2 * W * sides * C * deep
    args = [x for _, _, x in flat]
    if not before:
        return call(body, [sds((W, sides * C), F32)], at, apart=args, vmem=right, scratch=scratch, flops=flops, limit=24)[0]
    return call(
        body,
        [sds((H, W), F32), sds((H, W), F32), sds((B, W))],
        at,
        apart=args,
        vmem=[*right, *before],
        scratch=[pltpu.VMEM((W, 2 * C), F32), *scratch],
        flops=flops,
        limit=24,
    )


def left_piece(at, direction, left, d):
    cols = pl.ds(pl.multiple_of(chip_at(at, *d) * W, 128), W)
    return jnp.dot(direction, left[:, cols], preferred_element_type=F32).astype(BF)


EARLY = [(2, 1), (1, 1), (-1, 1), (1, 0), (-1, 0)]
LATE = [(2, 0), (0, 1), (0, 0)]


def moments(at, keep, near, far, avg, sq):
    def body(at, keep, near, far, avg, sq, new_avg, new_sq, direction):
        packed = keep[...] + near[0:H, :].astype(F32) + far[...].astype(F32)
        for half in range(2):
            here = slice(H * half, H * half + H)
            rotated = packed[:, B * half : B * half + B]
            a = 0.9 * avg[here, :] + 0.1 * rotated
            s = 0.95 * sq[here, :] + 0.05 * rotated * rotated
            new_avg[here, :] = a
            new_sq[here, :] = s
            direction[here, :] = (a / first_fix / (jnp.sqrt(s / second_fix) + 1e-08)).astype(BF)

    out = [sds((B, B), F32), sds((B, B), F32), sds((B, B))]
    return call(body, out, at, vmem=(keep, near, far, avg, sq), limit=16)


def left_early(at, own, other, left):
    def body(at, own, other, left, turned_out, *rest):
        outs, (stack, turned) = rest[: len(EARLY)], rest[len(EARLY) :]
        k = at[2]
        stack[rows(B * k, B), 0:B] = own[...]
        stack[rows(B * (1 - k), B), 0:B] = other[...]
        turned[...] = jnp.transpose(stack[...])
        direction = turned[rows(H * k, H), :]
        turned_out[...] = direction
        for d, out in zip(EARLY, outs):
            out[...] = left_piece(at, direction, left, d)

    direction, *parts = call(
        body,
        [sds((H, W))] * (1 + len(EARLY)),
        at,
        vmem=(own, other, left),
        scratch=[pltpu.VMEM((W, C), BF), pltpu.VMEM((C, W), BF)],
        flops=2 * H * W * 5 * W,
        limit=24,
    )
    return direction, dict(zip(EARLY, parts))


def left_back(at, direction, left):
    def body(at, direction, left, *outs):
        for d, out in zip(LATE, outs):
            out[...] = left_piece(at, direction[...], left, d)

    return dict(zip(LATE, call(body, [sds((H, W))] * 3, at, vmem=(direction, left), flops=2 * H * W * 3 * W, limit=24)))


def right_back(at, blocks, right, which):
    def body(at, *rest):
        own, near, far, far_near, right, right_far = rest[:6]
        outs, stack, chosen = rest[6:-2], rest[-2], rest[-1]
        k = at[2]
        stack[B:C, :] = jnp.zeros((C - B, W), BF)
        stack[C + B :, :] = jnp.zeros((C - B, W), BF)
        stack[rows(H * k, H), :] = own[...]
        stack[rows(H * (1 - k), H), :] = near[...]
        stack[rows(C + H * k, H), :] = far[...]
        stack[rows(C + H * (1 - k), H), :] = far_near[...]
        for i, d in enumerate(which):
            chosen[H * i : H * i + H, :C] = right[rows(ring_at(at, d) * H, H), :]
            chosen[H * i : H * i + H, C:] = right_far[rows(ring_at(at, d) * H, H), :]
        total = jnp.dot(chosen[...], stack[...], preferred_element_type=F32).astype(BF)
        for i in range(len(which)):
            outs[i][...] = total[H * i : H * i + H]

    n = len(which)
    outs = call(
        body,
        [sds((H, W))] * n,
        at,
        vmem=(*blocks, *right),
        scratch=[pltpu.VMEM((2 * C, W), BF), pltpu.VMEM((n * H, 2 * C), BF)],
        flops=2 * n * H * W * W,
        limit=24,
    )
    return dict(zip(which, outs))


def per_device(gradient, left_basis, right_basis, exp_avg, exp_avg_sq):
    row, col = lax.axis_index("row"), lax.axis_index("col")
    k, xh = row % 2, col // 8
    at = jnp.stack([row // 4, row // 2 % 2, k, xh, col % 8]).astype(jnp.int32)

    gradient_far = move(gradient, k=1)
    half = 8 * B
    own_left = after(left_basis.T, gradient_far)
    far_left = move(own_left, k=1)
    x, top, bottom = to_half(at, gradient, gradient_far, [(0, H), (0, STEP), (STEP, STEP)], far_sds)
    side = move(x, xl=1)
    behind, ahead = move(x, y=1), move(x, y=-1)
    bottom = after(bottom, far_left)
    far = [move(top, y=2), move(bottom, y=-2)]
    whole = after(right_basis.T, x)
    sent = lax.dynamic_slice(whole, (0, (1 - xh) * half), (B, half))
    kept = lax.dynamic_slice(whole, (0, xh * half), (B, half))
    left = both_left(at, in_hbm(after(own_left, sent, kept)), in_hbm(far_left))
    got = move(after(sent, left, side, behind, ahead, *far), xh=1, xl=1)
    side_in = after(side, left)
    side_behind, side_ahead = move(side_in, y=1), move(side_in, y=-1)
    side_far = [move(f, xl=1) for f in far]

    part = times_left(at, YX[:4], [[x], [behind], [ahead], [side]], left)
    x = times_left(at, YX[4:], [[side_behind], [side_ahead], far, side_far], left, part)
    own_right = right_half(at, after(kept, x))
    pieces, plus, minus = gather_z(x, own_right)
    own_part = times_right(at, ZS[:5], pieces[:5], [own_right])
    far_right = right_half(at, after(got, own_part, *pieces[5], *pieces[6]))
    pieces.append(gather_last(after(plus, own_part), after(minus, own_part)))
    far_part = times_right(at, ZS[:5], pieces[:5], [far_right])
    right = (own_right, far_right)
    keep, far, give = times_right(at, ZS[5:], pieces[5:], right, (own_part, far_part))
    near = move(give, k=1)
    far = move(add(far, near[H:]), xh=1)
    new_avg, new_sq, direction = moments(at, keep, near, far, exp_avg, exp_avg_sq)
    direction, part = left_early(at, direction, move(direction, k=1), left)
    part |= left_back(at, direction, left)

    own = scatter_yx(part)
    far = move(own, xh=1)
    blocks = (own, move(own, k=1), far, move(far, k=1))
    end = scatter_z(right_back(at, blocks, right, [4, 3, -3]) | right_back(at, blocks, right, [0, 2, -2, 1, -1]))
    update = from_half(at, [end], [move(end, k=1)])
    return (new_avg, new_sq, update)


def solution(mesh):
    placed = (P("row", "col"), P(None, "row"), P(None, "col"), P("row", "col"), P("row", "col"))
    return jax.shard_map(
        per_device,
        mesh=mesh,
        in_specs=placed,
        out_specs=(P("row", "col"), P("row", "col"), P("row", "col")),
        check_vma=False,
    )
```

```python
import jax
import jax.numpy as jnp
import numpy as np
from jax import lax
from jax.experimental import pallas as pl
from jax.experimental.pallas import tpu as pltpu
from jax.sharding import PartitionSpec as P

first_fix = 0.9999734386
second_fix = 0.9940794709

AXES = ("row", "col")
SIZES = {"y": 4, "xl": 2, "k": 2, "xh": 2, "z": 8}
BF, F32 = jnp.bfloat16, jnp.float32
B, H, W = 320, 160, 640
YX = [(0, 0), (-1, 0), (1, 0), (0, 1), (-1, 1), (1, 1), (2, 0), (2, 1)]
ZS = [0, -1, 1, -2, 2, -3, 3, 4]
STEP = 80
C = 384


def place(i):
    r, c = divmod(i, 16)
    return {"y": r // 4, "xl": r // 2 % 2, "k": r % 2, "xh": c // 8, "z": c % 8}


def move(x, **steps):
    pairs = []
    for i in range(256):
        d = place(i)
        k = d["k"]
        for name, step in steps.items():
            turned = -step if k and name in "yz" else step
            d[name] = (d[name] + turned) % SIZES[name]
        pairs.append((i, (d["y"] * 4 + d["xl"] * 2 + d["k"]) * 16 + d["xh"] * 8 + d["z"]))
    return lax.ppermute(x, AXES, pairs)


ANY = pl.BlockSpec(memory_space=pl.ANY)
VMEM = pl.BlockSpec(memory_space=pltpu.VMEM)
SMEM = pl.BlockSpec(memory_space=pltpu.SMEM)


def call(body, out, at, apart=(), vmem=(), scratch=(), limit=40, flops=0, out_spec=None):
    args = [at, *apart, *vmem]
    size = sum(a.size * a.dtype.itemsize for a in args) + sum(
        int(np.prod(o.shape)) * jnp.dtype(o.dtype).itemsize for o in out
    )
    return pl.pallas_call(
        body,
        out_shape=list(out),
        in_specs=[SMEM] + [ANY] * len(apart) + [VMEM] * len(vmem),
        out_specs=[out_spec or VMEM] * len(out),
        scratch_shapes=list(scratch),
        compiler_params=pltpu.CompilerParams(vmem_limit_bytes=limit << 20),
        cost_estimate=pl.CostEstimate(flops=flops, bytes_accessed=size, transcendentals=0),
    )(*args)


def sds(shape, dtype=BF):
    return jax.ShapeDtypeStruct(shape, dtype)


def far_sds(shape, dtype=BF):
    return pltpu.HBM(shape, dtype)


def in_hbm(x):
    return pltpu.with_memory_space_constraint(x, pltpu.HBM)


def in_vmem(x):
    return pltpu.with_memory_space_constraint(x, pltpu.VMEM)


def after(x, *others):
    return lax.optimization_barrier((x, *others))[0]


def chip_at(at, dy, p):
    return lax.rem(at[0] + (1 - 2 * at[2]) * dy + 4, 4) * 2 + lax.rem(at[1] + p, 2)


def ring_at(at, d):
    return lax.rem(at[4] + (1 - 2 * at[2]) * d + 8, 8)


def copies(pairs, sems):
    started = []
    for n, (a, b) in enumerate(pairs):
        c = pltpu.make_async_copy(a, b, sems.at[n])
        c.start()
        started.append(c)
    for c in started:
        c.wait()


def rows(i, n):
    return pl.ds(pl.multiple_of(i, 16), n)


def to_half(at, own, other, parts, shape=sds):
    dt = own.dtype

    def body(at, own, other, *rest):
        outs, (stack, turned, mine, sems) = rest[: len(parts)], rest[len(parts) :]
        k = at[2]
        copy = pltpu.make_async_copy(own, mine, sems.at[0])
        copy.start()
        stack[rows(B * (1 - k), B), 0:B] = other[...]
        copy.wait()
        stack[rows(B * k, B), 0:B] = mine[...]
        turned[...] = jnp.transpose(stack[...])
        for out, (lo, n) in zip(outs, parts):
            out[...] = turned[rows(H * k + lo, n), :]

    return call(
        body,
        [shape((n, W), dt) for _, n in parts],
        at,
        apart=[in_hbm(own)],
        vmem=[other],
        scratch=[pltpu.VMEM((W, C), dt), pltpu.VMEM((C, W), dt), pltpu.VMEM((B, B), dt), pltpu.SemaphoreType.DMA((1,))],
        limit=16,
        out_spec=pl.BlockSpec() if shape is far_sds else None,
    )


def from_half(at, own, other):
    n = len(own)
    dt = own[0].dtype

    def body(at, *rest):
        mine, theirs, (out, stack, turned) = rest[:n], rest[n : 2 * n], rest[2 * n :]
        k = at[2]
        lo = 0
        for a, b in zip(mine, theirs):
            h = a.shape[0]
            stack[rows(H * k + lo, h), :] = a[...]
            stack[rows(H * (1 - k) + lo, h), :] = b[...]
            lo += h
        turned[...] = jnp.transpose(stack[...])
        out[...] = turned[rows(B * k, B), 0:B]

    return call(
        body,
        [sds((B, B), dt)],
        at,
        vmem=(*own, *other),
        scratch=[pltpu.VMEM((384, W), dt), pltpu.VMEM((W, 384), dt)],
        limit=16,
    )[0]


def both_left(at, own, other):
    def body(at, own, other, out, sems):
        k = at[2]
        pairs = []
        for i in range(5):
            part = slice(64 * i, 64 * i + 64)
            pairs.append((own.at[part, :], out.at[rows(B * k + 64 * i, 64), :]))
            pairs.append((other.at[part, :], out.at[rows(B * (1 - k) + 64 * i, 64), :]))
        copies(pairs, sems)

    return in_vmem(
        call(
            body,
            [sds((W, 16 * B))],
            at,
            apart=(own, other),
            scratch=[pltpu.SemaphoreType.DMA((10,))],
            limit=4,
            out_spec=ANY,
        )[0]
    )


def right_half(at, columns):
    def body(at, columns, out, stack, turned):
        k = at[2]
        stack[B:, :] = jnp.zeros((C - B, 8 * B), BF)
        stack[0:B, :] = columns[...]
        for t in range(20):
            turned[128 * t : 128 * t + 128, :] = jnp.transpose(stack[:, 128 * t : 128 * t + 128])
        for z in range(8):
            out[H * z : H * z + H, :] = turned[rows(B * z + H * k, H), :]

    return call(
        body,
        [sds((4 * B, C))],
        at,
        vmem=[columns],
        scratch=[pltpu.VMEM((C, 8 * B), BF), pltpu.VMEM((8 * B, C), BF)],
        limit=24,
    )[0]


def add(*xs):
    total = xs[0].astype(F32)
    for x in xs[1:]:
        total = total + x.astype(F32)
    return total.astype(BF)


def scatter_yx(part):
    far = add(part[2, 0], move(part[2, 1], xl=1))
    side = add(part[0, 1], move(part[1, 1], y=1), move(part[-1, 1], y=-1))
    near = [move(part[1, 0], y=1), move(part[-1, 0], y=-1)]
    far = jnp.concatenate([move(far[:STEP], y=2), move(far[STEP:], y=-2)], 0)
    return add(part[0, 0], *near, far, move(side, xl=1))


def gather_z(x, early):
    plus = minus = x
    got = [[x]]
    for step in range(3):
        plus, minus = move(plus, z=1), move(minus, z=-1)
        got += [[plus], [minus]]
        plus, minus, *_ = lax.optimization_barrier((plus, minus, *([early] if step == 0 else [])))
    return got, plus, minus


def gather_last(plus, minus):
    return [move(plus[:STEP], z=1), move(minus[STEP:], z=-1)]


def scatter_z(part):
    plus, minus = move(part[4][:STEP], z=1), move(part[4][STEP:], z=-1)
    plus = jnp.concatenate([add(part[3][:STEP], plus), part[3][STEP:]], 0)
    minus = jnp.concatenate([part[-3][:STEP], add(part[-3][STEP:], minus)], 0)
    for s in (2, 1, 0):
        plus, minus, part[0] = lax.optimization_barrier((plus, minus, part[0]))
        plus, minus = move(plus, z=1), move(minus, z=-1)
        if s:
            plus, minus = add(part[s], plus), add(part[-s], minus)
    return add(part[0], plus, minus)


def times_left(at, which, pieces, left, before=None):
    flat = [(i, n, x) for i, xs in enumerate(pieces) for n, x in enumerate(xs)]
    n = len(flat)
    wide = len(which) * W

    def body(at, *rest):
        blocks, left, out, stack, sems = rest[:n], rest[n], *rest[-3:]
        waits = [[] for _ in which]
        for m, ((i, h, _), r) in enumerate(zip(flat, blocks)):
            to = stack.at[STEP * h : STEP * h + r.shape[0], W * i : W * i + W]
            copy = pltpu.make_async_copy(r, to, sems.at[m])
            copy.start()
            waits[i].append(copy)
        total = rest[n + 1][...] if before is not None else jnp.zeros((H, W), F32)
        for i, (dy, p) in enumerate(which):
            for copy in waits[i]:
                copy.wait()
            cols = pl.ds(pl.multiple_of(chip_at(at, dy, p) * W, 128), W)
            total += lax.dot_general(
                stack[:, W * i : W * i + W], left[:, cols], (((1,), (1,)), ((), ())), preferred_element_type=F32
            )
        out[...] = total.astype(out.dtype)

    last = before is not None
    return call(
        body,
        [sds((H, W), BF if last else F32)],
        at,
        apart=[x for _, _, x in flat],
        vmem=[left, before] if last else [left],
        scratch=[pltpu.VMEM((H, wide), BF), pltpu.SemaphoreType.DMA((n,))],
        flops=2 * H * W * wide,
        limit=24,
    )[0]


def times_right(at, which, pieces, right, before=()):
    sides = len(right)
    flat = [(i, h, x) for i, xs in enumerate(pieces) for h, x in enumerate(xs)]
    n = len(flat)
    deep = len(which) * H

    def body(at, *rest):
        blocks, right, stack, factor, sems = rest[:n], rest[n : n + sides], *rest[-3:]
        started = []
        for m, ((i, h, _), r) in enumerate(zip(flat, blocks)):
            to = stack.at[H * i + STEP * h : H * i + STEP * h + r.shape[0], :]
            started.append(pltpu.make_async_copy(r, to, sems.at[m]))
            started[-1].start()
        for i, d in enumerate(which):
            for side in range(sides):
                factor[H * i : H * i + H, C * side : C * side + C] = right[side][rows(ring_at(at, d) * H, H), :]
        for copy in started:
            copy.wait()
        part = lax.dot_general(stack[...], factor[...], (((0,), (0,)), ((), ())), preferred_element_type=F32)
        if not before:
            rest[n + sides][...] = part
            return
        keep, far, give, total = rest[n + 2 * sides : n + 2 * sides + 4]
        for side in range(sides):
            cols = slice(C * side, C * side + C)
            total[:, cols] = rest[n + sides + side][...] + part[:, cols]
        for half in range(2):
            lo, to = H * half, slice(B * half, B * half + B)
            mine, theirs = rows(B * at[2] + lo, H), rows(B * (1 - at[2]) + lo, H)
            keep[:, to] = total[mine, 0:B]
            far[:, to] = total[mine, C : C + B]
            give[0:H, to] = total[theirs, 0:B].astype(BF)
            give[H:, to] = total[theirs, C : C + B].astype(BF)

    scratch = [pltpu.VMEM((deep, W), BF), pltpu.VMEM((deep, sides * C), BF), pltpu.SemaphoreType.DMA((n,))]
    flops = 2 * W * sides * C * deep
    args = [x for _, _, x in flat]
    if not before:
        return call(body, [sds((W, sides * C), F32)], at, apart=args, vmem=right, scratch=scratch, flops=flops, limit=24)[0]
    return call(
        body,
        [sds((H, W), F32), sds((H, W), F32), sds((B, W))],
        at,
        apart=args,
        vmem=[*right, *before],
        scratch=[pltpu.VMEM((W, 2 * C), F32), *scratch],
        flops=flops,
        limit=24,
    )


def left_piece(at, direction, left, d):
    cols = pl.ds(pl.multiple_of(chip_at(at, *d) * W, 128), W)
    return jnp.dot(direction, left[:, cols], preferred_element_type=F32).astype(BF)


EARLY = [(2, 1), (1, 1), (-1, 1), (1, 0), (-1, 0)]
LATE = [(2, 0), (0, 1), (0, 0)]


def moments(at, keep, near, far, avg, sq):
    def body(at, keep, near, far, avg, sq, new_avg, new_sq, direction):
        packed = keep[...] + near[0:H, :].astype(F32) + far[...].astype(F32)
        for half in range(2):
            here = slice(H * half, H * half + H)
            rotated = packed[:, B * half : B * half + B]
            a = 0.9 * avg[here, :] + 0.1 * rotated
            s = 0.95 * sq[here, :] + 0.05 * rotated * rotated
            new_avg[here, :] = a
            new_sq[here, :] = s
            direction[here, :] = (a / first_fix / (jnp.sqrt(s / second_fix) + 1e-08)).astype(BF)

    out = [sds((B, B), F32), sds((B, B), F32), sds((B, B))]
    return call(body, out, at, vmem=(keep, near, far, avg, sq), limit=16)


def left_early(at, own, other, left):
    def body(at, own, other, left, turned_out, *rest):
        outs, (stack, turned) = rest[: len(EARLY)], rest[len(EARLY) :]
        k = at[2]
        stack[rows(B * k, B), 0:B] = own[...]
        stack[rows(B * (1 - k), B), 0:B] = other[...]
        turned[...] = jnp.transpose(stack[...])
        direction = turned[rows(H * k, H), :]
        turned_out[...] = direction
        for d, out in zip(EARLY, outs):
            out[...] = left_piece(at, direction, left, d)

    direction, *parts = call(
        body,
        [sds((H, W))] * (1 + len(EARLY)),
        at,
        vmem=(own, other, left),
        scratch=[pltpu.VMEM((W, C), BF), pltpu.VMEM((C, W), BF)],
        flops=2 * H * W * 5 * W,
        limit=24,
    )
    return direction, dict(zip(EARLY, parts))


def left_back(at, direction, left):
    def body(at, direction, left, *outs):
        for d, out in zip(LATE, outs):
            out[...] = left_piece(at, direction[...], left, d)

    return dict(zip(LATE, call(body, [sds((H, W))] * 3, at, vmem=(direction, left), flops=2 * H * W * 3 * W, limit=24)))


def right_back(at, blocks, right, which):
    def body(at, *rest):
        own, near, far, far_near, right, right_far = rest[:6]
        outs, stack, chosen = rest[6:-2], rest[-2], rest[-1]
        k = at[2]
        stack[B:C, :] = jnp.zeros((C - B, W), BF)
        stack[C + B :, :] = jnp.zeros((C - B, W), BF)
        stack[rows(H * k, H), :] = own[...]
        stack[rows(H * (1 - k), H), :] = near[...]
        stack[rows(C + H * k, H), :] = far[...]
        stack[rows(C + H * (1 - k), H), :] = far_near[...]
        for i, d in enumerate(which):
            chosen[H * i : H * i + H, :C] = right[rows(ring_at(at, d) * H, H), :]
            chosen[H * i : H * i + H, C:] = right_far[rows(ring_at(at, d) * H, H), :]
        total = jnp.dot(chosen[...], stack[...], preferred_element_type=F32).astype(BF)
        for i in range(len(which)):
            outs[i][...] = total[H * i : H * i + H]

    n = len(which)
    outs = call(
        body,
        [sds((H, W))] * n,
        at,
        vmem=(*blocks, *right),
        scratch=[pltpu.VMEM((2 * C, W), BF), pltpu.VMEM((n * H, 2 * C), BF)],
        flops=2 * n * H * W * W,
        limit=24,
    )
    return dict(zip(which, outs))


def per_device(gradient, left_basis, right_basis, exp_avg, exp_avg_sq):
    row, col = lax.axis_index("row"), lax.axis_index("col")
    k, xh = row % 2, col // 8
    at = jnp.stack([row // 4, row // 2 % 2, k, xh, col % 8]).astype(jnp.int32)

    gradient_far = move(gradient, k=1)
    half = 8 * B
    own_left = after(left_basis.T, gradient_far)
    far_left = move(own_left, k=1)
    x, top, bottom = to_half(at, gradient, gradient_far, [(0, H), (0, STEP), (STEP, STEP)], far_sds)
    side = move(x, xl=1)
    behind, ahead = move(x, y=1), move(x, y=-1)
    bottom = after(bottom, far_left)
    far = [move(top, y=2), move(bottom, y=-2)]
    whole = after(right_basis.T, x)
    sent = lax.dynamic_slice(whole, (0, (1 - xh) * half), (B, half))
    kept = lax.dynamic_slice(whole, (0, xh * half), (B, half))
    left = both_left(at, in_hbm(after(own_left, sent, kept)), in_hbm(far_left))
    got = move(after(sent, left, side, behind, ahead, *far), xh=1, xl=1)
    side_in = after(side, left)
    side_behind, side_ahead = move(side_in, y=1), move(side_in, y=-1)
    side_far = [move(f, xl=1) for f in far]

    part = times_left(at, YX[:4], [[x], [behind], [ahead], [side]], left)
    x = times_left(at, YX[4:], [[side_behind], [side_ahead], far, side_far], left, part)
    own_right = right_half(at, after(kept, x))
    pieces, plus, minus = gather_z(x, own_right)
    own_part = times_right(at, ZS[:5], pieces[:5], [own_right])
    far_right = right_half(at, after(got, own_part, *pieces[5], *pieces[6]))
    pieces.append(gather_last(after(plus, own_part), after(minus, own_part)))
    far_part = times_right(at, ZS[:5], pieces[:5], [far_right])
    right = (own_right, far_right)
    keep, far, give = times_right(at, ZS[5:], pieces[5:], right, (own_part, far_part))
    near = move(give, k=1)
    far = move(add(far, near[H:]), xh=1)
    new_avg, new_sq, direction = moments(at, keep, near, far, exp_avg, exp_avg_sq)
    direction, part = left_early(at, direction, move(direction, k=1), left)
    part |= left_back(at, direction, left)

    own = scatter_yx(part)
    far = move(own, xh=1)
    blocks = (own, move(own, k=1), far, move(far, k=1))
    end = scatter_z(right_back(at, blocks, right, [4, 3, -3]) | right_back(at, blocks, right, [0, 2, -2, 1, -1]))
    update = from_half(at, [end], [move(end, k=1)])
    return (new_avg, new_sq, update)


def solution(mesh):
    placed = (P("row", "col"), P(None, "row"), P(None, "col"), P("row", "col"), P("row", "col"))
    return jax.shard_map(
        per_device,
        mesh=mesh,
        in_specs=placed,
        out_specs=(P("row", "col"), P("row", "col"), P("row", "col")),
        check_vma=False,
    )
```

```python
import jax
import jax.numpy as jnp
import numpy as np
from jax import lax
from jax.experimental import pallas as pl
from jax.experimental.pallas import tpu as pltpu
from jax.sharding import PartitionSpec as P

first_fix = 0.9999734386
second_fix = 0.9940794709

AXES = ("row", "col")
SIZES = {"y": 4, "xl": 2, "k": 2, "xh": 2, "z": 8}
BF, F32 = jnp.bfloat16, jnp.float32
B, H, W = 320, 160, 640
YX = [(0, 0), (-1, 0), (1, 0), (0, 1), (-1, 1), (1, 1), (2, 0), (2, 1)]
ZS = [0, -1, 1, -2, 2, -3, 3, 4]
STEP = 80
C = 384


def place(i):
    r, c = divmod(i, 16)
    return {"y": r // 4, "xl": r // 2 % 2, "k": r % 2, "xh": c // 8, "z": c % 8}


def move(x, **steps):
    pairs = []
    for i in range(256):
        d = place(i)
        for name, step in steps.items():
            d[name] = (d[name] + step) % SIZES[name]
        pairs.append((i, (d["y"] * 4 + d["xl"] * 2 + d["k"]) * 16 + d["xh"] * 8 + d["z"]))
    return lax.ppermute(x, AXES, pairs)


ANY = pl.BlockSpec(memory_space=pl.ANY)
VMEM = pl.BlockSpec(memory_space=pltpu.VMEM)
SMEM = pl.BlockSpec(memory_space=pltpu.SMEM)


def call(body, out, at, apart=(), vmem=(), scratch=(), limit=40, flops=0, out_spec=None):
    args = [at, *apart, *vmem]
    size = sum(a.size * a.dtype.itemsize for a in args) + sum(
        int(np.prod(o.shape)) * jnp.dtype(o.dtype).itemsize for o in out
    )
    return pl.pallas_call(
        body,
        out_shape=list(out),
        in_specs=[SMEM] + [ANY] * len(apart) + [VMEM] * len(vmem),
        out_specs=[out_spec or VMEM] * len(out),
        scratch_shapes=list(scratch),
        compiler_params=pltpu.CompilerParams(vmem_limit_bytes=limit << 20),
        cost_estimate=pl.CostEstimate(flops=flops, bytes_accessed=size, transcendentals=0),
    )(*args)


def sds(shape, dtype=BF):
    return jax.ShapeDtypeStruct(shape, dtype)


def far_sds(shape, dtype=BF):
    return pltpu.HBM(shape, dtype)


def in_hbm(x):
    return pltpu.with_memory_space_constraint(x, pltpu.HBM)


def in_vmem(x):
    return pltpu.with_memory_space_constraint(x, pltpu.VMEM)


def after(x, *others):
    return lax.optimization_barrier((x, *others))[0]


def chip_at(at, dy, p):
    return lax.rem(at[0] + dy + 4, 4) * 2 + lax.rem(at[1] + p, 2)


def ring_at(at, d):
    return lax.rem(at[4] + d + 8, 8)


def copies(pairs, sems):
    started = []
    for n, (a, b) in enumerate(pairs):
        c = pltpu.make_async_copy(a, b, sems.at[n])
        c.start()
        started.append(c)
    for c in started:
        c.wait()


def rows(i, n):
    return pl.ds(pl.multiple_of(i, 16), n)


def to_half(at, own, other, parts, shape=sds):
    dt = own.dtype

    def body(at, own, other, *rest):
        outs, (stack, turned, mine, sems) = rest[: len(parts)], rest[len(parts) :]
        k = at[2]
        copy = pltpu.make_async_copy(own, mine, sems.at[0])
        copy.start()
        stack[rows(B * (1 - k), B), 0:B] = other[...]
        copy.wait()
        stack[rows(B * k, B), 0:B] = mine[...]
        turned[...] = jnp.transpose(stack[...])
        for out, (lo, n) in zip(outs, parts):
            out[...] = turned[rows(H * k + lo, n), :]

    return call(
        body,
        [shape((n, W), dt) for _, n in parts],
        at,
        apart=[in_hbm(own)],
        vmem=[other],
        scratch=[pltpu.VMEM((W, C), dt), pltpu.VMEM((C, W), dt), pltpu.VMEM((B, B), dt), pltpu.SemaphoreType.DMA((1,))],
        limit=16,
        out_spec=pl.BlockSpec() if shape is far_sds else None,
    )


def from_half(at, own, other):
    n = len(own)
    dt = own[0].dtype

    def body(at, *rest):
        mine, theirs, (out, stack, turned) = rest[:n], rest[n : 2 * n], rest[2 * n :]
        k = at[2]
        lo = 0
        for a, b in zip(mine, theirs):
            h = a.shape[0]
            stack[rows(H * k + lo, h), :] = a[...]
            stack[rows(H * (1 - k) + lo, h), :] = b[...]
            lo += h
        turned[...] = jnp.transpose(stack[...])
        out[...] = turned[rows(B * k, B), 0:B]

    return call(
        body,
        [sds((B, B), dt)],
        at,
        vmem=(*own, *other),
        scratch=[pltpu.VMEM((384, W), dt), pltpu.VMEM((W, 384), dt)],
        limit=16,
    )[0]


def both_left(at, own, other):
    def body(at, own, other, out, sems):
        k = at[2]
        pairs = []
        for i in range(5):
            part = slice(64 * i, 64 * i + 64)
            pairs.append((own.at[part, :], out.at[rows(B * k + 64 * i, 64), :]))
            pairs.append((other.at[part, :], out.at[rows(B * (1 - k) + 64 * i, 64), :]))
        copies(pairs, sems)

    return in_vmem(
        call(
            body,
            [sds((W, 16 * B))],
            at,
            apart=(own, other),
            scratch=[pltpu.SemaphoreType.DMA((10,))],
            limit=4,
            out_spec=ANY,
        )[0]
    )


def right_half(at, columns):
    def body(at, columns, out, stack, turned):
        k = at[2]
        stack[B:, :] = jnp.zeros((C - B, 8 * B), BF)
        stack[0:B, :] = columns[...]
        for t in range(20):
            turned[128 * t : 128 * t + 128, :] = jnp.transpose(stack[:, 128 * t : 128 * t + 128])
        for z in range(8):
            out[H * z : H * z + H, :] = turned[rows(B * z + H * k, H), :]

    return call(
        body,
        [sds((4 * B, C))],
        at,
        vmem=[columns],
        scratch=[pltpu.VMEM((C, 8 * B), BF), pltpu.VMEM((8 * B, C), BF)],
        limit=24,
    )[0]


def add(*xs):
    total = xs[0].astype(F32)
    for x in xs[1:]:
        total = total + x.astype(F32)
    return total.astype(BF)


def scatter_yx(part):
    far = add(part[2, 0], move(part[2, 1], xl=1))
    side = add(part[0, 1], move(part[1, 1], y=1), move(part[-1, 1], y=-1))
    near = [move(part[1, 0], y=1), move(part[-1, 0], y=-1)]
    far = jnp.concatenate([move(far[:STEP], y=2), move(far[STEP:], y=-2)], 0)
    return add(part[0, 0], *near, far, move(side, xl=1))


def gather_z(x, early):
    plus = minus = x
    got = [[x]]
    for step in range(3):
        plus, minus = move(plus, z=1), move(minus, z=-1)
        got += [[plus], [minus]]
        plus, minus, *_ = lax.optimization_barrier((plus, minus, *([early] if step == 0 else [])))
    return got, plus, minus


def gather_last(plus, minus):
    return [move(plus[:STEP], z=1), move(minus[STEP:], z=-1)]


def scatter_z(part):
    plus, minus = move(part[4][:STEP], z=1), move(part[4][STEP:], z=-1)
    plus = jnp.concatenate([add(part[3][:STEP], plus), part[3][STEP:]], 0)
    minus = jnp.concatenate([part[-3][:STEP], add(part[-3][STEP:], minus)], 0)
    for s in (2, 1, 0):
        plus, minus, part[0] = lax.optimization_barrier((plus, minus, part[0]))
        plus, minus = move(plus, z=1), move(minus, z=-1)
        if s:
            plus, minus = add(part[s], plus), add(part[-s], minus)
    return add(part[0], plus, minus)


def times_left(at, which, pieces, left, before=None):
    flat = [(i, n, x) for i, xs in enumerate(pieces) for n, x in enumerate(xs)]
    n = len(flat)
    wide = len(which) * W

    def body(at, *rest):
        blocks, left, out, stack, sems = rest[:n], rest[n], *rest[-3:]
        waits = [[] for _ in which]
        for m, ((i, h, _), r) in enumerate(zip(flat, blocks)):
            to = stack.at[STEP * h : STEP * h + r.shape[0], W * i : W * i + W]
            copy = pltpu.make_async_copy(r, to, sems.at[m])
            copy.start()
            waits[i].append(copy)
        total = rest[n + 1][...] if before is not None else jnp.zeros((H, W), F32)
        for i, (dy, p) in enumerate(which):
            for copy in waits[i]:
                copy.wait()
            cols = pl.ds(pl.multiple_of(chip_at(at, dy, p) * W, 128), W)
            total += lax.dot_general(
                stack[:, W * i : W * i + W], left[:, cols], (((1,), (1,)), ((), ())), preferred_element_type=F32
            )
        out[...] = total.astype(out.dtype)

    last = before is not None
    return call(
        body,
        [sds((H, W), BF if last else F32)],
        at,
        apart=[x for _, _, x in flat],
        vmem=[left, before] if last else [left],
        scratch=[pltpu.VMEM((H, wide), BF), pltpu.SemaphoreType.DMA((n,))],
        flops=2 * H * W * wide,
        limit=24,
    )[0]


def times_right(at, which, pieces, right, before=()):
    sides = len(right)
    flat = [(i, h, x) for i, xs in enumerate(pieces) for h, x in enumerate(xs)]
    n = len(flat)
    deep = len(which) * H

    def body(at, *rest):
        blocks, right, stack, factor, sems = rest[:n], rest[n : n + sides], *rest[-3:]
        started = []
        for m, ((i, h, _), r) in enumerate(zip(flat, blocks)):
            to = stack.at[H * i + STEP * h : H * i + STEP * h + r.shape[0], :]
            started.append(pltpu.make_async_copy(r, to, sems.at[m]))
            started[-1].start()
        for i, d in enumerate(which):
            for side in range(sides):
                factor[H * i : H * i + H, C * side : C * side + C] = right[side][rows(ring_at(at, d) * H, H), :]
        for copy in started:
            copy.wait()
        part = lax.dot_general(stack[...], factor[...], (((0,), (0,)), ((), ())), preferred_element_type=F32)
        if not before:
            rest[n + sides][...] = part
            return
        keep, far, give, total = rest[n + 2 * sides : n + 2 * sides + 4]
        for side in range(sides):
            cols = slice(C * side, C * side + C)
            total[:, cols] = rest[n + sides + side][...] + part[:, cols]
        for half in range(2):
            lo, to = H * half, slice(B * half, B * half + B)
            mine, theirs = rows(B * at[2] + lo, H), rows(B * (1 - at[2]) + lo, H)
            keep[:, to] = total[mine, 0:B]
            far[:, to] = total[mine, C : C + B]
            give[0:H, to] = total[theirs, 0:B].astype(BF)
            give[H:, to] = total[theirs, C : C + B].astype(BF)

    scratch = [pltpu.VMEM((deep, W), BF), pltpu.VMEM((deep, sides * C), BF), pltpu.SemaphoreType.DMA((n,))]
    flops = 2 * W * sides * C * deep
    args = [x for _, _, x in flat]
    if not before:
        return call(body, [sds((W, sides * C), F32)], at, apart=args, vmem=right, scratch=scratch, flops=flops, limit=24)[0]
    return call(
        body,
        [sds((H, W), F32), sds((H, W), F32), sds((B, W))],
        at,
        apart=args,
        vmem=[*right, *before],
        scratch=[pltpu.VMEM((W, 2 * C), F32), *scratch],
        flops=flops,
        limit=24,
    )


def left_piece(at, direction, left, d):
    cols = pl.ds(pl.multiple_of(chip_at(at, *d) * W, 128), W)
    return jnp.dot(direction, left[:, cols], preferred_element_type=F32).astype(BF)


EARLY = [(2, 1), (1, 1), (-1, 1), (1, 0), (-1, 0)]
LATE = [(2, 0), (0, 1), (0, 0)]


def moments(at, keep, near, far, avg, sq):
    def body(at, keep, near, far, avg, sq, new_avg, new_sq, direction):
        packed = keep[...] + near[0:H, :].astype(F32) + far[...].astype(F32)
        for half in range(2):
            here = slice(H * half, H * half + H)
            rotated = packed[:, B * half : B * half + B]
            a = 0.9 * avg[here, :] + 0.1 * rotated
            s = 0.95 * sq[here, :] + 0.05 * rotated * rotated
            new_avg[here, :] = a
            new_sq[here, :] = s
            direction[here, :] = (a / first_fix / (jnp.sqrt(s / second_fix) + 1e-08)).astype(BF)

    out = [sds((B, B), F32), sds((B, B), F32), sds((B, B))]
    return call(body, out, at, vmem=(keep, near, far, avg, sq), limit=16)


def left_early(at, own, other, left):
    def body(at, own, other, left, turned_out, *rest):
        outs, (stack, turned) = rest[: len(EARLY)], rest[len(EARLY) :]
        k = at[2]
        stack[rows(B * k, B), 0:B] = own[...]
        stack[rows(B * (1 - k), B), 0:B] = other[...]
        turned[...] = jnp.transpose(stack[...])
        direction = turned[rows(H * k, H), :]
        turned_out[...] = direction
        for d, out in zip(EARLY, outs):
            out[...] = left_piece(at, direction, left, d)

    direction, *parts = call(
        body,
        [sds((H, W))] * (1 + len(EARLY)),
        at,
        vmem=(own, other, left),
        scratch=[pltpu.VMEM((W, C), BF), pltpu.VMEM((C, W), BF)],
        flops=2 * H * W * 5 * W,
        limit=24,
    )
    return direction, dict(zip(EARLY, parts))


def left_back(at, direction, left):
    def body(at, direction, left, *outs):
        for d, out in zip(LATE, outs):
            out[...] = left_piece(at, direction[...], left, d)

    return dict(zip(LATE, call(body, [sds((H, W))] * 3, at, vmem=(direction, left), flops=2 * H * W * 3 * W, limit=24)))


def right_back(at, blocks, right, which):
    def body(at, *rest):
        own, near, far, far_near, right, right_far = rest[:6]
        outs, stack, chosen = rest[6:-2], rest[-2], rest[-1]
        k = at[2]
        stack[B:C, :] = jnp.zeros((C - B, W), BF)
        stack[C + B :, :] = jnp.zeros((C - B, W), BF)
        stack[rows(H * k, H), :] = own[...]
        stack[rows(H * (1 - k), H), :] = near[...]
        stack[rows(C + H * k, H), :] = far[...]
        stack[rows(C + H * (1 - k), H), :] = far_near[...]
        for i, d in enumerate(which):
            chosen[H * i : H * i + H, :C] = right[rows(ring_at(at, d) * H, H), :]
            chosen[H * i : H * i + H, C:] = right_far[rows(ring_at(at, d) * H, H), :]
        total = jnp.dot(chosen[...], stack[...], preferred_element_type=F32).astype(BF)
        for i in range(len(which)):
            outs[i][...] = total[H * i : H * i + H]

    n = len(which)
    outs = call(
        body,
        [sds((H, W))] * n,
        at,
        vmem=(*blocks, *right),
        scratch=[pltpu.VMEM((2 * C, W), BF), pltpu.VMEM((n * H, 2 * C), BF)],
        flops=2 * n * H * W * W,
        limit=24,
    )
    return dict(zip(which, outs))


def per_device(gradient, left_basis, right_basis, exp_avg, exp_avg_sq):
    row, col = lax.axis_index("row"), lax.axis_index("col")
    k, xh = row % 2, col // 8
    at = jnp.stack([row // 4, row // 2 % 2, k, xh, col % 8]).astype(jnp.int32)

    gradient_far = move(gradient, k=1)
    half = 8 * B
    own_left = after(left_basis.T, gradient_far)
    far_left = move(own_left, k=1)
    x, top, bottom = to_half(at, gradient, gradient_far, [(0, H), (0, STEP), (STEP, STEP)])
    side = move(x, xl=1)
    behind, ahead = move(x, y=1), move(x, y=-1)
    bottom = after(bottom, far_left)
    far = [move(top, y=2), move(bottom, y=-2)]
    whole = after(right_basis.T, x)
    sent = lax.dynamic_slice(whole, (0, (1 - xh) * half), (B, half))
    kept = lax.dynamic_slice(whole, (0, xh * half), (B, half))
    left = both_left(at, in_hbm(after(own_left, sent, kept)), far_left)
    got = move(after(sent, left, side, behind, ahead, *far), xh=1, xl=1)
    side_in = after(side, left)
    side_behind, side_ahead = move(side_in, y=1), move(side_in, y=-1)
    side_far = [move(f, xl=1) for f in far]

    part = times_left(at, YX[:4], [[x], [behind], [ahead], [side]], left)
    x = times_left(at, YX[4:], [[side_behind], [side_ahead], far, side_far], left, part)
    own_right = right_half(at, after(kept, x))
    pieces, plus, minus = gather_z(x, own_right)
    own_part = times_right(at, ZS[:5], pieces[:5], [own_right])
    far_right = right_half(at, after(got, own_part, *pieces[5], *pieces[6]))
    pieces.append(gather_last(after(plus, own_part), after(minus, own_part)))
    far_part = times_right(at, ZS[:5], pieces[:5], [far_right])
    right = (own_right, far_right)
    keep, far, give = times_right(at, ZS[5:], pieces[5:], right, (own_part, far_part))
    near = move(give, k=1)
    far = move(add(far, near[H:]), xh=1)
    new_avg, new_sq, direction = moments(at, keep, near, far, exp_avg, exp_avg_sq)
    direction, part = left_early(at, direction, move(direction, k=1), left)
    part |= left_back(at, direction, left)

    own = scatter_yx(part)
    far = move(own, xh=1)
    blocks = (own, move(own, k=1), far, move(far, k=1))
    end = scatter_z(right_back(at, blocks, right, [4, 3, -3]) | right_back(at, blocks, right, [0, 2, -2, 1, -1]))
    update = from_half(at, [end], [move(end, k=1)])
    return (new_avg, new_sq, update)


def solution(mesh):
    placed = (P("row", "col"), P(None, "row"), P(None, "col"), P("row", "col"), P("row", "col"))
    return jax.shard_map(
        per_device,
        mesh=mesh,
        in_specs=placed,
        out_specs=(P("row", "col"), P("row", "col"), P("row", "col")),
        check_vma=False,
    )
```

```python
import jax
import jax.numpy as jnp
import numpy as np
from jax import lax
from jax.experimental import pallas as pl
from jax.experimental.pallas import tpu as pltpu
from jax.sharding import PartitionSpec as P

first_fix = 0.9999734386
second_fix = 0.9940794709

AXES = ("row", "col")
SIZES = {"y": 4, "xl": 2, "k": 2, "xh": 2, "z": 8}
BF, F32 = jnp.bfloat16, jnp.float32
B, H, W = 320, 160, 640
YX = [(0, 0), (-1, 0), (1, 0), (0, 1), (-1, 1), (1, 1), (2, 0), (2, 1)]
ZS = [0, -1, 1, -2, 2, -3, 3, 4]
STEP = 80
C = 384


def place(i):
    r, c = divmod(i, 16)
    return {"y": r // 4, "xl": r // 2 % 2, "k": r % 2, "xh": c // 8, "z": c % 8}


def move(x, **steps):
    pairs = []
    for i in range(256):
        d = place(i)
        for name, step in steps.items():
            d[name] = (d[name] + step) % SIZES[name]
        pairs.append((i, (d["y"] * 4 + d["xl"] * 2 + d["k"]) * 16 + d["xh"] * 8 + d["z"]))
    return lax.ppermute(x, AXES, pairs)


ANY = pl.BlockSpec(memory_space=pl.ANY)
VMEM = pl.BlockSpec(memory_space=pltpu.VMEM)
SMEM = pl.BlockSpec(memory_space=pltpu.SMEM)


def call(body, out, at, apart=(), vmem=(), scratch=(), limit=40, flops=0, out_spec=None):
    args = [at, *apart, *vmem]
    size = sum(a.size * a.dtype.itemsize for a in args) + sum(
        int(np.prod(o.shape)) * jnp.dtype(o.dtype).itemsize for o in out
    )
    return pl.pallas_call(
        body,
        out_shape=list(out),
        in_specs=[SMEM] + [ANY] * len(apart) + [VMEM] * len(vmem),
        out_specs=[out_spec or VMEM] * len(out),
        scratch_shapes=list(scratch),
        compiler_params=pltpu.CompilerParams(vmem_limit_bytes=limit << 20),
        cost_estimate=pl.CostEstimate(flops=flops, bytes_accessed=size, transcendentals=0),
    )(*args)


def sds(shape, dtype=BF):
    return jax.ShapeDtypeStruct(shape, dtype)


def far_sds(shape, dtype=BF):
    return pltpu.HBM(shape, dtype)


def in_hbm(x):
    return pltpu.with_memory_space_constraint(x, pltpu.HBM)


def in_vmem(x):
    return pltpu.with_memory_space_constraint(x, pltpu.VMEM)


def after(x, *others):
    return lax.optimization_barrier((x, *others))[0]


def chip_at(at, dy, p):
    return lax.rem(at[0] + dy + 4, 4) * 2 + lax.rem(at[1] + p, 2)


def ring_at(at, d):
    return lax.rem(at[4] + d + 8, 8)


def copies(pairs, sems):
    started = []
    for n, (a, b) in enumerate(pairs):
        c = pltpu.make_async_copy(a, b, sems.at[n])
        c.start()
        started.append(c)
    for c in started:
        c.wait()


def rows(i, n):
    return pl.ds(pl.multiple_of(i, 16), n)


def to_half(at, own, other, parts, shape=sds):
    dt = own.dtype

    def body(at, own, other, *rest):
        outs, (stack, turned, mine, sems) = rest[: len(parts)], rest[len(parts) :]
        k = at[2]
        copy = pltpu.make_async_copy(own, mine, sems.at[0])
        copy.start()
        stack[rows(B * (1 - k), B), 0:B] = other[...]
        copy.wait()
        stack[rows(B * k, B), 0:B] = mine[...]
        turned[...] = jnp.transpose(stack[...])
        for out, (lo, n) in zip(outs, parts):
            out[...] = turned[rows(H * k + lo, n), :]

    return call(
        body,
        [shape((n, W), dt) for _, n in parts],
        at,
        apart=[in_hbm(own)],
        vmem=[other],
        scratch=[pltpu.VMEM((W, C), dt), pltpu.VMEM((C, W), dt), pltpu.VMEM((B, B), dt), pltpu.SemaphoreType.DMA((1,))],
        limit=16,
        out_spec=pl.BlockSpec() if shape is far_sds else None,
    )


def from_half(at, own, other):
    n = len(own)
    dt = own[0].dtype

    def body(at, *rest):
        mine, theirs, (out, stack, turned) = rest[:n], rest[n : 2 * n], rest[2 * n :]
        k = at[2]
        lo = 0
        for a, b in zip(mine, theirs):
            h = a.shape[0]
            stack[rows(H * k + lo, h), :] = a[...]
            stack[rows(H * (1 - k) + lo, h), :] = b[...]
            lo += h
        turned[...] = jnp.transpose(stack[...])
        out[...] = turned[rows(B * k, B), 0:B]

    return call(
        body,
        [sds((B, B), dt)],
        at,
        vmem=(*own, *other),
        scratch=[pltpu.VMEM((384, W), dt), pltpu.VMEM((W, 384), dt)],
        limit=16,
    )[0]


def both_left(at, own, other):
    def body(at, own, other, out, sems):
        k = at[2]
        pairs = []
        for i in range(5):
            part = slice(64 * i, 64 * i + 64)
            pairs.append((own.at[part, :], out.at[rows(B * k + 64 * i, 64), :]))
            pairs.append((other.at[part, :], out.at[rows(B * (1 - k) + 64 * i, 64), :]))
        copies(pairs, sems)

    return in_vmem(
        call(
            body,
            [sds((W, 16 * B))],
            at,
            apart=(own, other),
            scratch=[pltpu.SemaphoreType.DMA((10,))],
            limit=4,
            out_spec=ANY,
        )[0]
    )


def right_half(at, columns):
    def body(at, columns, out, stack, turned):
        k = at[2]
        stack[B:, :] = jnp.zeros((C - B, 8 * B), BF)
        stack[0:B, :] = columns[...]
        for t in range(20):
            turned[128 * t : 128 * t + 128, :] = jnp.transpose(stack[:, 128 * t : 128 * t + 128])
        for z in range(8):
            out[H * z : H * z + H, :] = turned[rows(B * z + H * k, H), :]

    return call(
        body,
        [sds((4 * B, C))],
        at,
        vmem=[columns],
        scratch=[pltpu.VMEM((C, 8 * B), BF), pltpu.VMEM((8 * B, C), BF)],
        limit=24,
    )[0]


def add(*xs):
    total = xs[0].astype(F32)
    for x in xs[1:]:
        total = total + x.astype(F32)
    return total.astype(BF)


def scatter_yx(part):
    far = add(part[2, 0], move(part[2, 1], xl=1))
    side = add(part[0, 1], move(part[1, 1], y=1), move(part[-1, 1], y=-1))
    near = [move(part[1, 0], y=1), move(part[-1, 0], y=-1)]
    far = jnp.concatenate([move(far[:STEP], y=2), move(far[STEP:], y=-2)], 0)
    return add(part[0, 0], *near, far, move(side, xl=1))


def gather_z(x, early):
    plus = minus = x
    got = [[x]]
    for step in range(3):
        plus, minus = move(plus, z=1), move(minus, z=-1)
        got += [[plus], [minus]]
        plus, minus, *_ = lax.optimization_barrier((plus, minus, *([early] if step == 0 else [])))
    return got, plus, minus


def gather_last(plus, minus):
    return [move(plus[:STEP], z=1), move(minus[STEP:], z=-1)]


def scatter_z(part):
    plus, minus = move(part[4][:STEP], z=1), move(part[4][STEP:], z=-1)
    plus = jnp.concatenate([add(part[3][:STEP], plus), part[3][STEP:]], 0)
    minus = jnp.concatenate([part[-3][:STEP], add(part[-3][STEP:], minus)], 0)
    for s in (2, 1, 0):
        plus, minus, part[0] = lax.optimization_barrier((plus, minus, part[0]))
        plus, minus = move(plus, z=1), move(minus, z=-1)
        if s:
            plus, minus = add(part[s], plus), add(part[-s], minus)
    return add(part[0], plus, minus)


def times_left(at, which, pieces, left, before=None):
    flat = [(i, n, x) for i, xs in enumerate(pieces) for n, x in enumerate(xs)]
    n = len(flat)
    wide = len(which) * W

    def body(at, *rest):
        blocks, left, out, stack = rest[:n], rest[n], *rest[-2:]
        for (i, h, _), r in zip(flat, blocks):
            stack[STEP * h : STEP * h + r.shape[0], W * i : W * i + W] = r[...]
        total = rest[n + 1][...] if before is not None else jnp.zeros((H, W), F32)
        for i, (dy, p) in enumerate(which):
            cols = pl.ds(pl.multiple_of(chip_at(at, dy, p) * W, 128), W)
            total += lax.dot_general(
                stack[:, W * i : W * i + W], left[:, cols], (((1,), (1,)), ((), ())), preferred_element_type=F32
            )
        out[...] = total.astype(out.dtype)

    last = before is not None
    return call(
        body,
        [sds((H, W), BF if last else F32)],
        at,
        vmem=[x for _, _, x in flat] + ([left, before] if last else [left]),
        scratch=[pltpu.VMEM((H, wide), BF)],
        flops=2 * H * W * wide,
        limit=24,
    )[0]


def times_right(at, which, pieces, right, before=()):
    sides = len(right)
    flat = [(i, h, x) for i, xs in enumerate(pieces) for h, x in enumerate(xs)]
    n = len(flat)
    deep = len(which) * H

    def body(at, *rest):
        blocks, right, stack, factor = rest[:n], rest[n : n + sides], *rest[-2:]
        for (i, h, _), r in zip(flat, blocks):
            stack[H * i + STEP * h : H * i + STEP * h + r.shape[0], :] = r[...]
        for i, d in enumerate(which):
            for side in range(sides):
                factor[H * i : H * i + H, C * side : C * side + C] = right[side][rows(ring_at(at, d) * H, H), :]
        part = lax.dot_general(stack[...], factor[...], (((0,), (0,)), ((), ())), preferred_element_type=F32)
        if not before:
            rest[n + sides][...] = part
            return
        keep, far, give, total = rest[n + 2 * sides : n + 2 * sides + 4]
        for side in range(sides):
            cols = slice(C * side, C * side + C)
            total[:, cols] = rest[n + sides + side][...] + part[:, cols]
        for half in range(2):
            lo, to = H * half, slice(B * half, B * half + B)
            mine, theirs = rows(B * at[2] + lo, H), rows(B * (1 - at[2]) + lo, H)
            keep[:, to] = total[mine, 0:B]
            far[:, to] = total[mine, C : C + B]
            give[0:H, to] = total[theirs, 0:B].astype(BF)
            give[H:, to] = total[theirs, C : C + B].astype(BF)

    scratch = [pltpu.VMEM((deep, W), BF), pltpu.VMEM((deep, sides * C), BF)]
    flops = 2 * W * sides * C * deep
    args = [x for _, _, x in flat]
    if not before:
        return call(body, [sds((W, sides * C), F32)], at, vmem=[*args, *right], scratch=scratch, flops=flops, limit=24)[0]
    return call(
        body,
        [sds((H, W), F32), sds((H, W), F32), sds((B, W))],
        at,
        vmem=[*args, *right, *before],
        scratch=[pltpu.VMEM((W, 2 * C), F32), *scratch],
        flops=flops,
        limit=24,
    )


def left_piece(at, direction, left, d):
    cols = pl.ds(pl.multiple_of(chip_at(at, *d) * W, 128), W)
    return jnp.dot(direction, left[:, cols], preferred_element_type=F32).astype(BF)


EARLY = [(2, 1), (1, 1), (-1, 1), (1, 0), (-1, 0)]
LATE = [(2, 0), (0, 1), (0, 0)]


def moments(at, keep, near, far, avg, sq):
    def body(at, keep, near, far, avg, sq, new_avg, new_sq, direction):
        packed = keep[...] + near[0:H, :].astype(F32) + far[...].astype(F32)
        for half in range(2):
            here = slice(H * half, H * half + H)
            rotated = packed[:, B * half : B * half + B]
            a = 0.9 * avg[here, :] + 0.1 * rotated
            s = 0.95 * sq[here, :] + 0.05 * rotated * rotated
            new_avg[here, :] = a
            new_sq[here, :] = s
            direction[here, :] = (a / first_fix / (jnp.sqrt(s / second_fix) + 1e-08)).astype(BF)

    out = [sds((B, B), F32), sds((B, B), F32), sds((B, B))]
    return call(body, out, at, vmem=(keep, near, far, avg, sq), limit=16)


def left_early(at, own, other, left):
    def body(at, own, other, left, turned_out, *rest):
        outs, (stack, turned) = rest[: len(EARLY)], rest[len(EARLY) :]
        k = at[2]
        stack[rows(B * k, B), 0:B] = own[...]
        stack[rows(B * (1 - k), B), 0:B] = other[...]
        turned[...] = jnp.transpose(stack[...])
        direction = turned[rows(H * k, H), :]
        turned_out[...] = direction
        for d, out in zip(EARLY, outs):
            out[...] = left_piece(at, direction, left, d)

    direction, *parts = call(
        body,
        [sds((H, W))] * (1 + len(EARLY)),
        at,
        vmem=(own, other, left),
        scratch=[pltpu.VMEM((W, C), BF), pltpu.VMEM((C, W), BF)],
        flops=2 * H * W * 5 * W,
        limit=24,
    )
    return direction, dict(zip(EARLY, parts))


def left_back(at, direction, left):
    def body(at, direction, left, *outs):
        for d, out in zip(LATE, outs):
            out[...] = left_piece(at, direction[...], left, d)

    return dict(zip(LATE, call(body, [sds((H, W))] * 3, at, vmem=(direction, left), flops=2 * H * W * 3 * W, limit=24)))


def right_back(at, blocks, right, which):
    def body(at, *rest):
        own, near, far, far_near, right, right_far = rest[:6]
        outs, stack, chosen = rest[6:-2], rest[-2], rest[-1]
        k = at[2]
        stack[B:C, :] = jnp.zeros((C - B, W), BF)
        stack[C + B :, :] = jnp.zeros((C - B, W), BF)
        stack[rows(H * k, H), :] = own[...]
        stack[rows(H * (1 - k), H), :] = near[...]
        stack[rows(C + H * k, H), :] = far[...]
        stack[rows(C + H * (1 - k), H), :] = far_near[...]
        for i, d in enumerate(which):
            chosen[H * i : H * i + H, :C] = right[rows(ring_at(at, d) * H, H), :]
            chosen[H * i : H * i + H, C:] = right_far[rows(ring_at(at, d) * H, H), :]
        total = jnp.dot(chosen[...], stack[...], preferred_element_type=F32).astype(BF)
        for i in range(len(which)):
            outs[i][...] = total[H * i : H * i + H]

    n = len(which)
    outs = call(
        body,
        [sds((H, W))] * n,
        at,
        vmem=(*blocks, *right),
        scratch=[pltpu.VMEM((2 * C, W), BF), pltpu.VMEM((n * H, 2 * C), BF)],
        flops=2 * n * H * W * W,
        limit=24,
    )
    return dict(zip(which, outs))


def per_device(gradient, left_basis, right_basis, exp_avg, exp_avg_sq):
    row, col = lax.axis_index("row"), lax.axis_index("col")
    k, xh = row % 2, col // 8
    at = jnp.stack([row // 4, row // 2 % 2, k, xh, col % 8]).astype(jnp.int32)

    gradient_far = move(gradient, k=1)
    half = 8 * B
    own_left = after(left_basis.T, gradient_far)
    far_left = move(own_left, k=1)
    x, top, bottom = to_half(at, gradient, gradient_far, [(0, H), (0, STEP), (STEP, STEP)])
    side = move(x, xl=1)
    behind, ahead = move(x, y=1), move(x, y=-1)
    bottom = after(bottom, far_left)
    far = [move(top, y=2), move(bottom, y=-2)]
    whole = after(right_basis.T, x)
    sent = lax.dynamic_slice(whole, (0, (1 - xh) * half), (B, half))
    kept = lax.dynamic_slice(whole, (0, xh * half), (B, half))
    left = both_left(at, in_hbm(after(own_left, sent, kept)), far_left)
    got = move(after(sent, left, side, behind, ahead, *far), xh=1, xl=1)
    side_in = after(side, left)
    side_behind, side_ahead = move(side_in, y=1), move(side_in, y=-1)
    side_far = [move(f, xl=1) for f in far]

    part = times_left(at, YX[:4], [[x], [behind], [ahead], [side]], left)
    x = times_left(at, YX[4:], [[side_behind], [side_ahead], far, side_far], left, part)
    own_right = right_half(at, after(kept, x))
    pieces, plus, minus = gather_z(x, own_right)
    own_part = times_right(at, ZS[:5], pieces[:5], [own_right])
    far_right = right_half(at, after(got, own_part, *pieces[5], *pieces[6]))
    pieces.append(gather_last(after(plus, own_part), after(minus, own_part)))
    far_part = times_right(at, ZS[:5], pieces[:5], [far_right])
    right = (own_right, far_right)
    keep, far, give = times_right(at, ZS[5:], pieces[5:], right, (own_part, far_part))
    near = move(give, k=1)
    far = move(add(far, near[H:]), xh=1)
    new_avg, new_sq, direction = moments(at, keep, near, far, exp_avg, exp_avg_sq)
    direction, part = left_early(at, direction, move(direction, k=1), left)
    part |= left_back(at, direction, left)

    own = scatter_yx(part)
    far = move(own, xh=1)
    blocks = (own, move(own, k=1), far, move(far, k=1))
    end = scatter_z(right_back(at, blocks, right, [4, 3, -3]) | right_back(at, blocks, right, [0, 2, -2, 1, -1]))
    update = from_half(at, [end], [move(end, k=1)])
    return (new_avg, new_sq, update)


def solution(mesh):
    placed = (P("row", "col"), P(None, "row"), P(None, "col"), P("row", "col"), P("row", "col"))
    return jax.shard_map(
        per_device,
        mesh=mesh,
        in_specs=placed,
        out_specs=(P("row", "col"), P("row", "col"), P("row", "col")),
        check_vma=False,
    )
```

```python
import jax
import jax.numpy as jnp
import numpy as np
from jax import lax
from jax.experimental import pallas as pl
from jax.experimental.pallas import tpu as pltpu
from jax.sharding import PartitionSpec as P

first_fix = 0.9999734386
second_fix = 0.9940794709

AXES = ("row", "col")
SIZES = {"y": 4, "xl": 2, "k": 2, "xh": 2, "z": 8}
BF, F32 = jnp.bfloat16, jnp.float32
B, H, W = 320, 160, 640
YX = [(0, 0), (-1, 0), (1, 0), (0, 1), (-1, 1), (1, 1), (2, 0), (2, 1)]
ZS = [0, -1, 1, -2, 2, -3, 3, 4]
STEP = 80
C = 384


def place(i):
    r, c = divmod(i, 16)
    return {"y": r // 4, "xl": r // 2 % 2, "k": r % 2, "xh": c // 8, "z": c % 8}


def move(x, **steps):
    pairs = []
    for i in range(256):
        d = place(i)
        for name, step in steps.items():
            d[name] = (d[name] + step) % SIZES[name]
        pairs.append((i, (d["y"] * 4 + d["xl"] * 2 + d["k"]) * 16 + d["xh"] * 8 + d["z"]))
    return lax.ppermute(x, AXES, pairs)


ANY = pl.BlockSpec(memory_space=pl.ANY)
VMEM = pl.BlockSpec(memory_space=pltpu.VMEM)
SMEM = pl.BlockSpec(memory_space=pltpu.SMEM)


def call(body, out, at, apart=(), vmem=(), scratch=(), limit=40, flops=0, out_spec=None):
    args = [at, *apart, *vmem]
    size = sum(a.size * a.dtype.itemsize for a in args) + sum(
        int(np.prod(o.shape)) * jnp.dtype(o.dtype).itemsize for o in out
    )
    return pl.pallas_call(
        body,
        out_shape=list(out),
        in_specs=[SMEM] + [ANY] * len(apart) + [VMEM] * len(vmem),
        out_specs=[out_spec or VMEM] * len(out),
        scratch_shapes=list(scratch),
        compiler_params=pltpu.CompilerParams(vmem_limit_bytes=limit << 20),
        cost_estimate=pl.CostEstimate(flops=flops, bytes_accessed=size, transcendentals=0),
    )(*args)


def sds(shape, dtype=BF):
    return jax.ShapeDtypeStruct(shape, dtype)


def far_sds(shape, dtype=BF):
    return pltpu.HBM(shape, dtype)


def in_hbm(x):
    return pltpu.with_memory_space_constraint(x, pltpu.HBM)


def in_vmem(x):
    return pltpu.with_memory_space_constraint(x, pltpu.VMEM)


def after(x, *others):
    return lax.optimization_barrier((x, *others))[0]


def chip_at(at, dy, p):
    return lax.rem(at[0] + dy + 4, 4) * 2 + lax.rem(at[1] + p, 2)


def ring_at(at, d):
    return lax.rem(at[4] + d + 8, 8)


def copies(pairs, sems):
    started = []
    for n, (a, b) in enumerate(pairs):
        c = pltpu.make_async_copy(a, b, sems.at[n])
        c.start()
        started.append(c)
    for c in started:
        c.wait()


def rows(i, n):
    return pl.ds(pl.multiple_of(i, 16), n)


def to_half(at, own, other, parts, shape=sds):
    dt = own.dtype

    def body(at, own, other, *rest):
        outs, (stack, turned, mine, sems) = rest[: len(parts)], rest[len(parts) :]
        k = at[2]
        copy = pltpu.make_async_copy(own, mine, sems.at[0])
        copy.start()
        stack[rows(B * (1 - k), B), 0:B] = other[...]
        copy.wait()
        stack[rows(B * k, B), 0:B] = mine[...]
        turned[...] = jnp.transpose(stack[...])
        for out, (lo, n) in zip(outs, parts):
            out[...] = turned[rows(H * k + lo, n), :]

    return call(
        body,
        [shape((n, W), dt) for _, n in parts],
        at,
        apart=[in_hbm(own)],
        vmem=[other],
        scratch=[pltpu.VMEM((W, C), dt), pltpu.VMEM((C, W), dt), pltpu.VMEM((B, B), dt), pltpu.SemaphoreType.DMA((1,))],
        limit=16,
        out_spec=pl.BlockSpec() if shape is far_sds else None,
    )


def from_half(at, own, other):
    n = len(own)
    dt = own[0].dtype

    def body(at, *rest):
        mine, theirs, (out, stack, turned) = rest[:n], rest[n : 2 * n], rest[2 * n :]
        k = at[2]
        lo = 0
        for a, b in zip(mine, theirs):
            h = a.shape[0]
            stack[rows(H * k + lo, h), :] = a[...]
            stack[rows(H * (1 - k) + lo, h), :] = b[...]
            lo += h
        turned[...] = jnp.transpose(stack[...])
        out[...] = turned[rows(B * k, B), 0:B]

    return call(
        body,
        [sds((B, B), dt)],
        at,
        vmem=(*own, *other),
        scratch=[pltpu.VMEM((384, W), dt), pltpu.VMEM((W, 384), dt)],
        limit=16,
    )[0]


def both_left(at, own, other):
    def body(at, own, other, out, sems):
        k = at[2]
        pairs = []
        for i in range(5):
            part = slice(64 * i, 64 * i + 64)
            pairs.append((own.at[part, :], out.at[rows(B * k + 64 * i, 64), :]))
            pairs.append((other.at[part, :], out.at[rows(B * (1 - k) + 64 * i, 64), :]))
        copies(pairs, sems)

    return in_vmem(
        call(
            body,
            [sds((W, 16 * B))],
            at,
            apart=(own, other),
            scratch=[pltpu.SemaphoreType.DMA((10,))],
            limit=4,
            out_spec=ANY,
        )[0]
    )


def right_half(at, columns):
    def body(at, columns, out, stack, turned):
        k = at[2]
        stack[B:, :] = jnp.zeros((C - B, 8 * B), BF)
        stack[0:B, :] = columns[...]
        for t in range(20):
            turned[128 * t : 128 * t + 128, :] = jnp.transpose(stack[:, 128 * t : 128 * t + 128])
        for z in range(8):
            out[H * z : H * z + H, :] = turned[rows(B * z + H * k, H), :]

    return call(
        body,
        [sds((4 * B, C))],
        at,
        vmem=[columns],
        scratch=[pltpu.VMEM((C, 8 * B), BF), pltpu.VMEM((8 * B, C), BF)],
        limit=24,
    )[0]


def add(*xs):
    total = xs[0].astype(F32)
    for x in xs[1:]:
        total = total + x.astype(F32)
    return total.astype(BF)


def scatter_yx(part):
    far = add(part[2, 0], move(part[2, 1], xl=1))
    side = add(part[0, 1], move(part[1, 1], y=1), move(part[-1, 1], y=-1))
    near = [move(part[1, 0], y=1), move(part[-1, 0], y=-1)]
    far = jnp.concatenate([move(far[:STEP], y=2), move(far[STEP:], y=-2)], 0)
    return add(part[0, 0], *near, far, move(side, xl=1))


def gather_z(x, early):
    plus = minus = x
    got = [[x]]
    for step in range(3):
        plus, minus = move(plus, z=1), move(minus, z=-1)
        got += [[plus], [minus]]
        plus, minus, *_ = lax.optimization_barrier((plus, minus, *([early] if step == 0 else [])))
    return got, plus, minus


def gather_last(plus, minus):
    return [move(plus[:STEP], z=1), move(minus[STEP:], z=-1)]


def scatter_z(part):
    plus, minus = move(part[4][:STEP], z=1), move(part[4][STEP:], z=-1)
    plus = jnp.concatenate([add(part[3][:STEP], plus), part[3][STEP:]], 0)
    minus = jnp.concatenate([part[-3][:STEP], add(part[-3][STEP:], minus)], 0)
    for s in (2, 1, 0):
        plus, minus, part[0] = lax.optimization_barrier((plus, minus, part[0]))
        plus, minus = move(plus, z=1), move(minus, z=-1)
        if s:
            plus, minus = add(part[s], plus), add(part[-s], minus)
    return add(part[0], plus, minus)


def times_left(at, which, pieces, left, before=None):
    flat = [(i, n, x) for i, xs in enumerate(pieces) for n, x in enumerate(xs)]
    n = len(flat)
    wide = len(which) * W

    def body(at, *rest):
        blocks, left, out, stack = rest[:n], rest[n], *rest[-2:]
        whole = {}
        for (i, h, _), r in zip(flat, blocks):
            if r.shape[0] == H:
                whole[i] = r
            else:
                stack[STEP * h : STEP * h + STEP, W * i : W * i + W] = r[...]
        total = rest[n + 1][...] if before is not None else jnp.zeros((H, W), F32)
        for i, (dy, p) in enumerate(which):
            cols = pl.ds(pl.multiple_of(chip_at(at, dy, p) * W, 128), W)
            total += lax.dot_general(
                whole[i][...] if i in whole else stack[:, W * i : W * i + W],
                left[:, cols],
                (((1,), (1,)), ((), ())),
                preferred_element_type=F32,
            )
        out[...] = total.astype(out.dtype)

    last = before is not None
    return call(
        body,
        [sds((H, W), BF if last else F32)],
        at,
        vmem=[x for _, _, x in flat] + ([left, before] if last else [left]),
        scratch=[pltpu.VMEM((H, wide), BF)],
        flops=2 * H * W * wide,
        limit=24,
    )[0]


def times_right(at, which, pieces, right, before=()):
    sides = len(right)
    flat = [(i, h, x) for i, xs in enumerate(pieces) for h, x in enumerate(xs)]
    n = len(flat)
    deep = len(which) * H

    def body(at, *rest):
        blocks, right, stack, factor = rest[:n], rest[n : n + sides], *rest[-2:]
        for (i, h, _), r in zip(flat, blocks):
            stack[H * i + STEP * h : H * i + STEP * h + r.shape[0], :] = r[...]
        for i, d in enumerate(which):
            for side in range(sides):
                factor[H * i : H * i + H, C * side : C * side + C] = right[side][rows(ring_at(at, d) * H, H), :]
        part = lax.dot_general(stack[...], factor[...], (((0,), (0,)), ((), ())), preferred_element_type=F32)
        if not before:
            rest[n + sides][...] = part
            return
        keep, far, give, total = rest[n + 2 * sides : n + 2 * sides + 4]
        for side in range(sides):
            cols = slice(C * side, C * side + C)
            total[:, cols] = rest[n + sides + side][...] + part[:, cols]
        for half in range(2):
            lo, to = H * half, slice(B * half, B * half + B)
            mine, theirs = rows(B * at[2] + lo, H), rows(B * (1 - at[2]) + lo, H)
            keep[:, to] = total[mine, 0:B]
            far[:, to] = total[mine, C : C + B]
            give[0:H, to] = total[theirs, 0:B].astype(BF)
            give[H:, to] = total[theirs, C : C + B].astype(BF)

    scratch = [pltpu.VMEM((deep, W), BF), pltpu.VMEM((deep, sides * C), BF)]
    flops = 2 * W * sides * C * deep
    args = [x for _, _, x in flat]
    if not before:
        return call(body, [sds((W, sides * C), F32)], at, vmem=[*args, *right], scratch=scratch, flops=flops, limit=24)[0]
    return call(
        body,
        [sds((H, W), F32), sds((H, W), F32), sds((B, W))],
        at,
        vmem=[*args, *right, *before],
        scratch=[pltpu.VMEM((W, 2 * C), F32), *scratch],
        flops=flops,
        limit=24,
    )


def left_piece(at, direction, left, d):
    cols = pl.ds(pl.multiple_of(chip_at(at, *d) * W, 128), W)
    return jnp.dot(direction, left[:, cols], preferred_element_type=F32).astype(BF)


EARLY = [(2, 1), (1, 1), (-1, 1), (1, 0), (-1, 0)]
LATE = [(2, 0), (0, 1), (0, 0)]


def moments(at, keep, near, far, avg, sq):
    def body(at, keep, near, far, avg, sq, new_avg, new_sq, direction):
        packed = keep[...] + near[0:H, :].astype(F32) + far[...].astype(F32)
        for half in range(2):
            here = slice(H * half, H * half + H)
            rotated = packed[:, B * half : B * half + B]
            a = 0.9 * avg[here, :] + 0.1 * rotated
            s = 0.95 * sq[here, :] + 0.05 * rotated * rotated
            new_avg[here, :] = a
            new_sq[here, :] = s
            direction[here, :] = (a / first_fix / (jnp.sqrt(s / second_fix) + 1e-08)).astype(BF)

    out = [sds((B, B), F32), sds((B, B), F32), sds((B, B))]
    return call(body, out, at, vmem=(keep, near, far, avg, sq), limit=16)


def left_early(at, own, other, left):
    def body(at, own, other, left, turned_out, *rest):
        outs, (stack, turned) = rest[: len(EARLY)], rest[len(EARLY) :]
        k = at[2]
        stack[rows(B * k, B), 0:B] = own[...]
        stack[rows(B * (1 - k), B), 0:B] = other[...]
        turned[...] = jnp.transpose(stack[...])
        direction = turned[rows(H * k, H), :]
        turned_out[...] = direction
        for d, out in zip(EARLY, outs):
            out[...] = left_piece(at, direction, left, d)

    direction, *parts = call(
        body,
        [sds((H, W))] * (1 + len(EARLY)),
        at,
        vmem=(own, other, left),
        scratch=[pltpu.VMEM((W, C), BF), pltpu.VMEM((C, W), BF)],
        flops=2 * H * W * 5 * W,
        limit=24,
    )
    return direction, dict(zip(EARLY, parts))


def left_back(at, direction, left):
    def body(at, direction, left, *outs):
        for d, out in zip(LATE, outs):
            out[...] = left_piece(at, direction[...], left, d)

    return dict(zip(LATE, call(body, [sds((H, W))] * 3, at, vmem=(direction, left), flops=2 * H * W * 3 * W, limit=24)))


def right_back(at, blocks, right, which):
    def body(at, *rest):
        own, near, far, far_near, right, right_far = rest[:6]
        outs, stack, chosen = rest[6:-2], rest[-2], rest[-1]
        k = at[2]
        stack[B:C, :] = jnp.zeros((C - B, W), BF)
        stack[C + B :, :] = jnp.zeros((C - B, W), BF)
        stack[rows(H * k, H), :] = own[...]
        stack[rows(H * (1 - k), H), :] = near[...]
        stack[rows(C + H * k, H), :] = far[...]
        stack[rows(C + H * (1 - k), H), :] = far_near[...]
        for i, d in enumerate(which):
            chosen[H * i : H * i + H, :C] = right[rows(ring_at(at, d) * H, H), :]
            chosen[H * i : H * i + H, C:] = right_far[rows(ring_at(at, d) * H, H), :]
        total = jnp.dot(chosen[...], stack[...], preferred_element_type=F32).astype(BF)
        for i in range(len(which)):
            outs[i][...] = total[H * i : H * i + H]

    n = len(which)
    outs = call(
        body,
        [sds((H, W))] * n,
        at,
        vmem=(*blocks, *right),
        scratch=[pltpu.VMEM((2 * C, W), BF), pltpu.VMEM((n * H, 2 * C), BF)],
        flops=2 * n * H * W * W,
        limit=24,
    )
    return dict(zip(which, outs))


def per_device(gradient, left_basis, right_basis, exp_avg, exp_avg_sq):
    row, col = lax.axis_index("row"), lax.axis_index("col")
    k, xh = row % 2, col // 8
    at = jnp.stack([row // 4, row // 2 % 2, k, xh, col % 8]).astype(jnp.int32)

    gradient_far = move(gradient, k=1)
    half = 8 * B
    own_left = after(left_basis.T, gradient_far)
    far_left = move(own_left, k=1)
    x, top, bottom = to_half(at, gradient, gradient_far, [(0, H), (0, STEP), (STEP, STEP)])
    side = move(x, xl=1)
    behind, ahead = move(x, y=1), move(x, y=-1)
    bottom = after(bottom, far_left)
    far = [move(top, y=2), move(bottom, y=-2)]
    whole = after(right_basis.T, x)
    sent = lax.dynamic_slice(whole, (0, (1 - xh) * half), (B, half))
    kept = lax.dynamic_slice(whole, (0, xh * half), (B, half))
    left = both_left(at, in_hbm(after(own_left, sent, kept)), far_left)
    got = move(after(sent, left, side, behind, ahead, *far), xh=1, xl=1)
    side_in = after(side, left)
    side_behind, side_ahead = move(side_in, y=1), move(side_in, y=-1)
    side_far = [move(f, xl=1) for f in far]

    part = times_left(at, YX[:4], [[x], [behind], [ahead], [side]], left)
    x = times_left(at, YX[4:], [[side_behind], [side_ahead], far, side_far], left, part)
    own_right = right_half(at, after(kept, x))
    pieces, plus, minus = gather_z(x, own_right)
    own_part = times_right(at, ZS[:5], pieces[:5], [own_right])
    far_right = right_half(at, after(got, own_part, *pieces[5], *pieces[6]))
    pieces.append(gather_last(after(plus, own_part), after(minus, own_part)))
    far_part = times_right(at, ZS[:5], pieces[:5], [far_right])
    right = (own_right, far_right)
    keep, far, give = times_right(at, ZS[5:], pieces[5:], right, (own_part, far_part))
    near = move(give, k=1)
    far = move(add(far, near[H:]), xh=1)
    new_avg, new_sq, direction = moments(at, keep, near, far, exp_avg, exp_avg_sq)
    direction, part = left_early(at, direction, move(direction, k=1), left)
    part |= left_back(at, direction, left)

    own = scatter_yx(part)
    far = move(own, xh=1)
    blocks = (own, move(own, k=1), far, move(far, k=1))
    end = scatter_z(right_back(at, blocks, right, [4, 3, -3]) | right_back(at, blocks, right, [0, 2, -2, 1, -1]))
    update = from_half(at, [end], [move(end, k=1)])
    return (new_avg, new_sq, update)


def solution(mesh):
    placed = (P("row", "col"), P(None, "row"), P(None, "col"), P("row", "col"), P("row", "col"))
    return jax.shard_map(
        per_device,
        mesh=mesh,
        in_specs=placed,
        out_specs=(P("row", "col"), P("row", "col"), P("row", "col")),
        check_vma=False,
    )
```
